512 devices in a mesh: gauss: 128 (over z, x, core), view: 4 (over y).
Axes of the slice: x: 4, y: 4, z: 16, core: 2. Of those that a mesh axis runs over, the one named last changes fastest.
Arguments:
- params: float32 [59, 65536], P(None, 'gauss'), as said below
- first_moment: float32 [59, 65536], P(None, 'gauss'), may hold values from -0.6 to 0.6
- second_moment: float32 [59, 65536], P(None, 'gauss'), may hold values from 0.0001 to 0.01
- cameras: float32 [4, 12], P('view'), as said below
- send_rows: int32 [4, 128, 512], P('view', 'gauss'), may hold values from 0 to 511, as said below
- lists: int32 [4, 256, 256], P('view', 'gauss'), may hold values from 0 to 511, as said below
- counts: int32 [4, 256], P('view', 'gauss'), may hold values from 1 to 256, 32768 in all within a row
- tile_ids: int32 [4, 256], P('view', 'gauss'), may hold values from 0 to 8159, as said below
- target: float32 [4, 256, 3, 256], P('view', 'gauss'), may hold values from 0 to 1
Outputs:
- new_params: float32 [59, 65536], P(None, 'gauss')
- new_first: float32 [59, 65536], P(None, 'gauss')
- new_second: float32 [59, 65536], P(None, 'gauss')
- tile_loss: float32 [4, 256], P('view', 'gauss')
The draws below stay inside these ranges and needn't reach their ends.
Inputs may be any that keep to these rules, and one draw needn't show every extreme that they name: `send_rows`: for each view and sender the 512 entries name every local row once. The 4 rows that a sender sends to one renderer form a group that goes whole to one renderer in every view, possibly another one in each view. `lists`: each tile's list names distinct slots; entries at positions counts or later are ignored. `tile_ids`: tiles of one view are distinct. Each view's counts sum to 32768. `params`: rows 0 and 1 lie within 7.5, row 2 within 0.25; rows 3 to 5 in [-4.5, -2]; row 6 in [0.5, 1.5], rows 7 to 9 within 1; row 10 in [-5.5, -1.5]. `cameras`: the matrix lies within 0.01 of the identity entrywise; translations x and y within 0.3, z in [7.95, 8.05].
All inputs are finite; a program needn't handle non-finite values. No bound on the sum of `counts` on one device may be relied on, other than what follows from the above.
Results may differ from the reference program's by a relative error of at most 0.0003.
Values sent between devices are 32-bit elements; how exact they have to be, the bound alone decides.
A program may use at most 64 MiB of HBM per device.

```python
import math
import jax
import jax.numpy as jnp
import numpy as np
from jax import lax

PARAMS = 59
PIXELS = 256
GAUSS_DEV = 512
TILES_DEV = 2
RECV = 512
LIST = 256
SHARDS = 128
VIEWS = 4
GAUSS = 65536
CAP = 4
TILES = 256


def layout(key):
    base = jax.random.fold_in(key, 97)
    streams = jax.random.split(base, 4)
    per_row = 116 // TILES_DEV
    chosen = jax.random.permutation(streams[0], 64 * per_row)[:SHARDS].astype(jnp.int32)
    strip_row = (2 + chosen // per_row).astype(jnp.int32)
    strip_col = (2 + chosen % per_row * TILES_DEV).astype(jnp.int32)
    shifts = jax.random.randint(streams[1], (VIEWS, 2), -2, 3).astype(jnp.int32)
    patches = jax.vmap(lambda single: jax.random.permutation(single, SHARDS))(jax.random.split(streams[2], VIEWS)).astype(jnp.int32)
    orders = jax.vmap(lambda single: jax.random.permutation(single, GAUSS_DEV))(jax.random.split(streams[3], SHARDS)).astype(jnp.int32)
    return (strip_row, strip_col, shifts, patches, orders)


def draw_params(key, part):
    strip_row, strip_col, shifts, patches, orders = layout(key)
    key = jax.random.fold_in(key, 11)
    streams = jax.random.split(key, 9)
    senders = jnp.arange(SHARDS, dtype=jnp.int32)[:, None]
    places = jnp.zeros((SHARDS, GAUSS_DEV), jnp.int32).at[senders, orders].set(jnp.arange(GAUSS_DEV, dtype=jnp.int32)[None, :])
    home = (places // CAP).reshape(GAUSS)
    home_row = strip_row[home].astype(jnp.float32)
    home_col = strip_col[home].astype(jnp.float32)
    mean_z = jax.random.uniform(streams[0], (GAUSS,), jnp.float32, -0.25, 0.25)
    pixel_u = 16.0 * home_col + jax.random.uniform(streams[1], (GAUSS,), jnp.float32, 0.0, 16.0 * TILES_DEV)
    pixel_v = 16.0 * home_row + jax.random.uniform(streams[2], (GAUSS,), jnp.float32, 0.0, 16.0)
    depth = 8.0 + mean_z
    mean_x = (pixel_u - 960.0) * depth / 1100.0
    mean_y = (pixel_v - 540.0) * depth / 1100.0
    log_scale = jax.random.uniform(streams[3], (3, GAUSS), jnp.float32, -4.5, -2.0)
    quat_w = jax.random.uniform(streams[4], (1, GAUSS), jnp.float32, 0.5, 1.5)
    quat_v = jax.random.uniform(streams[5], (3, GAUSS), jnp.float32, -1.0, 1.0)
    logit = jax.random.uniform(streams[6], (1, GAUSS), jnp.float32, -5.5, -1.5)
    colour_dc = jax.random.uniform(streams[7], (3, GAUSS), jnp.float32, -1.0, 1.0)
    colour_rest = 0.3 * jax.random.normal(streams[8], (45, GAUSS), jnp.float32)
    return jnp.concatenate([mean_x[None, :], mean_y[None, :], mean_z[None, :], log_scale, quat_w, quat_v, logit, colour_dc, colour_rest], axis=0)


def draw_cameras(key, part):
    strip_row, strip_col, shifts, patches, orders = layout(key)
    key = jax.random.fold_in(key, 23)
    streams = jax.random.split(key, 3)
    matrix = jnp.eye(3, dtype=jnp.float32).reshape(1, 9) + jax.random.uniform(streams[0], (VIEWS, 9), jnp.float32, -0.01, 0.01)
    jitter = jax.random.uniform(streams[1], (VIEWS, 2), jnp.float32, -0.02, 0.02)
    offset = shifts.astype(jnp.float32) * (16.0 * 8.0 / 1100.0) + jitter
    height = jax.random.uniform(streams[2], (VIEWS, 1), jnp.float32, 7.95, 8.05)
    return jnp.concatenate([matrix, offset, height], axis=1)


def draw_send_rows(key, part):
    strip_row, strip_col, shifts, patches, orders = layout(key)
    key = jax.random.fold_in(key, 37)
    scores = jax.random.randint(key, (VIEWS, SHARDS, SHARDS, CAP), 0, 1048576).astype(jnp.int32) * CAP + jnp.arange(CAP, dtype=jnp.int32)
    within = jnp.argsort(scores, axis=3).astype(jnp.int32)
    positions = patches[:, None, :, None] * CAP + within
    every = jnp.broadcast_to(orders[None, :, :], (VIEWS, SHARDS, GAUSS_DEV))
    picked = jnp.take_along_axis(every, positions.reshape(VIEWS, SHARDS, SHARDS * CAP), axis=2)
    return picked.astype(jnp.int32)


def draw_lists(key, part):
    key = jax.random.fold_in(key, 41)
    streams = jax.random.split(key, VIEWS * TILES)
    orders = jax.vmap(lambda single: jax.random.permutation(single, RECV)[:LIST])(streams)
    return orders.reshape(VIEWS, TILES, LIST).astype(jnp.int32)


def draw_tile_ids(key, part):
    strip_row, strip_col, shifts, patches, orders = layout(key)
    tile_row = strip_row[patches] + shifts[:, 1:2]
    tile_col = strip_col[patches] + shifts[:, 0:1]
    placed = (tile_row * 120 + tile_col)[:, :, None] + jnp.arange(TILES_DEV, dtype=jnp.int32)[None, None, :]
    return placed.reshape(VIEWS, TILES).astype(jnp.int32)


def steps_of(rng, extent, pieces, smallest, top_value):
    loudness, own = 1.0, jax.random.fold_in(rng, 6)
    for position, parts in pieces:
        steps = jnp.exp(jax.random.uniform(jax.random.fold_in(own, position), (parts,), jnp.float32, smallest / len(pieces), top_value / len(pieces)))
        loudness = loudness * jnp.repeat(steps, extent[position] // parts).reshape([-1 if axis == position else 1 for axis in range(len(extent))])
    return loudness


def profile(amount, total, bound, slope):
    loads = [(1 << 20) // math.isqrt(standing ** slope) + 1 for standing in range(2, amount + 1)]
    rest, given = total - bound - (amount - 1), [1] * (amount - 1)
    while rest > 0:
        free = [i for i in range(amount - 1) if given[i] < bound]
        mass, remaining = sum([loads[i] for i in free]), rest
        for i in free:
            extra = min(bound - given[i], max(1, remaining * loads[i] // mass), rest)
            given[i] = given[i] + extra
            rest = rest - extra
    return np.array([bound] + given)


def uneven_parts(key, amount, total, limit, skew):
    if amount == 2:
        one = jax.random.randint(key, (), max(1, total - limit), min(limit, total - 1) + 1)
        return jnp.stack([one, total - one])
    sizes = jnp.asarray(profile(amount, total, limit, skew), jnp.int32)
    pairs = (amount - 1) // 2
    donor, receiver = sizes[1:1 + 2 * pairs:2], sizes[2:2 + 2 * pairs:2]
    room = jnp.minimum(donor - 1, limit - receiver)
    passed = jax.random.randint(jax.random.fold_in(key, 1), (pairs,), 0, 1 << 20) % (room + 1)
    sizes = sizes.at[1:1 + 2 * pairs:2].set(donor - passed).at[2:2 + 2 * pairs:2].set(receiver + passed)
    return sizes[jax.random.permutation(jax.random.fold_in(key, 2), amount)]


def scatter_about(own_key, extent, deviation, bound, cuts=(), kind=jnp.bfloat16):
    array = deviation * jax.random.normal(own_key, extent, jnp.float32)
    if cuts:
        array = array * steps_of(own_key, extent, cuts, -0.22, 0.18)
    return jnp.clip(array, -bound, bound).astype(kind)


def setup_inputs(seed: int = 0) -> dict:
    arg_keys = jax.random.split(jax.random.key(seed), 10)
    return {
        "params": draw_params(jax.random.fold_in(arg_keys[9], 71), 0),
        "first_moment": scatter_about(arg_keys[1], (PARAMS, GAUSS), 0.1, 0.6, ((1, 128),), jnp.float32),
        "second_moment": jnp.clip(jnp.exp(math.log(0.01) - 4.6051702 * jax.random.uniform(arg_keys[2], (PARAMS, GAUSS), jnp.float32) ** steps_of(arg_keys[2], (PARAMS, GAUSS), ((1, 128),), -0.2, 0.2)), 0.0001, 0.01),
        "cameras": draw_cameras(jax.random.fold_in(arg_keys[9], 71), 0),
        "send_rows": draw_send_rows(jax.random.fold_in(arg_keys[9], 71), 0),
        "lists": draw_lists(jax.random.fold_in(arg_keys[9], 71), 0),
        "counts": jax.vmap(lambda own: uneven_parts(own, TILES, TILES * LIST // 2, LIST, 2))(jax.random.split(arg_keys[6], VIEWS)).reshape((VIEWS, TILES)).astype(jnp.int32),
        "tile_ids": draw_tile_ids(jax.random.fold_in(arg_keys[9], 71), 0),
        "target": jnp.clip(1.0 * jax.random.uniform(arg_keys[8], (VIEWS, TILES, 3, PIXELS), jnp.float32) ** steps_of(arg_keys[8], (VIEWS, TILES, 3, PIXELS), ((0, 4), (1, 128)), -0.2, 0.2), 0.0, 1.0),
    }


focal_length = 1100.0
centre_x = 960.0
centre_y = 540.0
beta_one = 0.9
beta_two = 0.999
adam_eps = 1e-15
adam_step = 100.0
sh_zero = 0.28209479177387814
sh_one = 0.4886025119029199
sh_two = [1.0925484305920792, -1.0925484305920792, 0.31539156525252005, -1.0925484305920792, 0.5462742152960396]
sh_three = [-0.5900435899266435, 2.890611442640554, -0.4570457994644658, 0.3731763325901154, -0.4570457994644658, 1.445305721320277, -0.5900435899266435]

def harmonics(dir_x, dir_y, dir_z):
    sq_x = dir_x * dir_x
    sq_y = dir_y * dir_y
    sq_z = dir_z * dir_z
    return [sh_zero + 0.0 * dir_x, -sh_one * dir_y, sh_one * dir_z, -sh_one * dir_x, sh_two[0] * dir_x * dir_y, sh_two[1] * dir_y * dir_z, sh_two[2] * (2.0 * sq_z - sq_x - sq_y), sh_two[3] * dir_x * dir_z, sh_two[4] * (sq_x - sq_y), sh_three[0] * dir_y * (3.0 * sq_x - sq_y), sh_three[1] * dir_x * dir_y * dir_z, sh_three[2] * dir_y * (4.0 * sq_z - sq_x - sq_y), sh_three[3] * dir_z * (2.0 * sq_z - 3.0 * sq_x - 3.0 * sq_y), sh_three[4] * dir_x * (4.0 * sq_z - sq_x - sq_y), sh_three[5] * dir_z * (sq_x - sq_y), sh_three[6] * dir_x * (sq_x - 3.0 * sq_y)]

def project(columns, camera):
    mean_x, mean_y, mean_z = (columns[0], columns[1], columns[2])
    scales = jnp.exp(columns[3:6])
    quat_w, quat_x, quat_y, quat_z = (columns[6], columns[7], columns[8], columns[9])
    length = jnp.sqrt(quat_w * quat_w + quat_x * quat_x + quat_y * quat_y + quat_z * quat_z)
    quat_w, quat_x, quat_y, quat_z = (quat_w / length, quat_x / length, quat_y / length, quat_z / length)
    turn = [[1.0 - 2.0 * (quat_y * quat_y + quat_z * quat_z), 2.0 * (quat_x * quat_y - quat_w * quat_z), 2.0 * (quat_x * quat_z + quat_w * quat_y)], [2.0 * (quat_x * quat_y + quat_w * quat_z), 1.0 - 2.0 * (quat_x * quat_x + quat_z * quat_z), 2.0 * (quat_y * quat_z - quat_w * quat_x)], [2.0 * (quat_x * quat_z - quat_w * quat_y), 2.0 * (quat_y * quat_z + quat_w * quat_x), 1.0 - 2.0 * (quat_x * quat_x + quat_y * quat_y)]]
    world = [[turn[outer][inner] * scales[inner] for inner in range(3)] for outer in range(3)]
    posed = [camera[3 * outer] * mean_x + camera[3 * outer + 1] * mean_y + camera[3 * outer + 2] * mean_z + camera[9 + outer] for outer in range(3)]
    cam_x, cam_y, depth = posed
    framed = [[camera[3 * outer] * world[0][inner] + camera[3 * outer + 1] * world[1][inner] + camera[3 * outer + 2] * world[2][inner] for inner in range(3)] for outer in range(3)]
    inverse = 1.0 / depth
    row_top = [focal_length * inverse * (framed[0][inner] - cam_x * inverse * framed[2][inner]) for inner in range(3)]
    row_low = [focal_length * inverse * (framed[1][inner] - cam_y * inverse * framed[2][inner]) for inner in range(3)]
    cov_a = row_top[0] * row_top[0] + row_top[1] * row_top[1] + row_top[2] * row_top[2] + 0.3
    cov_b = row_top[0] * row_low[0] + row_top[1] * row_low[1] + row_top[2] * row_low[2]
    cov_c = row_low[0] * row_low[0] + row_low[1] * row_low[1] + row_low[2] * row_low[2] + 0.3
    determinant = cov_a * cov_c - cov_b * cov_b
    centre_u = focal_length * cam_x * inverse + centre_x
    centre_v = focal_length * cam_y * inverse + centre_y
    distance = jnp.sqrt(cam_x * cam_x + cam_y * cam_y + depth * depth)
    basis = harmonics(cam_x / distance, cam_y / distance, depth / distance)
    colours = []
    for channel in range(3):
        total = 0.5 + 0.0 * mean_x
        for order in range(16):
            total = total + basis[order] * columns[11 + 3 * order + channel]
        colours.append(total)
    opacity = jax.nn.sigmoid(columns[10])
    return jnp.stack([centre_u, centre_v, cov_c / determinant, -cov_b / determinant, cov_a / determinant, opacity, colours[0], colours[1], colours[2]])

def shade_block(carry, picked, alive, pixel_x, pixel_y):
    transmit, colour = carry
    offset_x = pixel_x[:, None] - picked[0][None, :]
    offset_y = pixel_y[:, None] - picked[1][None, :]
    exponent = -0.5 * (picked[2][None, :] * offset_x * offset_x + picked[4][None, :] * offset_y * offset_y) - picked[3][None, :] * offset_x * offset_y
    opacity_map = (picked[5] * alive)[None, :] * jnp.exp(exponent)
    keep_log = jnp.log1p(-opacity_map)
    running = jnp.cumsum(keep_log, axis=1)
    weight = transmit[:, None] * jnp.exp(running - keep_log) * opacity_map
    colour = colour + jnp.dot(weight, picked[6:9].T, precision=lax.Precision.HIGHEST)
    transmit = transmit * jnp.exp(running[:, -1])
    return (transmit, colour)

def render_tile(attributes, entries, count, tile_id, target_tile):
    pixel = jnp.arange(256, dtype=jnp.int32)
    pixel_x = (tile_id % 120 * 16 + pixel % 16).astype(jnp.float32)
    pixel_y = (tile_id // 120 * 16 + pixel // 16).astype(jnp.float32)
    blocks = entries.shape[0] // 256
    picked = jnp.take(attributes, entries, axis=1).reshape(9, blocks, 256).transpose(1, 0, 2)
    alive = (jnp.arange(entries.shape[0], dtype=jnp.int32) < count).astype(jnp.float32).reshape(blocks, 256)
    shade = jax.checkpoint(shade_block)

    def advance(carry, block):
        return (shade(carry, block[0], block[1], pixel_x, pixel_y), None)
    start = (jnp.ones((256,), jnp.float32), jnp.zeros((256, 3), jnp.float32))
    (transmit, colour), unused = lax.scan(advance, start, (picked, alive))
    difference = colour.T - target_tile
    return 0.5 * jnp.sum(difference * difference)

def adam(params, first_moment, second_moment, grads):
    rates = jnp.concatenate([jnp.full((3,), 0.00016), jnp.full((3,), 0.005), jnp.full((4,), 0.001), jnp.full((1,), 0.05), jnp.full((3,), 0.0025), jnp.full((45,), 0.000125)]).astype(params.dtype)
    new_first = beta_one * first_moment + (1.0 - beta_one) * grads
    new_second = beta_two * second_moment + (1.0 - beta_two) * grads * grads
    step_size = rates[:, None] / (1.0 - beta_one ** adam_step)
    new_params = params - step_size * new_first / (jnp.sqrt(new_second / (1.0 - beta_two ** adam_step)) + adam_eps)
    return (new_params, new_first, new_second)

def reference(params, first_moment, second_moment, cameras, send_rows, lists, counts, tile_ids, target):
    owners = (jnp.arange(SHARDS, dtype=jnp.int32) * GAUSS_DEV)[:, None]

    def losses(weights):

        def one_view(view_index):
            attributes = project(weights, cameras[view_index])
            outgoing = send_rows[view_index]

            def one_device(device):
                local = lax.dynamic_slice_in_dim(outgoing, (device * CAP).astype(jnp.int32), CAP, 1)
                received = jnp.take(attributes, (local + owners).reshape(-1), axis=1)
                first_tile = device * TILES_DEV

                def one_tile(tile):
                    entry = first_tile + tile
                    return render_tile(received, lists[view_index, entry], counts[view_index, entry], tile_ids[view_index, entry], target[view_index, entry])
                return lax.map(one_tile, jnp.arange(TILES_DEV, dtype=jnp.int32))
            return lax.map(one_device, jnp.arange(SHARDS, dtype=jnp.int32)).reshape(-1)
        return lax.map(one_view, jnp.arange(VIEWS, dtype=jnp.int32))
    tile_loss, pullback = jax.vjp(losses, params)
    grads = pullback(jnp.ones_like(tile_loss))[0]
    new_params, new_first, new_second = adam(params, first_moment, second_moment, grads)
    return (new_params, new_first, new_second, tile_loss)
```

```python
import jax
import jax.numpy as jnp
from jax import lax
from jax.experimental import pallas as pl
from jax.experimental.pallas import tpu as pltpu
from jax.sharding import PartitionSpec as P

focal_length = 1100.0
centre_x = 960.0
centre_y = 540.0
beta_one = 0.9
beta_two = 0.999
adam_eps = 1e-15
adam_step = 100.0
log2_e = 1.4426950408889634
sh_zero = 0.28209479177387814
sh_one = 0.4886025119029199
sh_two = [
    1.0925484305920792,
    -1.0925484305920792,
    0.31539156525252005,
    -1.0925484305920792,
    0.5462742152960396,
]
sh_three = [
    -0.5900435899266435,
    2.890611442640554,
    -0.4570457994644658,
    0.3731763325901154,
    -0.4570457994644658,
    1.445305721320277,
    -0.5900435899266435,
]
LINE = 16
GROUP = 8
VIEWS = 4
MESH = pl.DeviceIdType.MESH
f32 = jnp.float32
bf16 = jnp.bfloat16


def harmonics(dir_x, dir_y, dir_z):
    sq_x = dir_x * dir_x
    sq_y = dir_y * dir_y
    sq_z = dir_z * dir_z
    return [
        -sh_one * dir_y,
        sh_one * dir_z,
        -sh_one * dir_x,
        sh_two[0] * dir_x * dir_y,
        sh_two[1] * dir_y * dir_z,
        sh_two[2] * (2.0 * sq_z - sq_x - sq_y),
        sh_two[3] * dir_x * dir_z,
        sh_two[4] * (sq_x - sq_y),
        sh_three[0] * dir_y * (3.0 * sq_x - sq_y),
        sh_three[1] * dir_x * dir_y * dir_z,
        sh_three[2] * dir_y * (4.0 * sq_z - sq_x - sq_y),
        sh_three[3] * dir_z * (2.0 * sq_z - 3.0 * sq_x - 3.0 * sq_y),
        sh_three[4] * dir_x * (4.0 * sq_z - sq_x - sq_y),
        sh_three[5] * dir_z * (sq_x - sq_y),
        sh_three[6] * dir_x * (sq_x - 3.0 * sq_y),
    ]


def project(columns, camera):
    mean_x, mean_y, mean_z = columns[0], columns[1], columns[2]
    scales = [jnp.exp(columns[3 + axis]) for axis in range(3)]
    quat_w, quat_x, quat_y, quat_z = columns[6:10]
    norm = 1.0 / jnp.sqrt(quat_w * quat_w + quat_x * quat_x + quat_y * quat_y + quat_z * quat_z)
    quat_w, quat_x, quat_y, quat_z = quat_w * norm, quat_x * norm, quat_y * norm, quat_z * norm
    turn = [
        [
            1.0 - 2.0 * (quat_y * quat_y + quat_z * quat_z),
            2.0 * (quat_x * quat_y - quat_w * quat_z),
            2.0 * (quat_x * quat_z + quat_w * quat_y),
        ],
        [
            2.0 * (quat_x * quat_y + quat_w * quat_z),
            1.0 - 2.0 * (quat_x * quat_x + quat_z * quat_z),
            2.0 * (quat_y * quat_z - quat_w * quat_x),
        ],
        [
            2.0 * (quat_x * quat_z - quat_w * quat_y),
            2.0 * (quat_y * quat_z + quat_w * quat_x),
            1.0 - 2.0 * (quat_x * quat_x + quat_y * quat_y),
        ],
    ]
    world = [[turn[outer][inner] * scales[inner] for inner in range(3)] for outer in range(3)]
    cam_x, cam_y, depth = [
        camera[3 * outer] * mean_x
        + camera[3 * outer + 1] * mean_y
        + camera[3 * outer + 2] * mean_z
        + camera[9 + outer]
        for outer in range(3)
    ]
    framed = [
        [
            camera[3 * outer] * world[0][inner]
            + camera[3 * outer + 1] * world[1][inner]
            + camera[3 * outer + 2] * world[2][inner]
            for inner in range(3)
        ]
        for outer in range(3)
    ]
    inverse = 1.0 / depth
    near = focal_length * inverse
    slope_x = cam_x * inverse
    slope_y = cam_y * inverse
    row_top = [near * (framed[0][inner] - slope_x * framed[2][inner]) for inner in range(3)]
    row_low = [near * (framed[1][inner] - slope_y * framed[2][inner]) for inner in range(3)]
    cov_a = row_top[0] * row_top[0] + row_top[1] * row_top[1] + row_top[2] * row_top[2] + 0.3
    cov_b = row_top[0] * row_low[0] + row_top[1] * row_low[1] + row_top[2] * row_low[2]
    cov_c = row_low[0] * row_low[0] + row_low[1] * row_low[1] + row_low[2] * row_low[2] + 0.3
    over = 1.0 / (cov_a * cov_c - cov_b * cov_b)
    centre_u = focal_length * slope_x + centre_x
    centre_v = focal_length * slope_y + centre_y
    away = 1.0 / jnp.sqrt(cam_x * cam_x + cam_y * cam_y + depth * depth)
    basis = harmonics(cam_x * away, cam_y * away, depth * away)
    colours = []
    for channel in range(3):
        total = 0.5 + sh_zero * columns[11 + channel]
        for order in range(15):
            total = total + basis[order] * columns[14 + 3 * order + channel]
        colours.append(total)
    opacity = 1.0 / (1.0 + jnp.exp(-columns[10]))
    return [
        centre_u,
        centre_v,
        cov_c * over,
        -cov_b * over,
        cov_a * over,
        opacity,
        colours[0],
        colours[1],
        colours[2],
    ]


def pieces(value):
    high = value.astype(bf16)
    rest = value - high.astype(f32)
    middle = rest.astype(bf16)
    low = (rest - middle.astype(f32)).astype(bf16)
    return high, middle, low


def dot_rows(left, right):
    return lax.dot_general(left, right, (((1,), (1,)), ((), ())), preferred_element_type=f32)


def dot_exact(left, right):
    high, middle, low = pieces(left)
    return (
        jnp.dot(high, right, preferred_element_type=f32)
        + jnp.dot(middle, right, preferred_element_type=f32)
    ) + jnp.dot(low, right, preferred_element_type=f32)


def dot_rows_exact(left, right):
    high, middle, low = pieces(left)
    return (dot_rows(high, right) + dot_rows(middle, right)) + dot_rows(low, right)


def iota(shape, axis):
    return lax.broadcasted_iota(jnp.int32, shape, axis)


def one_hot(test):
    return jnp.where(test, 1.0, 0.0).astype(bf16)


def swap(value):
    return pltpu.roll(value, 64, 1)


def reorder_row(row, width, place):
    split = jnp.concatenate([row >> 4, row & 15, jnp.zeros((6, width), jnp.int32)], axis=0)
    chosen = one_hot(iota((width, width), 0) == place(iota((width, width), 1)))
    moved = jnp.dot(split.astype(f32).astype(bf16), chosen, preferred_element_type=f32)
    return (moved[0:1] * 16.0 + moved[1:2]).astype(jnp.int32)


def sender_table(rows):
    moved = reorder_row(rows, 512, lambda n: 8 * (n & 63) + (n >> 6))
    return one_hot(iota((512, 512), 0) == moved)


def pack_messages(attributes, table):
    placed = dot_exact(attributes, table)
    parts = []
    for pair in range(4):
        both = placed[:, 128 * pair : 128 * pair + 128]
        parts += [both, swap(both)]
    return jnp.transpose(jnp.concatenate(parts, axis=0))[0:64]


def unpack_messages(messages, table):
    turned = jnp.transpose(jnp.concatenate([messages, jnp.zeros_like(messages)], axis=0))
    keep = iota((16, 128), 1) < 64
    parts = []
    for pair in range(4):
        left = turned[32 * pair : 32 * pair + 16]
        right = turned[32 * pair + 16 : 32 * pair + 32]
        parts.append(jnp.where(keep, left, swap(right)))
    return dot_rows_exact(jnp.concatenate(parts, axis=1), table)


def list_tables(lists):
    moved = []
    for tile in range(2):
        moved.append(reorder_row(lists[tile : tile + 1], 256, lambda n: 32 * (n & 7) + (n >> 3)))
    slot = jnp.concatenate(moved, axis=1)
    sender = slot >> 2
    line = sender >> 3
    row = (sender & 7) * 8 + (line & 7)
    group = (line >> 3) * 4 + (slot & 3)
    return one_hot(iota((64, 512), 0) == row), group


def pick(received, table, group):
    turned = jnp.transpose(jnp.concatenate([received, jnp.zeros_like(received)], axis=0))[:, 0:64]
    found = dot_exact(turned, table)
    found = jnp.where((iota((128, 512), 0) >> 4) == group, found, 0.0)
    total = found[0:16]
    for part in range(1, 8):
        total = total + found[16 * part : 16 * part + 16]
    return total


def unpick(grads, table, group):
    spread = jnp.concatenate([grads] * 8, axis=0)
    spread = jnp.where((iota((128, 512), 0) >> 4) == group, spread, 0.0)
    turned = dot_rows_exact(spread, table)
    return jnp.transpose(jnp.concatenate([turned, jnp.zeros((128, 64), f32)], axis=1))[0:64]


def place_of(position):
    return 32 * (position & 7) + (position >> 3)


def prepare_tile(attributes, count, tile_id):
    across = (16 * lax.rem(tile_id, 120)).astype(f32) + 7.5
    down = (16 * lax.div(tile_id, 120)).astype(f32) + 7.5
    centre_u = attributes[0:1] - across
    centre_v = attributes[1:2] - down
    alive = place_of(iota((1, 256), 1)) < count
    rows = [
        centre_u,
        centre_v,
        attributes[2:3] * (-0.5 * log2_e),
        attributes[3:4] * (-log2_e),
        attributes[4:5] * (-0.5 * log2_e),
        jnp.where(alive, attributes[5:6], 0.0),
        attributes[6:7],
        attributes[7:8],
        attributes[8:9],
        jnp.zeros((119, 256), f32),
    ]
    return jnp.transpose(jnp.concatenate(rows, axis=0)), centre_u, centre_v


def pixels():
    number = iota((1, 256), 1)
    return (number & 15).astype(f32) - 7.5, (number >> 4).astype(f32) - 7.5


def shade_step(columns, pixel_x, pixel_y, carry):
    keep, colour = carry
    offset_x = pixel_x - columns[:, 0:1]
    offset_y = pixel_y - columns[:, 1:2]
    power = offset_x * (columns[:, 2:3] * offset_x + columns[:, 3:4] * offset_y) + (
        columns[:, 4:5] * offset_y
    ) * offset_y
    alpha = columns[:, 5:6] * jnp.exp2(power)
    weight = keep * alpha
    colour = [colour[c] + weight * columns[:, 6 + c : 7 + c] for c in range(3)]
    return alpha, weight, (keep * (1.0 - alpha), colour)


def between(keep, colour, target):
    before = [jnp.ones((1, 256), f32)]
    for chunk in range(7):
        before.append(before[-1] * keep[chunk : chunk + 1])
    before = jnp.concatenate(before, axis=0)
    colour = [part * before for part in colour]
    residual = [jnp.sum(colour[c], axis=0, keepdims=True) - target[c : c + 1] for c in range(3)]
    own = residual[0] * colour[0] + residual[1] * colour[1] + residual[2] * colour[2]
    after = [jnp.zeros((1, 256), f32)]
    for chunk in range(7, 0, -1):
        after.append(after[-1] + own[chunk : chunk + 1])
    after = jnp.concatenate(after[::-1], axis=0)
    squares = residual[0] * residual[0] + residual[1] * residual[1] + residual[2] * residual[2]
    return before, after, residual, 0.5 * jnp.sum(squares, axis=1, keepdims=True)


def back_step(columns, alpha, weight, before, after, residual, later):
    shade = (
        residual[0] * columns[:, 6:7] + residual[1] * columns[:, 7:8] + residual[2] * columns[:, 8:9]
    )
    own = weight * shade
    ratio = alpha / (1.0 - alpha)
    slope = before * (own - later * ratio) - after * ratio
    return slope, before * weight, later + own


def moments(slope, weight, residual):
    pixel_x, pixel_y = pixels()
    ones = jnp.ones((1, 256), f32)
    powers = [ones, pixel_x, pixel_y, pixel_x * pixel_x, pixel_x * pixel_y, pixel_y * pixel_y]
    powers = jnp.concatenate(powers + [jnp.zeros((122, 256), f32)], axis=0).astype(bf16)
    shown = jnp.concatenate(
        [jnp.zeros((6, 256), f32)] + residual + [jnp.zeros((119, 256), f32)], axis=0
    )
    high, middle, low = pieces(shown)
    first, second, third = pieces(weight)
    total = dot_rows_exact(slope, powers)
    total = total + (dot_rows(first, high) + (dot_rows(first, middle) + dot_rows(second, high)))
    total = total + (dot_rows(first, low) + (dot_rows(second, middle) + dot_rows(third, high)))
    return jnp.transpose(total)[0:16]


def finish_tile(sums, attributes, centre_u, centre_v):
    whole, by_x, by_y, by_xx, by_xy, by_yy = [sums[n : n + 1] for n in range(6)]
    sum_x = by_x - centre_u * whole
    sum_y = by_y - centre_v * whole
    sum_xx = by_xx - centre_u * (by_x + sum_x)
    sum_xy = by_xy - centre_u * by_y - centre_v * sum_x
    sum_yy = by_yy - centre_v * (by_y + sum_y)
    conic = [attributes[2 + n : 3 + n] for n in range(3)]
    rows = [
        conic[0] * sum_x + conic[1] * sum_y,
        conic[1] * sum_x + conic[2] * sum_y,
        -0.5 * sum_xx,
        -sum_xy,
        -0.5 * sum_yy,
        whole,
        sums[6:9],
        jnp.zeros((7, 256), f32),
    ]
    return jnp.concatenate(rows, axis=0)


def exchange(
    params,
    camera,
    rows,
    lists,
    counts,
    tile_ids,
    target,
    out,
    loss,
    msg,
    land1,
    pass1,
    land2,
    back1,
    land3,
    pass2,
    land4,
    own,
    land5,
    columns,
    alphas,
    weights,
    table,
    send1,
    recv1,
    send2,
    recv2,
    send3,
    recv3,
    send4,
    recv4,
    send5,
    recv5,
):
    here = lax.axis_index("gauss")
    view = lax.axis_index("view")
    line = here // GROUP
    group = lax.rem(here, GROUP)

    def on_line(step):
        other = lax.rem(line + step, LINE)
        return other, {"gauss": other * GROUP + group, "view": view}

    def in_group(step):
        other = lax.rem(group + step, GROUP)
        return other, {"gauss": line * GROUP + other, "view": view}

    def over_views(step):
        other = lax.rem(view + step, VIEWS)
        return other, {"gauss": here, "view": other}

    def each(peers, count, action):
        def one(step, unused):
            action(step, *peers(step))
            return unused

        lax.fori_loop(1, count, one, 0)

    barrier = pltpu.get_barrier_semaphore()

    def greet(step, other, device):
        pl.semaphore_signal(barrier, inc=1, device_id=device, device_id_type=MESH)

    each(on_line, LINE, greet)
    each(in_group, GROUP, greet)
    each(over_views, VIEWS, greet)

    def swap_blocks(peers, count, mine, source, target_buffer, sent, arrived):
        def copy(step, other, device):
            return pltpu.make_async_remote_copy(
                src_ref=source.at[other],
                dst_ref=target_buffer.at[mine],
                send_sem=sent.at[step],
                recv_sem=arrived.at[mine],
                device_id=device,
                device_id_type=MESH,
            )

        def wait(step, other, device):
            pltpu.make_async_remote_copy(
                src_ref=source.at[other],
                dst_ref=target_buffer.at[other],
                send_sem=sent.at[step],
                recv_sem=arrived.at[other],
                device_id=device,
                device_id_type=MESH,
            ).wait()

        each(peers, count, lambda *peer: copy(*peer).start())
        target_buffer[mine] = source[mine]
        return lambda: each(peers, count, wait)

    table[...] = sender_table(rows[...])
    scalars = [camera[0, n] for n in range(12)]
    attributes = project([params[n : n + 1, :] for n in range(59)], scalars)
    messages = pack_messages(
        jnp.concatenate(attributes + [jnp.zeros((7, 512), f32)], axis=0), table[...]
    )
    msg[...] = messages.reshape(LINE, 4, 128)

    pl.semaphore_wait(barrier, LINE + GROUP + VIEWS - 3)
    arrive = swap_blocks(on_line, LINE, line, msg, land1, send1, recv1)
    picked, lane_group = list_tables(lists[0])
    arrive()
    low_lanes = iota((8, 128), 1) < 64
    for pair in range(4):
        lower, upper = land1[0:8, pair, :], land1[8:16, pair, :]
        pass1[2 * pair] = jnp.where(low_lanes, lower, swap(upper))
        pass1[2 * pair + 1] = jnp.where(low_lanes, swap(lower), upper)
    arrive = swap_blocks(in_group, GROUP, group, pass1, land2, send2, recv2)
    arrive()

    found = pick(land2[...].reshape(64, 128), picked, lane_group)
    pixel_x, pixel_y = pixels()
    centres = []
    for tile in range(2):
        entries = found[:, 256 * tile : 256 * tile + 256]
        filled, centre_u, centre_v = prepare_tile(entries, counts[0, tile], tile_ids[0, tile])
        columns[tile] = filled
        centres.append((entries, centre_u, centre_v))

    def forward(step, carry):
        rows_here = pl.ds(pl.multiple_of(step * 8, 8), 8)
        left = []
        for tile in range(2):
            alpha, weight, rest = shade_step(
                columns[tile, rows_here, :], pixel_x, pixel_y, carry[tile]
            )
            alphas[tile, rows_here, :] = alpha
            weights[tile, rows_here, :] = weight
            left.append(rest)
        return left

    fresh = (jnp.ones((8, 256), f32), [jnp.zeros((8, 256), f32)] * 3)
    carry = lax.fori_loop(0, 32, forward, [fresh, fresh], unroll=4)
    around = []
    for tile in range(2):
        around.append(between(carry[tile][0], carry[tile][1], target[0, tile]))
    spot = iota((1, 128), 1)
    loss[...] = jnp.where(spot == 0, around[0][3], jnp.where(spot == 1, around[1][3], 0.0))

    def backward(step, later):
        rows_here = pl.ds(pl.multiple_of((31 - step) * 8, 8), 8)
        left = []
        for tile in range(2):
            before, after, residual, unused = around[tile]
            slope, weight, rest = back_step(
                columns[tile, rows_here, :],
                alphas[tile, rows_here, :],
                weights[tile, rows_here, :],
                before,
                after,
                residual,
                later[tile],
            )
            alphas[tile, rows_here, :] = slope
            weights[tile, rows_here, :] = weight
            left.append(rest)
        return left

    lax.fori_loop(0, 32, backward, [jnp.zeros((8, 256), f32)] * 2, unroll=4)
    grads = []
    for tile in range(2):
        sums = moments(alphas[tile], weights[tile], around[tile][2])
        grads.append(finish_tile(sums, *centres[tile]))
    grads = jnp.concatenate(grads, axis=1)
    back1[...] = unpick(grads, picked, lane_group).reshape(GROUP, 8, 128)

    arrive = swap_blocks(in_group, GROUP, group, back1, land3, send3, recv3)
    arrive()
    for pair in range(4):
        even, odd = land3[2 * pair], land3[2 * pair + 1]
        pass2[0:8, pair, :] = jnp.where(low_lanes, even, swap(odd))
        pass2[8:16, pair, :] = jnp.where(low_lanes, swap(even), odd)
    arrive = swap_blocks(on_line, LINE, line, pass2, land4, send4, recv4)
    arrive()
    returned = unpack_messages(land4[...].reshape(64, 128), table[...])

    lanes = iota((1, 512), 1)
    pose = jnp.zeros((1, 512), f32)
    for n in range(12):
        pose = jnp.where(lanes == n, scalars[n], pose)
    own[...] = jnp.concatenate([returned[0:9], pose, jnp.zeros((6, 512), f32)], axis=0)

    def share(step, other, device):
        return pltpu.make_async_remote_copy(
            src_ref=own,
            dst_ref=land5.at[view],
            send_sem=send5.at[step],
            recv_sem=recv5.at[view],
            device_id=device,
            device_id_type=MESH,
        )

    def take(step, other, device):
        pltpu.make_async_remote_copy(
            src_ref=own,
            dst_ref=land5.at[other],
            send_sem=send5.at[step],
            recv_sem=recv5.at[other],
            device_id=device,
            device_id_type=MESH,
        ).wait()

    each(over_views, VIEWS, lambda *peer: share(*peer).start())
    land5[view] = own[...]
    each(over_views, VIEWS, take)
    out[...] = land5[...]


def update(params, first, second, grads, loss, new_params, new_first, new_second, tile_loss, whole):
    columns = [jnp.broadcast_to(params[n : n + 1, :], (VIEWS, 512)) for n in range(59)]
    camera = [grads[:, 9, n : n + 1] for n in range(12)]
    attributes, back = jax.vjp(lambda rows: project(rows, camera)[0:5] + project(rows, camera)[6:9], columns)
    given = [grads[:, n, :] for n in range(9)]
    pulled = back(given[0:5] + given[6:9])[0]
    opacity = 1.0 / (1.0 + jnp.exp(-columns[10]))
    pulled[10] = given[5] * (1.0 - opacity)
    for n in range(59):
        whole[n : n + 1, :] = jnp.sum(pulled[n], axis=0, keepdims=True)
    total = whole[...]
    row = iota((59, 1), 0)
    rate = jnp.where(row < 3, 0.00016, 0.005)
    rate = jnp.where(row < 6, rate, 0.001)
    rate = jnp.where(row < 10, rate, 0.05)
    rate = jnp.where(row < 11, rate, 0.0025)
    rate = jnp.where(row < 14, rate, 0.000125)
    rate = rate / (1.0 - beta_one**adam_step)
    moved = beta_one * first[...] + (1.0 - beta_one) * total
    spread = beta_two * second[...] + (1.0 - beta_two) * total * total
    new_first[...] = moved
    new_second[...] = spread
    new_params[...] = params[...] - rate * moved / (
        jnp.sqrt(spread / (1.0 - beta_two**adam_step)) + adam_eps
    )
    tile_loss[...] = loss[:, 0:2]


def body(params, first_moment, second_moment, cameras, send_rows, lists, counts, tile_ids, target):
    vmem = pl.BlockSpec(memory_space=pltpu.VMEM)
    smem = pl.BlockSpec(memory_space=pltpu.SMEM)
    dma = pltpu.SemaphoreType.DMA
    grads, loss = pl.pallas_call(
        exchange,
        out_shape=(
            jax.ShapeDtypeStruct((VIEWS, 16, 512), f32),
            jax.ShapeDtypeStruct((1, 128), f32),
        ),
        in_specs=[vmem, smem, vmem, vmem, smem, smem, vmem],
        out_specs=(vmem, vmem),
        scratch_shapes=[
            pltpu.VMEM((LINE, 4, 128), f32),
            pltpu.VMEM((LINE, 4, 128), f32),
            pltpu.VMEM((GROUP, 8, 128), f32),
            pltpu.VMEM((GROUP, 8, 128), f32),
            pltpu.VMEM((GROUP, 8, 128), f32),
            pltpu.VMEM((GROUP, 8, 128), f32),
            pltpu.VMEM((LINE, 4, 128), f32),
            pltpu.VMEM((LINE, 4, 128), f32),
            pltpu.VMEM((16, 512), f32),
            pltpu.VMEM((VIEWS, 16, 512), f32),
            pltpu.VMEM((2, 256, 128), f32),
            pltpu.VMEM((2, 256, 256), f32),
            pltpu.VMEM((2, 256, 256), f32),
            pltpu.VMEM((512, 512), bf16),
            dma((LINE,)),
            dma((LINE,)),
            dma((GROUP,)),
            dma((GROUP,)),
            dma((GROUP,)),
            dma((GROUP,)),
            dma((LINE,)),
            dma((LINE,)),
            dma((VIEWS,)),
            dma((VIEWS,)),
        ],
        compiler_params=pltpu.CompilerParams(
            collective_id=0, has_side_effects=True, vmem_limit_bytes=32 * 1024 * 1024
        ),
        name="exchange",
    )(params, cameras, send_rows.reshape(1, 512), lists, counts, tile_ids, target)
    whole = jax.ShapeDtypeStruct((59, 512), f32)
    return pl.pallas_call(
        update,
        out_shape=(whole, whole, whole, jax.ShapeDtypeStruct((1, 2), f32)),
        in_specs=[vmem] * 5,
        out_specs=(vmem,) * 4,
        scratch_shapes=[pltpu.VMEM((59, 512), f32)],
        compiler_params=pltpu.CompilerParams(vmem_limit_bytes=32 * 1024 * 1024),
        name="update",
    )(params, first_moment, second_moment, grads, loss)


def solution(mesh):
    in_specs = (
        P(None, "gauss"),
        P(None, "gauss"),
        P(None, "gauss"),
        P("view", None),
        P("view", "gauss", None),
        P("view", "gauss", None),
        P("view", "gauss"),
        P("view", "gauss"),
        P("view", "gauss", None, None),
    )
    out_specs = (P(None, "gauss"), P(None, "gauss"), P(None, "gauss"), P("view", "gauss"))
    return jax.shard_map(body, mesh=mesh, in_specs=in_specs, out_specs=out_specs, check_vma=False)
```

```python
import jax
import jax.numpy as jnp
from jax import lax
from jax.experimental import pallas as pl
from jax.experimental.pallas import tpu as pltpu
from jax.sharding import PartitionSpec as P

focal_length = 1100.0
centre_x = 960.0
centre_y = 540.0
beta_one = 0.9
beta_two = 0.999
adam_eps = 1e-15
adam_step = 100.0
log2_e = 1.4426950408889634
sh_zero = 0.28209479177387814
sh_one = 0.4886025119029199
sh_two = [
    1.0925484305920792,
    -1.0925484305920792,
    0.31539156525252005,
    -1.0925484305920792,
    0.5462742152960396,
]
sh_three = [
    -0.5900435899266435,
    2.890611442640554,
    -0.4570457994644658,
    0.3731763325901154,
    -0.4570457994644658,
    1.445305721320277,
    -0.5900435899266435,
]
LINE = 16
SIDE = 4
CHIPS = LINE * SIDE
VIEWS = 4
MESH = pl.DeviceIdType.MESH
f32 = jnp.float32
bf16 = jnp.bfloat16


def harmonics(dir_x, dir_y, dir_z):
    sq_x = dir_x * dir_x
    sq_y = dir_y * dir_y
    sq_z = dir_z * dir_z
    return [
        -sh_one * dir_y,
        sh_one * dir_z,
        -sh_one * dir_x,
        sh_two[0] * dir_x * dir_y,
        sh_two[1] * dir_y * dir_z,
        sh_two[2] * (2.0 * sq_z - sq_x - sq_y),
        sh_two[3] * dir_x * dir_z,
        sh_two[4] * (sq_x - sq_y),
        sh_three[0] * dir_y * (3.0 * sq_x - sq_y),
        sh_three[1] * dir_x * dir_y * dir_z,
        sh_three[2] * dir_y * (4.0 * sq_z - sq_x - sq_y),
        sh_three[3] * dir_z * (2.0 * sq_z - 3.0 * sq_x - 3.0 * sq_y),
        sh_three[4] * dir_x * (4.0 * sq_z - sq_x - sq_y),
        sh_three[5] * dir_z * (sq_x - sq_y),
        sh_three[6] * dir_x * (sq_x - 3.0 * sq_y),
    ]


def project(columns, camera):
    mean_x, mean_y, mean_z = columns[0], columns[1], columns[2]
    scales = [jnp.exp(columns[3 + axis]) for axis in range(3)]
    quat_w, quat_x, quat_y, quat_z = columns[6:10]
    norm = 1.0 / jnp.sqrt(quat_w * quat_w + quat_x * quat_x + quat_y * quat_y + quat_z * quat_z)
    quat_w, quat_x, quat_y, quat_z = quat_w * norm, quat_x * norm, quat_y * norm, quat_z * norm
    turn = [
        [
            1.0 - 2.0 * (quat_y * quat_y + quat_z * quat_z),
            2.0 * (quat_x * quat_y - quat_w * quat_z),
            2.0 * (quat_x * quat_z + quat_w * quat_y),
        ],
        [
            2.0 * (quat_x * quat_y + quat_w * quat_z),
            1.0 - 2.0 * (quat_x * quat_x + quat_z * quat_z),
            2.0 * (quat_y * quat_z - quat_w * quat_x),
        ],
        [
            2.0 * (quat_x * quat_z - quat_w * quat_y),
            2.0 * (quat_y * quat_z + quat_w * quat_x),
            1.0 - 2.0 * (quat_x * quat_x + quat_y * quat_y),
        ],
    ]
    world = [[turn[outer][inner] * scales[inner] for inner in range(3)] for outer in range(3)]
    cam_x, cam_y, depth = [
        camera[3 * outer] * mean_x
        + camera[3 * outer + 1] * mean_y
        + camera[3 * outer + 2] * mean_z
        + camera[9 + outer]
        for outer in range(3)
    ]
    framed = [
        [
            camera[3 * outer] * world[0][inner]
            + camera[3 * outer + 1] * world[1][inner]
            + camera[3 * outer + 2] * world[2][inner]
            for inner in range(3)
        ]
        for outer in range(3)
    ]
    inverse = 1.0 / depth
    near = focal_length * inverse
    slope_x = cam_x * inverse
    slope_y = cam_y * inverse
    row_top = [near * (framed[0][inner] - slope_x * framed[2][inner]) for inner in range(3)]
    row_low = [near * (framed[1][inner] - slope_y * framed[2][inner]) for inner in range(3)]
    cov_a = row_top[0] * row_top[0] + row_top[1] * row_top[1] + row_top[2] * row_top[2] + 0.3
    cov_b = row_top[0] * row_low[0] + row_top[1] * row_low[1] + row_top[2] * row_low[2]
    cov_c = row_low[0] * row_low[0] + row_low[1] * row_low[1] + row_low[2] * row_low[2] + 0.3
    over = 1.0 / (cov_a * cov_c - cov_b * cov_b)
    centre_u = focal_length * slope_x + centre_x
    centre_v = focal_length * slope_y + centre_y
    away = 1.0 / jnp.sqrt(cam_x * cam_x + cam_y * cam_y + depth * depth)
    basis = harmonics(cam_x * away, cam_y * away, depth * away)
    colours = []
    for channel in range(3):
        total = 0.5 + sh_zero * columns[11 + channel]
        for order in range(15):
            total = total + basis[order] * columns[14 + 3 * order + channel]
        colours.append(total)
    opacity = 1.0 / (1.0 + jnp.exp(-columns[10]))
    return [
        centre_u,
        centre_v,
        cov_c * over,
        -cov_b * over,
        cov_a * over,
        opacity,
        colours[0],
        colours[1],
        colours[2],
    ]


def pieces(value):
    high = value.astype(bf16)
    rest = value - high.astype(f32)
    middle = rest.astype(bf16)
    low = (rest - middle.astype(f32)).astype(bf16)
    return high, middle, low


def dot_rows(left, right):
    return lax.dot_general(left, right, (((1,), (1,)), ((), ())), preferred_element_type=f32)


def add_pieces(stacked):
    rows = stacked.shape[0] // 3
    return (stacked[0:rows] + stacked[rows : 2 * rows]) + stacked[2 * rows :]


def dot_exact(left, right):
    stacked = jnp.concatenate(pieces(left), axis=0)
    return add_pieces(jnp.dot(stacked, right, preferred_element_type=f32))


def dot_rows_exact(left, right):
    return add_pieces(dot_rows(jnp.concatenate(pieces(left), axis=0), right))


def iota(shape, axis):
    return lax.broadcasted_iota(jnp.int32, shape, axis)


def one_hot(test):
    return jnp.where(test, 1.0, 0.0).astype(bf16)


def swap(value):
    return pltpu.roll(value, 64, 1)


def reorder_row(row, width, place):
    split = jnp.concatenate([row >> 4, row & 15, jnp.zeros((6, width), jnp.int32)], axis=0)
    chosen = one_hot(iota((width, width), 0) == place(iota((width, width), 1)))
    moved = jnp.dot(split.astype(f32).astype(bf16), chosen, preferred_element_type=f32)
    return (moved[0:1] * 16.0 + moved[1:2]).astype(jnp.int32)


def sender_table(rows):
    moved = reorder_row(rows, 512, lambda n: 8 * (n & 63) + (n >> 6))
    return one_hot(iota((512, 512), 0) == moved)


def pack_messages(attributes, table):
    placed = dot_exact(attributes, table)
    parts = []
    for pair in range(4):
        both = placed[:, 128 * pair : 128 * pair + 128]
        parts += [both, swap(both)]
    return jnp.transpose(jnp.concatenate(parts, axis=0))[0:64]


def unpack_messages(messages, table):
    turned = jnp.transpose(jnp.concatenate([messages, jnp.zeros_like(messages)], axis=0))
    keep = iota((16, 128), 1) < 64
    parts = []
    for pair in range(4):
        left = turned[32 * pair : 32 * pair + 16]
        right = turned[32 * pair + 16 : 32 * pair + 32]
        parts.append(jnp.where(keep, left, swap(right)))
    return dot_rows_exact(jnp.concatenate(parts, axis=1), table)


def list_tables(lists):
    moved = []
    for tile in range(2):
        moved.append(reorder_row(lists[tile : tile + 1], 256, lambda n: 32 * (n & 7) + (n >> 3)))
    slot = jnp.concatenate(moved, axis=1)
    return one_hot(iota((64, 512), 0) == (slot >> 3)), slot & 7


def pick(received, table, group):
    turned = jnp.transpose(jnp.concatenate([received, jnp.zeros_like(received)], axis=0))[:, 0:64]
    found = dot_exact(turned, table)
    found = jnp.where((iota((128, 512), 0) >> 4) == group, found, 0.0)
    total = found[0:16]
    for part in range(1, 8):
        total = total + found[16 * part : 16 * part + 16]
    return total


def unpick(grads, table, group):
    spread = jnp.concatenate([grads] * 8, axis=0)
    spread = jnp.where((iota((128, 512), 0) >> 4) == group, spread, 0.0)
    turned = dot_rows_exact(spread, table)
    return jnp.transpose(jnp.concatenate([turned, jnp.zeros((128, 64), f32)], axis=1))[0:64]


def place_of(position):
    return 32 * (position & 7) + (position >> 3)


def prepare_tile(attributes, count, tile_id):
    across = (16 * lax.rem(tile_id, 120)).astype(f32) + 7.5
    down = (16 * lax.div(tile_id, 120)).astype(f32) + 7.5
    centre_u = attributes[0:1] - across
    centre_v = attributes[1:2] - down
    alive = place_of(iota((1, 256), 1)) < count
    rows = [
        centre_u,
        centre_v,
        attributes[2:3] * (-0.5 * log2_e),
        attributes[3:4] * (-log2_e),
        attributes[4:5] * (-0.5 * log2_e),
        jnp.where(alive, attributes[5:6], 0.0),
        attributes[6:7],
        attributes[7:8],
        attributes[8:9],
        jnp.zeros((119, 256), f32),
    ]
    return jnp.transpose(jnp.concatenate(rows, axis=0)), centre_u, centre_v


def pixels():
    number = iota((1, 256), 1)
    return (number & 15).astype(f32) - 7.5, (number >> 4).astype(f32) - 7.5


def shade_step(columns, pixel_x, pixel_y, carry):
    keep, colour = carry
    offset_x = pixel_x - columns[:, 0:1]
    offset_y = pixel_y - columns[:, 1:2]
    power = offset_x * (columns[:, 2:3] * offset_x + columns[:, 3:4] * offset_y) + (
        columns[:, 4:5] * offset_y
    ) * offset_y
    alpha = columns[:, 5:6] * jnp.exp2(power)
    weight = keep * alpha
    colour = [colour[c] + weight * columns[:, 6 + c : 7 + c] for c in range(3)]
    return alpha, weight, (keep * (1.0 - alpha), colour)


def between(keep, colour, target):
    before = [jnp.ones((1, 256), f32)]
    for chunk in range(7):
        before.append(before[-1] * keep[chunk : chunk + 1])
    before = jnp.concatenate(before, axis=0)
    colour = [part * before for part in colour]
    residual = [jnp.sum(colour[c], axis=0, keepdims=True) - target[c : c + 1] for c in range(3)]
    own = residual[0] * colour[0] + residual[1] * colour[1] + residual[2] * colour[2]
    after = [jnp.zeros((1, 256), f32)]
    for chunk in range(7, 0, -1):
        after.append(after[-1] + own[chunk : chunk + 1])
    after = jnp.concatenate(after[::-1], axis=0)
    squares = residual[0] * residual[0] + residual[1] * residual[1] + residual[2] * residual[2]
    return before, after, residual, 0.5 * jnp.sum(squares, axis=1, keepdims=True)


def back_step(columns, alpha, weight, before, after, residual, later):
    shade = (
        residual[0] * columns[:, 6:7] + residual[1] * columns[:, 7:8] + residual[2] * columns[:, 8:9]
    )
    own = weight * shade
    left = 1.0 - alpha
    guess = pl.reciprocal(left, approx=True)
    ratio = alpha * (guess * (2.0 - left * guess))
    slope = before * (own - later * ratio) - after * ratio
    return slope, before * weight, later + own


def moments(slope, weight, residual):
    pixel_x, pixel_y = pixels()
    ones = jnp.ones((1, 256), f32)
    powers = [ones, pixel_x, pixel_y, pixel_x * pixel_x, pixel_x * pixel_y, pixel_y * pixel_y]
    shown = [part.astype(f32) for part in pieces(jnp.concatenate(residual, axis=0))]
    factors = jnp.concatenate(powers + shown + [jnp.zeros((1, 256), f32)], axis=0).astype(bf16)

    def over_pixels(value):
        return sum(dot_rows(factors, part) for part in pieces(value)[::-1])

    by_power = over_pixels(slope)[0:6]
    by_shown = over_pixels(weight)
    by_shown = by_shown[6:9] + (by_shown[9:12] + by_shown[12:15])
    return jnp.concatenate([by_power, by_shown], axis=0)


def finish_tile(sums, attributes, centre_u, centre_v):
    whole, by_x, by_y, by_xx, by_xy, by_yy = [sums[n : n + 1] for n in range(6)]
    sum_x = by_x - centre_u * whole
    sum_y = by_y - centre_v * whole
    sum_xx = by_xx - centre_u * (by_x + sum_x)
    sum_xy = by_xy - centre_u * by_y - centre_v * sum_x
    sum_yy = by_yy - centre_v * (by_y + sum_y)
    conic = [attributes[2 + n : 3 + n] for n in range(3)]
    rows = [
        conic[0] * sum_x + conic[1] * sum_y,
        conic[1] * sum_x + conic[2] * sum_y,
        -0.5 * sum_xx,
        -sum_xy,
        -0.5 * sum_yy,
        whole,
        sums[6:9],
        jnp.zeros((7, 256), f32),
    ]
    return jnp.concatenate(rows, axis=0)


def exchange(
    params_in,
    first_in,
    second_in,
    camera_in,
    rows_in,
    lists_in,
    counts_in,
    tile_ids_in,
    target_in,
    params,
    first,
    second,
    out,
    loss,
    camera,
    rows,
    lists,
    counts,
    tile_ids,
    target,
    msg,
    land1,
    land2,
    back1,
    land3,
    back2,
    land4,
    own,
    land5,
    columns,
    alphas,
    weights,
    table,
    loads,
    send1,
    recv1,
    send2,
    recv2,
    send3,
    recv3,
    send4,
    recv4,
    send5,
    recv5,
):
    here = lax.axis_index("gauss")
    view = lax.axis_index("view")
    core = lax.rem(here, 2)
    chip = here // 2
    line = chip // SIDE
    side = lax.rem(chip, SIDE)

    def on_chip(step_z, step_x):
        other = lax.rem(line + step_z, LINE) * SIDE + lax.rem(side + step_x, SIDE)
        return other, {"gauss": other * 2 + core, "view": view}

    def far_first(action):
        def one(step, unused):
            step_z = LINE // 2 + (1 - 2 * (step & 1)) * ((step + 1) >> 1)
            for step_x in (2, 1, 3, 0):
                action(*on_chip(step_z, step_x))
            return unused

        lax.fori_loop(0, LINE - 1, one, 0)
        for step_x in (2, 1, 3):
            action(*on_chip(0, step_x))

    other_core = {"gauss": here + 1 - 2 * core, "view": view}

    def over_views(action):
        for step in (2, 1, 3):
            other = lax.rem(view + step, VIEWS)
            action(step, other, {"gauss": here, "view": other})

    barrier = pltpu.get_barrier_semaphore()

    def greet(device):
        pl.semaphore_signal(barrier, inc=1, device_id=device, device_id_type=MESH)

    far_first(lambda other, device: greet(device))
    over_views(lambda step, other, device: greet(device))
    greet(other_core)

    pairs = [
        (rows_in, rows),
        (params_in, params),
        (camera_in, camera),
        (lists_in, lists),
        (counts_in, counts),
        (tile_ids_in, tile_ids),
        (target_in, target),
        (first_in, first),
        (second_in, second),
    ]
    copies = [
        pltpu.make_async_copy(source, place, loads.at[n]) for n, (source, place) in enumerate(pairs)
    ]
    for copy in copies:
        copy.start()

    def remote(source, place, sent, arrived, device):
        return pltpu.make_async_remote_copy(
            src_ref=source,
            dst_ref=place,
            send_sem=sent,
            recv_sem=arrived,
            device_id=device,
            device_id_type=MESH,
        )

    def to_chips(source, place, sent, arrived):
        def send(other, device):
            remote(source.at[other], place.at[chip], sent, arrived, device).start()

        far_first(send)
        place[chip] = source[chip]

    def from_chips(place, arrived):
        whole = place.at[pl.ds(0, CHIPS - 1)]
        pltpu.make_async_copy(whole, whole, arrived).wait()

    low_lanes = iota((64, 128), 1) < 64
    mine = low_lanes == (core == 0)

    def with_other_core(source, place, sent, arrived):
        copy = remote(source, place, sent, arrived, other_core)
        copy.start()
        copy.wait()
        kept = source[...].reshape(64, 128)
        return jnp.where(mine, kept, swap(place[...].reshape(64, 128)))

    copies[0].wait()
    table[...] = sender_table(rows[0])
    copies[1].wait()
    copies[2].wait()
    scalars = [camera[0, n] for n in range(12)]
    attributes = project([params[n : n + 1, :] for n in range(59)], scalars)
    messages = pack_messages(
        jnp.concatenate(attributes + [jnp.zeros((7, 512), f32)], axis=0), table[...]
    )
    msg[...] = messages.reshape(CHIPS, 1, 128)
    for copy in copies[3:]:
        copy.wait()

    pl.semaphore_wait(barrier, CHIPS + VIEWS - 1)
    to_chips(msg, land1, send1, recv1)
    picked, lane_group = list_tables(lists[0])
    from_chips(land1, recv1)
    received = with_other_core(land1, land2, send2, recv2)

    found = pick(received, picked, lane_group)
    pixel_x, pixel_y = pixels()
    centres = []
    for tile in range(2):
        entries = found[:, 256 * tile : 256 * tile + 256]
        filled, centre_u, centre_v = prepare_tile(entries, counts[0, tile], tile_ids[0, tile])
        columns[tile] = filled
        centres.append((entries, centre_u, centre_v))

    def forward(step, carry):
        rows_here = pl.ds(pl.multiple_of(step * 8, 8), 8)
        left = []
        for tile in range(2):
            alpha, weight, rest = shade_step(
                columns[tile, rows_here, :], pixel_x, pixel_y, carry[tile]
            )
            alphas[tile, rows_here, :] = alpha
            weights[tile, rows_here, :] = weight
            left.append(rest)
        return left

    fresh = (jnp.ones((8, 256), f32), [jnp.zeros((8, 256), f32)] * 3)
    carry = lax.fori_loop(0, 32, forward, [fresh, fresh], unroll=4)
    around = []
    for tile in range(2):
        around.append(between(carry[tile][0], carry[tile][1], target[:, tile, :]))
    spot = iota((1, 128), 1)
    loss[...] = jnp.where(spot == 0, around[0][3], jnp.where(spot == 1, around[1][3], 0.0))

    def backward(step, later):
        rows_here = pl.ds(pl.multiple_of((31 - step) * 8, 8), 8)
        left = []
        for tile in range(2):
            before, after, residual, unused = around[tile]
            slope, weight, rest = back_step(
                columns[tile, rows_here, :],
                alphas[tile, rows_here, :],
                weights[tile, rows_here, :],
                before,
                after,
                residual,
                later[tile],
            )
            alphas[tile, rows_here, :] = slope
            weights[tile, rows_here, :] = weight
            left.append(rest)
        return left

    lax.fori_loop(0, 32, backward, [jnp.zeros((8, 256), f32)] * 2, unroll=4)
    grads = []
    for tile in range(2):
        sums = moments(alphas[tile], weights[tile], around[tile][2])
        grads.append(finish_tile(sums, *centres[tile]))
    grads = jnp.concatenate(grads, axis=1)
    back1[...] = unpick(grads, picked, lane_group)

    back2[...] = with_other_core(back1, land3, send3, recv3).reshape(CHIPS, 1, 128)
    to_chips(back2, land4, send4, recv4)
    from_chips(land4, recv4)
    returned = unpack_messages(land4[...].reshape(64, 128), table[...])

    lanes = iota((1, 128), 1)
    pose = jnp.zeros((1, 128), f32)
    for n in range(12):
        pose = jnp.where(lanes == n, scalars[n], pose)
    for part in range(4):
        own[10 * part : 10 * part + 9, :] = returned[0:9, 128 * part : 128 * part + 128]
        own[10 * part + 9 : 10 * part + 10, :] = pose

    def share(step, other, device):
        remote(own, land5.at[view], send5.at[step], recv5.at[view], device).start()

    def take(step, other, device):
        remote(own, land5.at[other], send5.at[step], recv5.at[other], device).wait()

    over_views(share)
    land5[view] = own[...]
    over_views(take)
    out[...] = land5[...]

    for sent, buffer in ((send1, msg), (send4, back2)):
        whole = buffer.at[pl.ds(0, CHIPS - 1)]
        pltpu.make_async_copy(whole, whole, sent).wait()


def update(
    params, first, second, grads, loss, new_params, new_first, new_second, tile_loss, spread, total
):
    for part in range(4):
        block = params[:, 128 * part : 128 * part + 128]
        for view in range(VIEWS):
            start = 64 * (4 * view + part)
            spread[start : start + 59, :] = block
    columns = [spread[pl.ds(n, 16, stride=64), :] for n in range(59)]
    given = [grads[pl.ds(n, 16, stride=10), :] for n in range(10)]
    camera = [given[9][:, n : n + 1] for n in range(12)]

    def shown(rows):
        attributes = project(rows, camera)
        return attributes[0:5] + attributes[6:9]

    pulled = jax.vjp(shown, columns)[1](given[0:5] + given[6:9])[0]
    pulled[10] = given[5] * (1.0 - 1.0 / (1.0 + jnp.exp(-columns[10])))
    for n in range(59):
        both = pulled[n][0:8] + pulled[n][8:16]
        total[pl.ds(n, 4, stride=64), :] = both[0:4] + both[4:8]
    row = iota((59, 1), 0)
    rate = jnp.where(row < 3, 0.00016, 0.005)
    rate = jnp.where(row < 6, rate, 0.001)
    rate = jnp.where(row < 10, rate, 0.05)
    rate = jnp.where(row < 11, rate, 0.0025)
    rate = jnp.where(row < 14, rate, 0.000125)
    rate = rate / (1.0 - beta_one**adam_step)
    for part in range(4):
        here = slice(128 * part, 128 * part + 128)
        slope = total[64 * part : 64 * part + 59, :]
        moved = beta_one * first[:, here] + (1.0 - beta_one) * slope
        square = beta_two * second[:, here] + (1.0 - beta_two) * slope * slope
        new_first[:, here] = moved
        new_second[:, here] = square
        new_params[:, here] = params[:, here] - rate * moved / (
            jnp.sqrt(square / (1.0 - beta_two**adam_step)) + adam_eps
        )
    tile_loss[...] = loss[:, 0:2]


def body(params, first_moment, second_moment, cameras, send_rows, lists, counts, tile_ids, target):
    vmem = pl.BlockSpec(memory_space=pltpu.VMEM)
    hbm = pl.BlockSpec(memory_space=pltpu.HBM)
    dma = pltpu.SemaphoreType.DMA
    whole = jax.ShapeDtypeStruct((59, 512), f32)
    messages = pltpu.VMEM((CHIPS, 1, 128), f32)
    params_near, first_near, second_near, grads, loss = pl.pallas_call(
        exchange,
        out_shape=(
            whole,
            whole,
            whole,
            jax.ShapeDtypeStruct((VIEWS, 40, 128), f32),
            jax.ShapeDtypeStruct((1, 128), f32),
        ),
        in_specs=[hbm] * 9,
        out_specs=(vmem,) * 5,
        scratch_shapes=[
            pltpu.SMEM((1, 12), f32),
            pltpu.VMEM((1, 1, 512), jnp.int32),
            pltpu.VMEM((1, 2, 256), jnp.int32),
            pltpu.SMEM((1, 2), jnp.int32),
            pltpu.SMEM((1, 2), jnp.int32),
            pltpu.VMEM((3, 2, 256), f32),
            messages,
            messages,
            messages,
            pltpu.VMEM((CHIPS, 128), f32),
            pltpu.VMEM((CHIPS, 128), f32),
            messages,
            messages,
            pltpu.VMEM((40, 128), f32),
            pltpu.VMEM((VIEWS, 40, 128), f32),
            pltpu.VMEM((2, 256, 128), f32),
            pltpu.VMEM((2, 256, 256), f32),
            pltpu.VMEM((2, 256, 256), f32),
            pltpu.VMEM((512, 512), bf16),
            dma((9,)),
            dma,
            dma,
            dma,
            dma,
            dma,
            dma,
            dma,
            dma,
            dma((VIEWS,)),
            dma((VIEWS,)),
        ],
        compiler_params=pltpu.CompilerParams(
            collective_id=0, has_side_effects=True, vmem_limit_bytes=32 * 1024 * 1024
        ),
        name="exchange",
    )(
        params,
        first_moment,
        second_moment,
        cameras,
        send_rows,
        lists,
        counts,
        tile_ids,
        target[0].transpose(1, 0, 2),
    )
    return pl.pallas_call(
        update,
        out_shape=(whole, whole, whole, jax.ShapeDtypeStruct((1, 2), f32)),
        in_specs=[vmem] * 5,
        out_specs=(vmem,) * 4,
        scratch_shapes=[pltpu.VMEM((1024, 128), f32), pltpu.VMEM((256, 128), f32)],
        compiler_params=pltpu.CompilerParams(vmem_limit_bytes=32 * 1024 * 1024),
        name="update",
    )(params_near, first_near, second_near, grads.reshape(VIEWS * 40, 128), loss)


def solution(mesh):
    in_specs = (
        P(None, "gauss"),
        P(None, "gauss"),
        P(None, "gauss"),
        P("view", None),
        P("view", "gauss", None),
        P("view", "gauss", None),
        P("view", "gauss"),
        P("view", "gauss"),
        P("view", "gauss", None, None),
    )
    out_specs = (P(None, "gauss"), P(None, "gauss"), P(None, "gauss"), P("view", "gauss"))
    return jax.shard_map(body, mesh=mesh, in_specs=in_specs, out_specs=out_specs, check_vma=False)
```

```python
import jax
import jax.numpy as jnp
from jax import lax
from jax.experimental import pallas as pl
from jax.experimental.pallas import tpu as pltpu
from jax.sharding import PartitionSpec as P

focal_length = 1100.0
centre_x = 960.0
centre_y = 540.0
beta_one = 0.9
beta_two = 0.999
adam_eps = 1e-15
adam_step = 100.0
log2_e = 1.4426950408889634
sh_zero = 0.28209479177387814
sh_one = 0.4886025119029199
sh_two = [
    1.0925484305920792,
    -1.0925484305920792,
    0.31539156525252005,
    -1.0925484305920792,
    0.5462742152960396,
]
sh_three = [
    -0.5900435899266435,
    2.890611442640554,
    -0.4570457994644658,
    0.3731763325901154,
    -0.4570457994644658,
    1.445305721320277,
    -0.5900435899266435,
]
LINE = 16
SIDE = 4
CHIPS = LINE * SIDE
VIEWS = 4
VMEM_BYTES = 62 * 1024 * 1024
MESH = pl.DeviceIdType.MESH
f32 = jnp.float32
bf16 = jnp.bfloat16


def harmonics(dir_x, dir_y, dir_z):
    sq_x = dir_x * dir_x
    sq_y = dir_y * dir_y
    sq_z = dir_z * dir_z
    return [
        -sh_one * dir_y,
        sh_one * dir_z,
        -sh_one * dir_x,
        sh_two[0] * dir_x * dir_y,
        sh_two[1] * dir_y * dir_z,
        sh_two[2] * (2.0 * sq_z - sq_x - sq_y),
        sh_two[3] * dir_x * dir_z,
        sh_two[4] * (sq_x - sq_y),
        sh_three[0] * dir_y * (3.0 * sq_x - sq_y),
        sh_three[1] * dir_x * dir_y * dir_z,
        sh_three[2] * dir_y * (4.0 * sq_z - sq_x - sq_y),
        sh_three[3] * dir_z * (2.0 * sq_z - 3.0 * sq_x - 3.0 * sq_y),
        sh_three[4] * dir_x * (4.0 * sq_z - sq_x - sq_y),
        sh_three[5] * dir_z * (sq_x - sq_y),
        sh_three[6] * dir_x * (sq_x - 3.0 * sq_y),
    ]


def project(columns, camera):
    mean_x, mean_y, mean_z = columns[0], columns[1], columns[2]
    scales = [jnp.exp(columns[3 + axis]) for axis in range(3)]
    quat_w, quat_x, quat_y, quat_z = columns[6:10]
    norm = 1.0 / jnp.sqrt(quat_w * quat_w + quat_x * quat_x + quat_y * quat_y + quat_z * quat_z)
    quat_w, quat_x, quat_y, quat_z = quat_w * norm, quat_x * norm, quat_y * norm, quat_z * norm
    turn = [
        [
            1.0 - 2.0 * (quat_y * quat_y + quat_z * quat_z),
            2.0 * (quat_x * quat_y - quat_w * quat_z),
            2.0 * (quat_x * quat_z + quat_w * quat_y),
        ],
        [
            2.0 * (quat_x * quat_y + quat_w * quat_z),
            1.0 - 2.0 * (quat_x * quat_x + quat_z * quat_z),
            2.0 * (quat_y * quat_z - quat_w * quat_x),
        ],
        [
            2.0 * (quat_x * quat_z - quat_w * quat_y),
            2.0 * (quat_y * quat_z + quat_w * quat_x),
            1.0 - 2.0 * (quat_x * quat_x + quat_y * quat_y),
        ],
    ]
    world = [[turn[outer][inner] * scales[inner] for inner in range(3)] for outer in range(3)]
    cam_x, cam_y, depth = [
        camera[3 * outer] * mean_x
        + camera[3 * outer + 1] * mean_y
        + camera[3 * outer + 2] * mean_z
        + camera[9 + outer]
        for outer in range(3)
    ]
    framed = [
        [
            camera[3 * outer] * world[0][inner]
            + camera[3 * outer + 1] * world[1][inner]
            + camera[3 * outer + 2] * world[2][inner]
            for inner in range(3)
        ]
        for outer in range(3)
    ]
    inverse = 1.0 / depth
    near = focal_length * inverse
    slope_x = cam_x * inverse
    slope_y = cam_y * inverse
    row_top = [near * (framed[0][inner] - slope_x * framed[2][inner]) for inner in range(3)]
    row_low = [near * (framed[1][inner] - slope_y * framed[2][inner]) for inner in range(3)]
    cov_a = row_top[0] * row_top[0] + row_top[1] * row_top[1] + row_top[2] * row_top[2] + 0.3
    cov_b = row_top[0] * row_low[0] + row_top[1] * row_low[1] + row_top[2] * row_low[2]
    cov_c = row_low[0] * row_low[0] + row_low[1] * row_low[1] + row_low[2] * row_low[2] + 0.3
    over = 1.0 / (cov_a * cov_c - cov_b * cov_b)
    centre_u = focal_length * slope_x + centre_x
    centre_v = focal_length * slope_y + centre_y
    away = 1.0 / jnp.sqrt(cam_x * cam_x + cam_y * cam_y + depth * depth)
    basis = harmonics(cam_x * away, cam_y * away, depth * away)
    colours = []
    for channel in range(3):
        total = 0.5 + sh_zero * columns[11 + channel]
        for order in range(15):
            total = total + basis[order] * columns[14 + 3 * order + channel]
        colours.append(total)
    opacity = 1.0 / (1.0 + jnp.exp(-columns[10]))
    return [
        centre_u,
        centre_v,
        cov_c * over,
        -cov_b * over,
        cov_a * over,
        opacity,
        colours[0],
        colours[1],
        colours[2],
    ]


def pieces(value):
    high = value.astype(bf16)
    rest = value - high.astype(f32)
    middle = rest.astype(bf16)
    low = (rest - middle.astype(f32)).astype(bf16)
    return high, middle, low


def dot_rows(left, right):
    return lax.dot_general(left, right, (((1,), (1,)), ((), ())), preferred_element_type=f32)


def add_pieces(stacked):
    rows = stacked.shape[0] // 3
    return (stacked[0:rows] + stacked[rows : 2 * rows]) + stacked[2 * rows :]


def dot_exact(left, right):
    stacked = jnp.concatenate(pieces(left), axis=0)
    return add_pieces(jnp.dot(stacked, right, preferred_element_type=f32))


def dot_rows_exact(left, right):
    return add_pieces(dot_rows(jnp.concatenate(pieces(left), axis=0), right))


def iota(shape, axis):
    return lax.broadcasted_iota(jnp.int32, shape, axis)


def one_hot(test):
    return jnp.where(test, 1.0, 0.0).astype(bf16)


def swap(value):
    return pltpu.roll(value, 64, 1)


def reorder_row(row, width, place):
    split = jnp.concatenate([row >> 4, row & 15, jnp.zeros((6, width), jnp.int32)], axis=0)
    chosen = one_hot(iota((width, width), 0) == place(iota((width, width), 1)))
    moved = jnp.dot(split.astype(f32).astype(bf16), chosen, preferred_element_type=f32)
    return (moved[0:1] * 16.0 + moved[1:2]).astype(jnp.int32)


def sender_table(rows):
    moved = reorder_row(rows, 512, lambda n: 8 * (n & 63) + (n >> 6))
    return one_hot(iota((512, 512), 0) == moved)


def pack_messages(attributes, table):
    placed = dot_exact(attributes, table)
    parts = []
    for pair in range(4):
        both = placed[:, 128 * pair : 128 * pair + 128]
        parts += [both, swap(both)]
    return jnp.transpose(jnp.concatenate(parts, axis=0))[0:64]


def unpack_messages(messages, table):
    turned = jnp.transpose(jnp.concatenate([messages, jnp.zeros_like(messages)], axis=0))
    keep = iota((16, 128), 1) < 64
    parts = []
    for pair in range(4):
        left = turned[32 * pair : 32 * pair + 16]
        right = turned[32 * pair + 16 : 32 * pair + 32]
        parts.append(jnp.where(keep, left, swap(right)))
    return dot_rows_exact(jnp.concatenate(parts, axis=1), table)


def list_tables(lists):
    moved = []
    for tile in range(2):
        moved.append(reorder_row(lists[tile : tile + 1], 256, lambda n: 32 * (n & 7) + (n >> 3)))
    slot = jnp.concatenate(moved, axis=1)
    return one_hot(iota((64, 512), 0) == (slot >> 3)), slot & 7


def pick(received, table, group):
    turned = jnp.transpose(jnp.concatenate([received, jnp.zeros_like(received)], axis=0))[:, 0:64]
    found = dot_exact(turned, table)
    found = jnp.where((iota((128, 512), 0) >> 4) == group, found, 0.0)
    total = found[0:16]
    for part in range(1, 8):
        total = total + found[16 * part : 16 * part + 16]
    return total


def unpick(grads, table, group):
    spread = jnp.concatenate([grads] * 8, axis=0)
    spread = jnp.where((iota((128, 512), 0) >> 4) == group, spread, 0.0)
    turned = dot_rows_exact(spread, table)
    return jnp.transpose(jnp.concatenate([turned, jnp.zeros((128, 64), f32)], axis=1))[0:64]


def place_of(position):
    return 32 * (position & 7) + (position >> 3)


def prepare_tile(attributes, count, tile_id):
    across = (16 * lax.rem(tile_id, 120)).astype(f32) + 7.5
    down = (16 * lax.div(tile_id, 120)).astype(f32) + 7.5
    centre_u = attributes[0:1] - across
    centre_v = attributes[1:2] - down
    alive = place_of(iota((1, 256), 1)) < count
    rows = [
        centre_u,
        centre_v,
        attributes[2:3] * (-0.5 * log2_e),
        attributes[3:4] * (-log2_e),
        attributes[4:5] * (-0.5 * log2_e),
        jnp.where(alive, attributes[5:6], 0.0),
        attributes[6:7],
        attributes[7:8],
        attributes[8:9],
        jnp.zeros((119, 256), f32),
    ]
    return jnp.transpose(jnp.concatenate(rows, axis=0)), centre_u, centre_v


def pixels():
    number = iota((1, 256), 1)
    return (number & 15).astype(f32) - 7.5, (number >> 4).astype(f32) - 7.5


def shade_step(columns, pixel_x, pixel_y, carry):
    keep, colour = carry
    offset_x = pixel_x - columns[:, 0:1]
    offset_y = pixel_y - columns[:, 1:2]
    power = offset_x * (columns[:, 2:3] * offset_x + columns[:, 3:4] * offset_y) + (
        columns[:, 4:5] * offset_y
    ) * offset_y
    alpha = columns[:, 5:6] * jnp.exp2(power)
    weight = keep * alpha
    colour = [colour[c] + weight * columns[:, 6 + c : 7 + c] for c in range(3)]
    return alpha, weight, (keep * (1.0 - alpha), colour)


def between(keep, colour, target):
    before = [jnp.ones((1, 256), f32)]
    for chunk in range(7):
        before.append(before[-1] * keep[chunk : chunk + 1])
    before = jnp.concatenate(before, axis=0)
    colour = [part * before for part in colour]
    residual = [jnp.sum(colour[c], axis=0, keepdims=True) - target[c : c + 1] for c in range(3)]
    own = residual[0] * colour[0] + residual[1] * colour[1] + residual[2] * colour[2]
    after = [jnp.zeros((1, 256), f32)]
    for chunk in range(7, 0, -1):
        after.append(after[-1] + own[chunk : chunk + 1])
    after = jnp.concatenate(after[::-1], axis=0)
    squares = residual[0] * residual[0] + residual[1] * residual[1] + residual[2] * residual[2]
    return before, after, residual, 0.5 * jnp.sum(squares, axis=1, keepdims=True)


def back_step(columns, alpha, weight, before, after, residual, later):
    shade = (
        residual[0] * columns[:, 6:7] + residual[1] * columns[:, 7:8] + residual[2] * columns[:, 8:9]
    )
    own = weight * shade
    left = 1.0 - alpha
    guess = pl.reciprocal(left, approx=True)
    ratio = alpha * (guess * (2.0 - left * guess))
    slope = before * (own - later * ratio) - after * ratio
    return slope, before * weight, later + own


def moments(slope, weight, residual):
    pixel_x, pixel_y = pixels()
    ones = jnp.ones((1, 256), f32)
    powers = [ones, pixel_x, pixel_y, pixel_x * pixel_x, pixel_x * pixel_y, pixel_y * pixel_y]
    shown = [part.astype(f32) for part in pieces(jnp.concatenate(residual, axis=0))]
    factors = jnp.concatenate(powers + shown + [jnp.zeros((1, 256), f32)], axis=0).astype(bf16)

    def over_pixels(value):
        return sum(dot_rows(factors, part) for part in pieces(value)[::-1])

    by_power = over_pixels(slope)[0:6]
    by_shown = over_pixels(weight)
    by_shown = by_shown[6:9] + (by_shown[9:12] + by_shown[12:15])
    return jnp.concatenate([by_power, by_shown], axis=0)


def finish_tile(sums, attributes, centre_u, centre_v):
    whole, by_x, by_y, by_xx, by_xy, by_yy = [sums[n : n + 1] for n in range(6)]
    sum_x = by_x - centre_u * whole
    sum_y = by_y - centre_v * whole
    sum_xx = by_xx - centre_u * (by_x + sum_x)
    sum_xy = by_xy - centre_u * by_y - centre_v * sum_x
    sum_yy = by_yy - centre_v * (by_y + sum_y)
    conic = [attributes[2 + n : 3 + n] for n in range(3)]
    rows = [
        conic[0] * sum_x + conic[1] * sum_y,
        conic[1] * sum_x + conic[2] * sum_y,
        -0.5 * sum_xx,
        -sum_xy,
        -0.5 * sum_yy,
        whole,
        sums[6:9],
        jnp.zeros((7, 256), f32),
    ]
    return jnp.concatenate(rows, axis=0)


def exchange(
    params_in,
    camera_in,
    rows_in,
    lists_in,
    counts_in,
    tile_ids_in,
    target_in,
    out,
    loss,
    params,
    camera,
    rows,
    lists,
    counts,
    tile_ids,
    target,
    msg,
    land1,
    land2,
    back1,
    land3,
    back2,
    land4,
    own,
    losses,
    columns,
    alphas,
    weights,
    table,
    loads,
    send1,
    recv1,
    send2,
    recv2,
    send3,
    recv3,
    send4,
    recv4,
    send5,
    recv5,
    kept5,
):
    here = lax.axis_index("gauss")
    view = lax.axis_index("view")
    core = lax.rem(here, 2)
    chip = here // 2
    line = chip // SIDE
    side = lax.rem(chip, SIDE)

    def on_chip(step_z, step_x):
        other = lax.rem(line + step_z, LINE) * SIDE + lax.rem(side + step_x, SIDE)
        return other, {"gauss": other * 2 + core, "view": view}

    def far_first(action):
        def one(step, unused):
            step_z = LINE // 2 + (1 - 2 * (step & 1)) * ((step + 1) >> 1)
            for step_x in (2, 1, 3, 0):
                action(*on_chip(step_z, step_x))
            return unused

        lax.fori_loop(0, LINE - 1, one, 0)
        for step_x in (2, 1, 3):
            action(*on_chip(0, step_x))

    other_core = {"gauss": here + 1 - 2 * core, "view": view}

    def over_views(action):
        for step in (2, 1, 3):
            other = lax.rem(view + step, VIEWS)
            action(step, other, {"gauss": here, "view": other})

    barrier = pltpu.get_barrier_semaphore()

    def greet(device):
        pl.semaphore_signal(barrier, inc=1, device_id=device, device_id_type=MESH)

    far_first(lambda other, device: greet(device))
    over_views(lambda step, other, device: greet(device))
    greet(other_core)

    pairs = [
        (rows_in, rows),
        (params_in, params),
        (camera_in, camera),
        (lists_in, lists),
        (counts_in, counts),
        (tile_ids_in, tile_ids),
        (target_in, target),
    ]
    copies = [
        pltpu.make_async_copy(source, place, loads.at[n]) for n, (source, place) in enumerate(pairs)
    ]
    for copy in copies:
        copy.start()

    def remote(source, place, sent, arrived, device):
        return pltpu.make_async_remote_copy(
            src_ref=source,
            dst_ref=place,
            send_sem=sent,
            recv_sem=arrived,
            device_id=device,
            device_id_type=MESH,
        )

    def to_chips(source, place, sent, arrived):
        def send(other, device):
            remote(source.at[other], place.at[chip], sent, arrived, device).start()

        far_first(send)
        place[chip] = source[chip]

    def from_chips(place, arrived):
        whole = place.at[pl.ds(0, CHIPS - 1)]
        pltpu.make_async_copy(whole, whole, arrived).wait()

    low_lanes = iota((64, 128), 1) < 64
    mine = low_lanes == (core == 0)

    def with_other_core(source, place, sent, arrived):
        copy = remote(source, place, sent, arrived, other_core)
        copy.start()
        copy.wait()
        kept = source[...].reshape(64, 128)
        return jnp.where(mine, kept, swap(place[...].reshape(64, 128)))

    copies[0].wait()
    table[...] = sender_table(rows[0])
    copies[1].wait()
    copies[2].wait()
    scalars = [camera[0, n] for n in range(12)]
    attributes = project([params[n : n + 1, :] for n in range(59)], scalars)
    messages = pack_messages(
        jnp.concatenate(attributes + [jnp.zeros((7, 512), f32)], axis=0), table[...]
    )
    msg[...] = messages.reshape(CHIPS, 1, 128)
    for copy in copies[3:]:
        copy.wait()

    pl.semaphore_wait(barrier, CHIPS + VIEWS - 1)
    to_chips(msg, land1, send1, recv1)
    picked, lane_group = list_tables(lists[0])
    from_chips(land1, recv1)
    received = with_other_core(land1, land2, send2, recv2)

    found = pick(received, picked, lane_group)
    pixel_x, pixel_y = pixels()
    centres = []
    for tile in range(2):
        entries = found[:, 256 * tile : 256 * tile + 256]
        filled, centre_u, centre_v = prepare_tile(entries, counts[0, tile], tile_ids[0, tile])
        columns[tile] = filled
        centres.append((entries, centre_u, centre_v))

    def forward(step, carry):
        rows_here = pl.ds(pl.multiple_of(step * 8, 8), 8)
        left = []
        for tile in range(2):
            alpha, weight, rest = shade_step(
                columns[tile, rows_here, :], pixel_x, pixel_y, carry[tile]
            )
            alphas[tile, rows_here, :] = alpha
            weights[tile, rows_here, :] = weight
            left.append(rest)
        return left

    fresh = (jnp.ones((8, 256), f32), [jnp.zeros((8, 256), f32)] * 3)
    carry = lax.fori_loop(0, 32, forward, [fresh, fresh], unroll=4)
    around = []
    for tile in range(2):
        around.append(between(carry[tile][0], carry[tile][1], target[:, tile, :]))
    spot = iota((1, 128), 1)
    losses[...] = jnp.where(spot == 0, around[0][3], jnp.where(spot == 1, around[1][3], 0.0))
    loss_copy = pltpu.make_async_copy(losses, loss, loads.at[7])
    loss_copy.start()

    def backward(step, later):
        rows_here = pl.ds(pl.multiple_of((31 - step) * 8, 8), 8)
        left = []
        for tile in range(2):
            before, after, residual, unused = around[tile]
            slope, weight, rest = back_step(
                columns[tile, rows_here, :],
                alphas[tile, rows_here, :],
                weights[tile, rows_here, :],
                before,
                after,
                residual,
                later[tile],
            )
            alphas[tile, rows_here, :] = slope
            weights[tile, rows_here, :] = weight
            left.append(rest)
        return left

    lax.fori_loop(0, 32, backward, [jnp.zeros((8, 256), f32)] * 2, unroll=4)
    grads = []
    for tile in range(2):
        sums = moments(alphas[tile], weights[tile], around[tile][2])
        grads.append(finish_tile(sums, *centres[tile]))
    grads = jnp.concatenate(grads, axis=1)
    back1[...] = unpick(grads, picked, lane_group)

    back2[...] = with_other_core(back1, land3, send3, recv3).reshape(CHIPS, 1, 128)
    to_chips(back2, land4, send4, recv4)
    from_chips(land4, recv4)
    returned = unpack_messages(land4[...].reshape(64, 128), table[...])

    lanes = iota((1, 128), 1)
    pose = jnp.zeros((1, 128), f32)
    for n in range(12):
        pose = jnp.where(lanes == n, scalars[n], pose)
    for part in range(4):
        own[10 * part : 10 * part + 9, :] = returned[0:9, 128 * part : 128 * part + 128]
        own[10 * part + 9 : 10 * part + 10, :] = pose

    def share(step, other, device):
        remote(own, out.at[view], send5.at[step], recv5.at[view], device).start()

    def take(step, other, device):
        remote(own, out.at[other], send5.at[step], recv5.at[other], device).wait()

    over_views(share)
    keep = pltpu.make_async_copy(own, out.at[view], kept5)
    keep.start()
    loss_copy.wait()

    for sent, buffer in ((send1, msg), (send4, back2)):
        whole = buffer.at[pl.ds(0, CHIPS - 1)]
        pltpu.make_async_copy(whole, whole, sent).wait()
    keep.wait()
    over_views(take)


def update(
    params_in,
    first_in,
    second_in,
    grads_in,
    loss_in,
    new_params,
    new_first,
    new_second,
    tile_loss,
    params,
    first,
    second,
    grads,
    loss,
    spread,
    total,
    loads,
):
    pairs = [
        (params_in, params),
        (grads_in, grads),
        (first_in, first),
        (second_in, second),
        (loss_in, loss),
    ]
    copies = [
        pltpu.make_async_copy(source, place, loads.at[n]) for n, (source, place) in enumerate(pairs)
    ]
    for copy in copies:
        copy.start()
    copies[0].wait()

    for part in range(4):
        block = params[:, 128 * part : 128 * part + 128]
        for view in range(VIEWS):
            start = 64 * (4 * view + part)
            spread[start : start + 59, :] = block
    columns = [spread[pl.ds(n, 16, stride=64), :] for n in range(59)]
    copies[1].wait()
    given = [grads[pl.ds(n, 16, stride=10), :] for n in range(10)]
    camera = [given[9][:, n : n + 1] for n in range(12)]

    def shown(rows):
        attributes = project(rows, camera)
        return attributes[0:5] + attributes[6:9]

    pulled = jax.vjp(shown, columns)[1](given[0:5] + given[6:9])[0]
    pulled[10] = given[5] * (1.0 - 1.0 / (1.0 + jnp.exp(-columns[10])))
    for n in range(59):
        both = pulled[n][0:8] + pulled[n][8:16]
        total[pl.ds(n, 4, stride=64), :] = both[0:4] + both[4:8]
    for copy in copies[2:]:
        copy.wait()
    row = iota((59, 1), 0)
    rate = jnp.where(row < 3, 0.00016, 0.005)
    rate = jnp.where(row < 6, rate, 0.001)
    rate = jnp.where(row < 10, rate, 0.05)
    rate = jnp.where(row < 11, rate, 0.0025)
    rate = jnp.where(row < 14, rate, 0.000125)
    rate = rate / (1.0 - beta_one**adam_step)
    for part in range(4):
        here = slice(128 * part, 128 * part + 128)
        slope = total[64 * part : 64 * part + 59, :]
        moved = beta_one * first[:, here] + (1.0 - beta_one) * slope
        square = beta_two * second[:, here] + (1.0 - beta_two) * slope * slope
        new_first[:, here] = moved
        new_second[:, here] = square
        new_params[:, here] = params[:, here] - rate * moved / (
            jnp.sqrt(square / (1.0 - beta_two**adam_step)) + adam_eps
        )
    tile_loss[...] = loss[:, 0:2]


def body(params, first_moment, second_moment, cameras, send_rows, lists, counts, tile_ids, target):
    vmem = pl.BlockSpec(memory_space=pltpu.VMEM)
    hbm = pl.BlockSpec(memory_space=pltpu.HBM)
    dma = pltpu.SemaphoreType.DMA
    whole = jax.ShapeDtypeStruct((59, 512), f32)
    messages = pltpu.VMEM((CHIPS, 1, 128), f32)
    some = pltpu.CompilerParams(vmem_limit_bytes=VMEM_BYTES)
    grads, loss = pl.pallas_call(
        exchange,
        out_shape=(
            jax.ShapeDtypeStruct((VIEWS, 40, 128), f32),
            jax.ShapeDtypeStruct((1, 128), f32),
        ),
        in_specs=[hbm] * 7,
        out_specs=(hbm,) * 2,
        scratch_shapes=[
            pltpu.VMEM((59, 512), f32),
            pltpu.SMEM((1, 12), f32),
            pltpu.VMEM((1, 1, 512), jnp.int32),
            pltpu.VMEM((1, 2, 256), jnp.int32),
            pltpu.SMEM((1, 2), jnp.int32),
            pltpu.SMEM((1, 2), jnp.int32),
            pltpu.VMEM((3, 2, 256), f32),
            messages,
            messages,
            messages,
            pltpu.VMEM((CHIPS, 128), f32),
            pltpu.VMEM((CHIPS, 128), f32),
            messages,
            messages,
            pltpu.VMEM((40, 128), f32),
            pltpu.VMEM((1, 128), f32),
            pltpu.VMEM((2, 256, 128), f32),
            pltpu.VMEM((2, 256, 256), f32),
            pltpu.VMEM((2, 256, 256), f32),
            pltpu.VMEM((512, 512), bf16),
            dma((8,)),
            dma,
            dma,
            dma,
            dma,
            dma,
            dma,
            dma,
            dma,
            dma((VIEWS,)),
            dma((VIEWS,)),
            dma,
        ],
        compiler_params=pltpu.CompilerParams(
            collective_id=0, has_side_effects=True, vmem_limit_bytes=VMEM_BYTES
        ),
        name="exchange",
    )(
        params,
        cameras,
        send_rows,
        lists,
        counts,
        tile_ids,
        target[0].transpose(1, 0, 2),
    )
    near = pltpu.VMEM((59, 512), f32)
    return pl.pallas_call(
        update,
        out_shape=(whole, whole, whole, jax.ShapeDtypeStruct((1, 2), f32)),
        in_specs=[hbm] * 5,
        out_specs=(vmem,) * 4,
        scratch_shapes=[
            near,
            near,
            near,
            pltpu.VMEM((VIEWS * 40, 128), f32),
            pltpu.VMEM((1, 128), f32),
            pltpu.VMEM((1024, 128), f32),
            pltpu.VMEM((256, 128), f32),
            dma((5,)),
        ],
        compiler_params=some,
        name="update",
    )(params, first_moment, second_moment, grads.reshape(VIEWS * 40, 128), loss)


def solution(mesh):
    in_specs = (
        P(None, "gauss"),
        P(None, "gauss"),
        P(None, "gauss"),
        P("view", None),
        P("view", "gauss", None),
        P("view", "gauss", None),
        P("view", "gauss"),
        P("view", "gauss"),
        P("view", "gauss", None, None),
    )
    out_specs = (P(None, "gauss"), P(None, "gauss"), P(None, "gauss"), P("view", "gauss"))
    return jax.shard_map(body, mesh=mesh, in_specs=in_specs, out_specs=out_specs, check_vma=False)
```

```python
import jax
import jax.numpy as jnp
from jax import lax
from jax.experimental import pallas as pl
from jax.experimental.pallas import tpu as pltpu
from jax.sharding import PartitionSpec as P

focal_length = 1100.0
centre_x = 960.0
centre_y = 540.0
beta_one = 0.9
beta_two = 0.999
adam_eps = 1e-15
adam_step = 100.0
log2_e = 1.4426950408889634
sh_zero = 0.28209479177387814
sh_one = 0.4886025119029199
sh_two = [
    1.0925484305920792,
    -1.0925484305920792,
    0.31539156525252005,
    -1.0925484305920792,
    0.5462742152960396,
]
sh_three = [
    -0.5900435899266435,
    2.890611442640554,
    -0.4570457994644658,
    0.3731763325901154,
    -0.4570457994644658,
    1.445305721320277,
    -0.5900435899266435,
]
LINE = 16
SIDE = 4
CHIPS = LINE * SIDE
VIEWS = 4
VMEM_BYTES = 62 * 1024 * 1024
MESH = pl.DeviceIdType.MESH
f32 = jnp.float32
bf16 = jnp.bfloat16


def harmonics(dir_x, dir_y, dir_z):
    sq_x = dir_x * dir_x
    sq_y = dir_y * dir_y
    sq_z = dir_z * dir_z
    return [
        -sh_one * dir_y,
        sh_one * dir_z,
        -sh_one * dir_x,
        sh_two[0] * dir_x * dir_y,
        sh_two[1] * dir_y * dir_z,
        sh_two[2] * (2.0 * sq_z - sq_x - sq_y),
        sh_two[3] * dir_x * dir_z,
        sh_two[4] * (sq_x - sq_y),
        sh_three[0] * dir_y * (3.0 * sq_x - sq_y),
        sh_three[1] * dir_x * dir_y * dir_z,
        sh_three[2] * dir_y * (4.0 * sq_z - sq_x - sq_y),
        sh_three[3] * dir_z * (2.0 * sq_z - 3.0 * sq_x - 3.0 * sq_y),
        sh_three[4] * dir_x * (4.0 * sq_z - sq_x - sq_y),
        sh_three[5] * dir_z * (sq_x - sq_y),
        sh_three[6] * dir_x * (sq_x - 3.0 * sq_y),
    ]


def project(columns, camera):
    mean_x, mean_y, mean_z = columns[0], columns[1], columns[2]
    scales = [jnp.exp(columns[3 + axis]) for axis in range(3)]
    quat_w, quat_x, quat_y, quat_z = columns[6:10]
    norm = 1.0 / jnp.sqrt(quat_w * quat_w + quat_x * quat_x + quat_y * quat_y + quat_z * quat_z)
    quat_w, quat_x, quat_y, quat_z = quat_w * norm, quat_x * norm, quat_y * norm, quat_z * norm
    turn = [
        [
            1.0 - 2.0 * (quat_y * quat_y + quat_z * quat_z),
            2.0 * (quat_x * quat_y - quat_w * quat_z),
            2.0 * (quat_x * quat_z + quat_w * quat_y),
        ],
        [
            2.0 * (quat_x * quat_y + quat_w * quat_z),
            1.0 - 2.0 * (quat_x * quat_x + quat_z * quat_z),
            2.0 * (quat_y * quat_z - quat_w * quat_x),
        ],
        [
            2.0 * (quat_x * quat_z - quat_w * quat_y),
            2.0 * (quat_y * quat_z + quat_w * quat_x),
            1.0 - 2.0 * (quat_x * quat_x + quat_y * quat_y),
        ],
    ]
    world = [[turn[outer][inner] * scales[inner] for inner in range(3)] for outer in range(3)]
    cam_x, cam_y, depth = [
        camera[3 * outer] * mean_x
        + camera[3 * outer + 1] * mean_y
        + camera[3 * outer + 2] * mean_z
        + camera[9 + outer]
        for outer in range(3)
    ]
    framed = [
        [
            camera[3 * outer] * world[0][inner]
            + camera[3 * outer + 1] * world[1][inner]
            + camera[3 * outer + 2] * world[2][inner]
            for inner in range(3)
        ]
        for outer in range(3)
    ]
    inverse = 1.0 / depth
    near = focal_length * inverse
    slope_x = cam_x * inverse
    slope_y = cam_y * inverse
    row_top = [near * (framed[0][inner] - slope_x * framed[2][inner]) for inner in range(3)]
    row_low = [near * (framed[1][inner] - slope_y * framed[2][inner]) for inner in range(3)]
    cov_a = row_top[0] * row_top[0] + row_top[1] * row_top[1] + row_top[2] * row_top[2] + 0.3
    cov_b = row_top[0] * row_low[0] + row_top[1] * row_low[1] + row_top[2] * row_low[2]
    cov_c = row_low[0] * row_low[0] + row_low[1] * row_low[1] + row_low[2] * row_low[2] + 0.3
    over = 1.0 / (cov_a * cov_c - cov_b * cov_b)
    centre_u = focal_length * slope_x + centre_x
    centre_v = focal_length * slope_y + centre_y
    away = 1.0 / jnp.sqrt(cam_x * cam_x + cam_y * cam_y + depth * depth)
    basis = harmonics(cam_x * away, cam_y * away, depth * away)
    colours = []
    for channel in range(3):
        total = 0.5 + sh_zero * columns[11 + channel]
        for order in range(15):
            total = total + basis[order] * columns[14 + 3 * order + channel]
        colours.append(total)
    opacity = 1.0 / (1.0 + jnp.exp(-columns[10]))
    return [
        centre_u,
        centre_v,
        cov_c * over,
        -cov_b * over,
        cov_a * over,
        opacity,
        colours[0],
        colours[1],
        colours[2],
    ]


def pieces(value):
    high = value.astype(bf16)
    rest = value - high.astype(f32)
    middle = rest.astype(bf16)
    low = (rest - middle.astype(f32)).astype(bf16)
    return high, middle, low


def dot_rows(left, right):
    return lax.dot_general(left, right, (((1,), (1,)), ((), ())), preferred_element_type=f32)


def add_pieces(stacked):
    rows = stacked.shape[0] // 3
    return (stacked[0:rows] + stacked[rows : 2 * rows]) + stacked[2 * rows :]


def dot_exact(left, right):
    stacked = jnp.concatenate(pieces(left), axis=0)
    return add_pieces(jnp.dot(stacked, right, preferred_element_type=f32))


def dot_rows_exact(left, right):
    return add_pieces(dot_rows(jnp.concatenate(pieces(left), axis=0), right))


def iota(shape, axis):
    return lax.broadcasted_iota(jnp.int32, shape, axis)


def one_hot(test):
    return jnp.where(test, 1.0, 0.0).astype(bf16)


def swap(value):
    return pltpu.roll(value, 64, 1)


def reorder_row(row, width, place):
    split = jnp.concatenate([row >> 4, row & 15, jnp.zeros((6, width), jnp.int32)], axis=0)
    chosen = one_hot(iota((width, width), 0) == place(iota((width, width), 1)))
    moved = jnp.dot(split.astype(f32).astype(bf16), chosen, preferred_element_type=f32)
    return (moved[0:1] * 16.0 + moved[1:2]).astype(jnp.int32)


def sender_table(rows):
    moved = reorder_row(rows, 512, lambda n: 8 * (n & 63) + (n >> 6))
    return one_hot(iota((512, 512), 0) == moved)


def pack_messages(attributes, table):
    placed = dot_exact(attributes, table)
    parts = []
    for pair in range(4):
        both = placed[:, 128 * pair : 128 * pair + 128]
        parts += [both, swap(both)]
    return jnp.transpose(jnp.concatenate(parts, axis=0))[0:64]


def unpack_messages(messages, table):
    turned = jnp.transpose(jnp.concatenate([messages, jnp.zeros_like(messages)], axis=0))
    keep = iota((16, 128), 1) < 64
    parts = []
    for pair in range(4):
        left = turned[32 * pair : 32 * pair + 16]
        right = turned[32 * pair + 16 : 32 * pair + 32]
        parts.append(jnp.where(keep, left, swap(right)))
    return dot_rows_exact(jnp.concatenate(parts, axis=1), table)


def list_tables(lists):
    moved = []
    for tile in range(2):
        moved.append(reorder_row(lists[tile : tile + 1], 256, lambda n: 32 * (n & 7) + (n >> 3)))
    slot = jnp.concatenate(moved, axis=1)
    return one_hot(iota((64, 512), 0) == (slot >> 3)), slot & 7


def pick(received, table, group):
    turned = jnp.transpose(jnp.concatenate([received, jnp.zeros_like(received)], axis=0))[:, 0:64]
    found = dot_exact(turned, table)
    found = jnp.where((iota((128, 512), 0) >> 4) == group, found, 0.0)
    total = found[0:16]
    for part in range(1, 8):
        total = total + found[16 * part : 16 * part + 16]
    return total


def unpick(grads, table, group):
    spread = jnp.concatenate([grads] * 8, axis=0)
    spread = jnp.where((iota((128, 512), 0) >> 4) == group, spread, 0.0)
    turned = dot_rows_exact(spread, table)
    return jnp.transpose(jnp.concatenate([turned, jnp.zeros((128, 64), f32)], axis=1))[0:64]


def place_of(position):
    return 32 * (position & 7) + (position >> 3)


def split(rows):
    return [part.astype(f32) for part in pieces(rows)]


def prepare_tile(attributes, count, tile_id):
    across = (16 * lax.rem(tile_id, 120)).astype(f32) + 7.5
    down = (16 * lax.div(tile_id, 120)).astype(f32) + 7.5
    centre_u = attributes[0:1] - across
    centre_v = attributes[1:2] - down
    alive = place_of(iota((1, 256), 1)) < count
    by_xx = attributes[2:3] * (-0.5 * log2_e)
    by_xy = attributes[3:4] * (-log2_e)
    by_yy = attributes[4:5] * (-0.5 * log2_e)
    by_x = -2.0 * by_xx * centre_u - by_xy * centre_v
    by_y = -2.0 * by_yy * centre_v - by_xy * centre_u
    whole = (by_xx * centre_u + by_xy * centre_v) * centre_u + (by_yy * centre_v) * centre_v
    whole = jnp.where(alive, whole + jnp.log(attributes[5:6]) * log2_e, -1e30)
    power = split(jnp.concatenate([whole, by_x, by_y, by_xx, by_xy, by_yy], axis=0))
    colour = attributes[6:9]
    high, middle, low = split(colour)
    rows = power + [high, high, high, middle, middle, low, colour, jnp.zeros((89, 256), f32)]
    return jnp.transpose(jnp.concatenate(rows, axis=0)), centre_u, centre_v


def pixels():
    number = iota((1, 256), 1)
    return (number & 15).astype(f32) - 7.5, (number >> 4).astype(f32) - 7.5


def monomials():
    pixel_x, pixel_y = pixels()
    ones = jnp.ones((1, 256), f32)
    return [ones, pixel_x, pixel_y, pixel_x * pixel_x, pixel_x * pixel_y, pixel_y * pixel_y]


def exponents(columns):
    right = jnp.concatenate(monomials() * 3 + [jnp.zeros((110, 256), f32)], axis=0)
    return jnp.dot(columns, right.astype(bf16), preferred_element_type=f32)


def shades(columns, residual):
    high, middle, low = split(jnp.concatenate(residual, axis=0))
    rows = [jnp.zeros((18, 256), f32), high, middle, low, high, middle, high]
    right = jnp.concatenate(rows + [jnp.zeros((92, 256), f32)], axis=0)
    return jnp.dot(columns, right.astype(bf16), preferred_element_type=f32)


def shade_step(columns, power, carry):
    keep, colour = carry
    alpha = jnp.exp2(power)
    weight = keep * alpha
    colour = [colour[c] + weight * columns[:, 36 + c : 37 + c] for c in range(3)]
    return alpha, weight, (keep - weight, colour)


def between(keep, colour, target):
    before = [jnp.ones((1, 256), f32)]
    for chunk in range(7):
        before.append(before[-1] * keep[chunk : chunk + 1])
    before = jnp.concatenate(before, axis=0)
    colour = [part * before for part in colour]
    residual = [jnp.sum(colour[c], axis=0, keepdims=True) - target[c : c + 1] for c in range(3)]
    own = residual[0] * colour[0] + residual[1] * colour[1] + residual[2] * colour[2]
    after = [jnp.zeros((1, 256), f32)]
    for chunk in range(7, 0, -1):
        after.append(after[-1] + own[chunk : chunk + 1])
    after = jnp.concatenate(after[::-1], axis=0)
    squares = residual[0] * residual[0] + residual[1] * residual[1] + residual[2] * residual[2]
    return before, after, residual, 0.5 * jnp.sum(squares, axis=1, keepdims=True)


def back_step(shade, alpha, weight, before, after, later):
    own = weight * shade
    left = 1.0 - alpha
    guess = pl.reciprocal(left, approx=True)
    ratio = alpha * (guess * (2.0 - left * guess))
    slope = before * own - (before * later + after) * ratio
    return slope, before * weight, later + own


def moments(slope, weight, residual):
    shown = split(jnp.concatenate(residual, axis=0))
    factors = jnp.concatenate(monomials() + shown + [jnp.zeros((1, 256), f32)], axis=0).astype(bf16)

    def over_pixels(value):
        high, middle, unused = pieces(value)
        return dot_rows(factors, middle) + dot_rows(factors, high)

    by_power = over_pixels(slope)[0:6]
    by_shown = over_pixels(weight)
    by_shown = by_shown[6:9] + (by_shown[9:12] + by_shown[12:15])
    return jnp.concatenate([by_power, by_shown], axis=0)


def finish_tile(sums, attributes, centre_u, centre_v):
    whole, by_x, by_y, by_xx, by_xy, by_yy = [sums[n : n + 1] for n in range(6)]
    sum_x = by_x - centre_u * whole
    sum_y = by_y - centre_v * whole
    sum_xx = by_xx - centre_u * (by_x + sum_x)
    sum_xy = by_xy - centre_u * by_y - centre_v * sum_x
    sum_yy = by_yy - centre_v * (by_y + sum_y)
    conic = [attributes[2 + n : 3 + n] for n in range(3)]
    rows = [
        conic[0] * sum_x + conic[1] * sum_y,
        conic[1] * sum_x + conic[2] * sum_y,
        -0.5 * sum_xx,
        -sum_xy,
        -0.5 * sum_yy,
        whole,
        sums[6:9],
        jnp.zeros((7, 256), f32),
    ]
    return jnp.concatenate(rows, axis=0)


def exchange(
    params_in,
    camera_in,
    rows_in,
    lists_in,
    counts_in,
    tile_ids_in,
    target_in,
    out,
    loss,
    params,
    camera,
    rows,
    lists,
    counts,
    tile_ids,
    target,
    msg,
    land1,
    land2,
    back1,
    land3,
    back2,
    land4,
    own,
    losses,
    columns,
    alphas,
    weights,
    shaded,
    table,
    loads,
    send1,
    recv1,
    send2,
    recv2,
    send3,
    recv3,
    send4,
    recv4,
    send5,
    recv5,
    kept5,
):
    here = lax.axis_index("gauss")
    view = lax.axis_index("view")
    core = lax.rem(here, 2)
    chip = here // 2
    line = chip // SIDE
    side = lax.rem(chip, SIDE)

    def on_chip(step_z, step_x):
        other = lax.rem(line + step_z, LINE) * SIDE + lax.rem(side + step_x, SIDE)
        return other, {"gauss": other * 2 + core, "view": view}

    def far_first(action):
        def one(step, unused):
            step_z = LINE // 2 + (1 - 2 * (step & 1)) * ((step + 1) >> 1)
            for step_x in (2, 1, 3, 0):
                action(*on_chip(step_z, step_x))
            return unused

        lax.fori_loop(0, LINE - 1, one, 0)
        for step_x in (2, 1, 3):
            action(*on_chip(0, step_x))

    other_core = {"gauss": here + 1 - 2 * core, "view": view}

    def over_views(action):
        for step in (2, 1, 3):
            other = lax.rem(view + step, VIEWS)
            action(step, other, {"gauss": here, "view": other})

    barrier = pltpu.get_barrier_semaphore()

    def greet(device):
        pl.semaphore_signal(barrier, inc=1, device_id=device, device_id_type=MESH)

    far_first(lambda other, device: greet(device))
    over_views(lambda step, other, device: greet(device))
    greet(other_core)

    pairs = [
        (rows_in, rows),
        (params_in, params),
        (camera_in, camera),
        (lists_in, lists),
        (counts_in, counts),
        (tile_ids_in, tile_ids),
        (target_in, target),
    ]
    copies = [
        pltpu.make_async_copy(source, place, loads.at[n]) for n, (source, place) in enumerate(pairs)
    ]
    for copy in copies:
        copy.start()

    def remote(source, place, sent, arrived, device):
        return pltpu.make_async_remote_copy(
            src_ref=source,
            dst_ref=place,
            send_sem=sent,
            recv_sem=arrived,
            device_id=device,
            device_id_type=MESH,
        )

    def to_chips(source, place, sent, arrived):
        def send(other, device):
            remote(source.at[other], place.at[chip], sent, arrived, device).start()

        far_first(send)
        place[chip] = source[chip]

    def from_chips(place, arrived):
        whole = place.at[pl.ds(0, CHIPS - 1)]
        pltpu.make_async_copy(whole, whole, arrived).wait()

    low_lanes = iota((64, 128), 1) < 64
    mine = low_lanes == (core == 0)

    def with_other_core(source, place, sent, arrived):
        copy = remote(source, place, sent, arrived, other_core)
        copy.start()
        copy.wait()
        kept = source[...].reshape(64, 128)
        return jnp.where(mine, kept, swap(place[...].reshape(64, 128)))

    copies[0].wait()
    table[...] = sender_table(rows[0])
    copies[1].wait()
    copies[2].wait()
    scalars = [camera[0, n] for n in range(12)]
    attributes = project([params[n : n + 1, :] for n in range(59)], scalars)
    messages = pack_messages(
        jnp.concatenate(attributes + [jnp.zeros((7, 512), f32)], axis=0), table[...]
    )
    msg[...] = messages.reshape(CHIPS, 1, 128)
    for copy in copies[3:]:
        copy.wait()

    pl.semaphore_wait(barrier, CHIPS + VIEWS - 1)
    to_chips(msg, land1, send1, recv1)
    picked, lane_group = list_tables(lists[0])
    from_chips(land1, recv1)
    received = with_other_core(land1, land2, send2, recv2)

    found = pick(received, picked, lane_group)
    centres = []
    for tile in range(2):
        entries = found[:, 256 * tile : 256 * tile + 256]
        filled, centre_u, centre_v = prepare_tile(entries, counts[0, tile], tile_ids[0, tile])
        columns[tile] = filled
        alphas[tile] = exponents(filled.astype(bf16))
        centres.append((entries, centre_u, centre_v))

    def forward(step, carry):
        rows_here = pl.ds(pl.multiple_of(step * 8, 8), 8)
        left = []
        for tile in range(2):
            alpha, weight, rest = shade_step(
                columns[tile, rows_here, :], alphas[tile, rows_here, :], carry[tile]
            )
            alphas[tile, rows_here, :] = alpha
            weights[tile, rows_here, :] = weight
            left.append(rest)
        return left

    fresh = (jnp.ones((8, 256), f32), [jnp.zeros((8, 256), f32)] * 3)
    carry = lax.fori_loop(0, 32, forward, [fresh, fresh], unroll=16)
    around = []
    for tile in range(2):
        around.append(between(carry[tile][0], carry[tile][1], target[:, tile, :]))
        shaded[tile] = shades(columns[tile].astype(bf16), around[tile][2])
    spot = iota((1, 128), 1)
    losses[...] = jnp.where(spot == 0, around[0][3], jnp.where(spot == 1, around[1][3], 0.0))
    loss_copy = pltpu.make_async_copy(losses, loss, loads.at[7])
    loss_copy.start()

    def backward(step, later):
        rows_here = pl.ds(pl.multiple_of((31 - step) * 8, 8), 8)
        left = []
        for tile in range(2):
            before, after = around[tile][0:2]
            slope, weight, rest = back_step(
                shaded[tile, rows_here, :],
                alphas[tile, rows_here, :],
                weights[tile, rows_here, :],
                before,
                after,
                later[tile],
            )
            alphas[tile, rows_here, :] = slope
            weights[tile, rows_here, :] = weight
            left.append(rest)
        return left

    lax.fori_loop(0, 32, backward, [jnp.zeros((8, 256), f32)] * 2, unroll=16)
    grads = []
    for tile in range(2):
        sums = moments(alphas[tile], weights[tile], around[tile][2])
        grads.append(finish_tile(sums, *centres[tile]))
    grads = jnp.concatenate(grads, axis=1)
    back1[...] = unpick(grads, picked, lane_group)

    back2[...] = with_other_core(back1, land3, send3, recv3).reshape(CHIPS, 1, 128)
    to_chips(back2, land4, send4, recv4)
    from_chips(land4, recv4)
    returned = unpack_messages(land4[...].reshape(64, 128), table[...])

    lanes = iota((1, 128), 1)
    pose = jnp.zeros((1, 128), f32)
    for n in range(12):
        pose = jnp.where(lanes == n, scalars[n], pose)
    for part in range(4):
        own[10 * part : 10 * part + 9, :] = returned[0:9, 128 * part : 128 * part + 128]
        own[10 * part + 9 : 10 * part + 10, :] = pose

    def share(step, other, device):
        remote(own, out.at[view], send5.at[step], recv5.at[view], device).start()

    def take(step, other, device):
        remote(own, out.at[other], send5.at[step], recv5.at[other], device).wait()

    over_views(share)
    keep = pltpu.make_async_copy(own, out.at[view], kept5)
    keep.start()
    loss_copy.wait()

    for sent, buffer in ((send1, msg), (send4, back2)):
        whole = buffer.at[pl.ds(0, CHIPS - 1)]
        pltpu.make_async_copy(whole, whole, sent).wait()
    keep.wait()
    over_views(take)


def update(
    params_in,
    first_in,
    second_in,
    grads_in,
    loss_in,
    new_params,
    new_first,
    new_second,
    tile_loss,
    params,
    first,
    second,
    grads,
    loss,
    spread,
    total,
    loads,
):
    pairs = [
        (params_in, params),
        (grads_in, grads),
        (first_in, first),
        (second_in, second),
        (loss_in, loss),
    ]
    copies = [
        pltpu.make_async_copy(source, place, loads.at[n]) for n, (source, place) in enumerate(pairs)
    ]
    for copy in copies:
        copy.start()
    copies[0].wait()

    for part in range(4):
        block = params[:, 128 * part : 128 * part + 128]
        for view in range(VIEWS):
            start = 64 * (4 * view + part)
            spread[start : start + 59, :] = block
    columns = [spread[pl.ds(n, 16, stride=64), :] for n in range(59)]
    copies[1].wait()
    given = [grads[pl.ds(n, 16, stride=10), :] for n in range(10)]
    camera = [given[9][:, n : n + 1] for n in range(12)]

    def shown(rows):
        attributes = project(rows, camera)
        return attributes[0:5] + attributes[6:9]

    pulled = jax.vjp(shown, columns)[1](given[0:5] + given[6:9])[0]
    pulled[10] = given[5] * (1.0 - 1.0 / (1.0 + jnp.exp(-columns[10])))
    for n in range(59):
        both = pulled[n][0:8] + pulled[n][8:16]
        total[pl.ds(n, 4, stride=64), :] = both[0:4] + both[4:8]
    for copy in copies[2:]:
        copy.wait()
    row = iota((59, 1), 0)
    rate = jnp.where(row < 3, 0.00016, 0.005)
    rate = jnp.where(row < 6, rate, 0.001)
    rate = jnp.where(row < 10, rate, 0.05)
    rate = jnp.where(row < 11, rate, 0.0025)
    rate = jnp.where(row < 14, rate, 0.000125)
    rate = rate / (1.0 - beta_one**adam_step)
    for part in range(4):
        here = slice(128 * part, 128 * part + 128)
        slope = total[64 * part : 64 * part + 59, :]
        moved = beta_one * first[:, here] + (1.0 - beta_one) * slope
        square = beta_two * second[:, here] + (1.0 - beta_two) * slope * slope
        new_first[:, here] = moved
        new_second[:, here] = square
        new_params[:, here] = params[:, here] - rate * moved / (
            jnp.sqrt(square / (1.0 - beta_two**adam_step)) + adam_eps
        )
    tile_loss[...] = loss[:, 0:2]


def body(params, first_moment, second_moment, cameras, send_rows, lists, counts, tile_ids, target):
    vmem = pl.BlockSpec(memory_space=pltpu.VMEM)
    hbm = pl.BlockSpec(memory_space=pltpu.HBM)
    dma = pltpu.SemaphoreType.DMA
    whole = jax.ShapeDtypeStruct((59, 512), f32)
    messages = pltpu.VMEM((CHIPS, 1, 128), f32)
    some = pltpu.CompilerParams(vmem_limit_bytes=VMEM_BYTES)
    grads, loss = pl.pallas_call(
        exchange,
        out_shape=(
            jax.ShapeDtypeStruct((VIEWS, 40, 128), f32),
            jax.ShapeDtypeStruct((1, 128), f32),
        ),
        in_specs=[hbm] * 7,
        out_specs=(hbm,) * 2,
        scratch_shapes=[
            pltpu.VMEM((59, 512), f32),
            pltpu.SMEM((1, 12), f32),
            pltpu.VMEM((1, 1, 512), jnp.int32),
            pltpu.VMEM((1, 2, 256), jnp.int32),
            pltpu.SMEM((1, 2), jnp.int32),
            pltpu.SMEM((1, 2), jnp.int32),
            pltpu.VMEM((3, 2, 256), f32),
            messages,
            messages,
            messages,
            pltpu.VMEM((CHIPS, 128), f32),
            pltpu.VMEM((CHIPS, 128), f32),
            messages,
            messages,
            pltpu.VMEM((40, 128), f32),
            pltpu.VMEM((1, 128), f32),
            pltpu.VMEM((2, 256, 128), f32),
            pltpu.VMEM((2, 256, 256), f32),
            pltpu.VMEM((2, 256, 256), f32),
            pltpu.VMEM((2, 256, 256), f32),
            pltpu.VMEM((512, 512), bf16),
            dma((8,)),
            dma,
            dma,
            dma,
            dma,
            dma,
            dma,
            dma,
            dma,
            dma((VIEWS,)),
            dma((VIEWS,)),
            dma,
        ],
        compiler_params=pltpu.CompilerParams(
            collective_id=0, has_side_effects=True, vmem_limit_bytes=VMEM_BYTES
        ),
        name="exchange",
    )(
        params,
        cameras,
        send_rows,
        lists,
        counts,
        tile_ids,
        target[0].transpose(1, 0, 2),
    )
    near = pltpu.VMEM((59, 512), f32)
    return pl.pallas_call(
        update,
        out_shape=(whole, whole, whole, jax.ShapeDtypeStruct((1, 2), f32)),
        in_specs=[hbm] * 5,
        out_specs=(vmem,) * 4,
        scratch_shapes=[
            near,
            near,
            near,
            pltpu.VMEM((VIEWS * 40, 128), f32),
            pltpu.VMEM((1, 128), f32),
            pltpu.VMEM((1024, 128), f32),
            pltpu.VMEM((256, 128), f32),
            dma((5,)),
        ],
        compiler_params=some,
        name="update",
    )(params, first_moment, second_moment, grads.reshape(VIEWS * 40, 128), loss)


def solution(mesh):
    in_specs = (
        P(None, "gauss"),
        P(None, "gauss"),
        P(None, "gauss"),
        P("view", None),
        P("view", "gauss", None),
        P("view", "gauss", None),
        P("view", "gauss"),
        P("view", "gauss"),
        P("view", "gauss", None, None),
    )
    out_specs = (P(None, "gauss"), P(None, "gauss"), P(None, "gauss"), P("view", "gauss"))
    return jax.shard_map(body, mesh=mesh, in_specs=in_specs, out_specs=out_specs, check_vma=False)
```

```python
import jax
import jax.numpy as jnp
from jax import lax
from jax.experimental import pallas as pl
from jax.experimental.pallas import tpu as pltpu
from jax.sharding import PartitionSpec as P

focal_length = 1100.0
centre_x = 960.0
centre_y = 540.0
beta_one = 0.9
beta_two = 0.999
adam_eps = 1e-15
adam_step = 100.0
log2_e = 1.4426950408889634
sh_zero = 0.28209479177387814
sh_one = 0.4886025119029199
sh_two = [
    1.0925484305920792,
    -1.0925484305920792,
    0.31539156525252005,
    -1.0925484305920792,
    0.5462742152960396,
]
sh_three = [
    -0.5900435899266435,
    2.890611442640554,
    -0.4570457994644658,
    0.3731763325901154,
    -0.4570457994644658,
    1.445305721320277,
    -0.5900435899266435,
]
LINE = 16
SIDE = 4
CHIPS = LINE * SIDE
SHARE = 4
RENDER = CHIPS // SHARE
VIEWS = 4
VMEM_BYTES = 62 * 1024 * 1024
MESH = pl.DeviceIdType.MESH
f32 = jnp.float32
bf16 = jnp.bfloat16


def harmonics(dir_x, dir_y, dir_z):
    sq_x = dir_x * dir_x
    sq_y = dir_y * dir_y
    sq_z = dir_z * dir_z
    return [
        -sh_one * dir_y,
        sh_one * dir_z,
        -sh_one * dir_x,
        sh_two[0] * dir_x * dir_y,
        sh_two[1] * dir_y * dir_z,
        sh_two[2] * (2.0 * sq_z - sq_x - sq_y),
        sh_two[3] * dir_x * dir_z,
        sh_two[4] * (sq_x - sq_y),
        sh_three[0] * dir_y * (3.0 * sq_x - sq_y),
        sh_three[1] * dir_x * dir_y * dir_z,
        sh_three[2] * dir_y * (4.0 * sq_z - sq_x - sq_y),
        sh_three[3] * dir_z * (2.0 * sq_z - 3.0 * sq_x - 3.0 * sq_y),
        sh_three[4] * dir_x * (4.0 * sq_z - sq_x - sq_y),
        sh_three[5] * dir_z * (sq_x - sq_y),
        sh_three[6] * dir_x * (sq_x - 3.0 * sq_y),
    ]


def project(columns, camera):
    mean_x, mean_y, mean_z = columns[0], columns[1], columns[2]
    scales = [jnp.exp(columns[3 + axis]) for axis in range(3)]
    quat_w, quat_x, quat_y, quat_z = columns[6:10]
    norm = 1.0 / jnp.sqrt(quat_w * quat_w + quat_x * quat_x + quat_y * quat_y + quat_z * quat_z)
    quat_w, quat_x, quat_y, quat_z = quat_w * norm, quat_x * norm, quat_y * norm, quat_z * norm
    turn = [
        [
            1.0 - 2.0 * (quat_y * quat_y + quat_z * quat_z),
            2.0 * (quat_x * quat_y - quat_w * quat_z),
            2.0 * (quat_x * quat_z + quat_w * quat_y),
        ],
        [
            2.0 * (quat_x * quat_y + quat_w * quat_z),
            1.0 - 2.0 * (quat_x * quat_x + quat_z * quat_z),
            2.0 * (quat_y * quat_z - quat_w * quat_x),
        ],
        [
            2.0 * (quat_x * quat_z - quat_w * quat_y),
            2.0 * (quat_y * quat_z + quat_w * quat_x),
            1.0 - 2.0 * (quat_x * quat_x + quat_y * quat_y),
        ],
    ]
    world = [[turn[outer][inner] * scales[inner] for inner in range(3)] for outer in range(3)]
    cam_x, cam_y, depth = [
        camera[3 * outer] * mean_x
        + camera[3 * outer + 1] * mean_y
        + camera[3 * outer + 2] * mean_z
        + camera[9 + outer]
        for outer in range(3)
    ]
    framed = [
        [
            camera[3 * outer] * world[0][inner]
            + camera[3 * outer + 1] * world[1][inner]
            + camera[3 * outer + 2] * world[2][inner]
            for inner in range(3)
        ]
        for outer in range(3)
    ]
    inverse = 1.0 / depth
    near = focal_length * inverse
    slope_x = cam_x * inverse
    slope_y = cam_y * inverse
    row_top = [near * (framed[0][inner] - slope_x * framed[2][inner]) for inner in range(3)]
    row_low = [near * (framed[1][inner] - slope_y * framed[2][inner]) for inner in range(3)]
    cov_a = row_top[0] * row_top[0] + row_top[1] * row_top[1] + row_top[2] * row_top[2] + 0.3
    cov_b = row_top[0] * row_low[0] + row_top[1] * row_low[1] + row_top[2] * row_low[2]
    cov_c = row_low[0] * row_low[0] + row_low[1] * row_low[1] + row_low[2] * row_low[2] + 0.3
    over = 1.0 / (cov_a * cov_c - cov_b * cov_b)
    centre_u = focal_length * slope_x + centre_x
    centre_v = focal_length * slope_y + centre_y
    away = 1.0 / jnp.sqrt(cam_x * cam_x + cam_y * cam_y + depth * depth)
    basis = harmonics(cam_x * away, cam_y * away, depth * away)
    colours = []
    for channel in range(3):
        total = 0.5 + sh_zero * columns[11 + channel]
        for order in range(15):
            total = total + basis[order] * columns[14 + 3 * order + channel]
        colours.append(total)
    opacity = 1.0 / (1.0 + jnp.exp(-columns[10]))
    return [
        centre_u,
        centre_v,
        cov_c * over,
        -cov_b * over,
        cov_a * over,
        opacity,
        colours[0],
        colours[1],
        colours[2],
    ]


def pieces(value):
    high = value.astype(bf16)
    rest = value - high.astype(f32)
    middle = rest.astype(bf16)
    low = (rest - middle.astype(f32)).astype(bf16)
    return high, middle, low


def dot_rows(left, right):
    return lax.dot_general(left, right, (((1,), (1,)), ((), ())), preferred_element_type=f32)


def add_pieces(stacked):
    rows = stacked.shape[0] // 3
    return (stacked[0:rows] + stacked[rows : 2 * rows]) + stacked[2 * rows :]


def dot_exact(left, right):
    stacked = jnp.concatenate(pieces(left), axis=0)
    return add_pieces(jnp.dot(stacked, right, preferred_element_type=f32))


def dot_rows_exact(left, right):
    return add_pieces(dot_rows(jnp.concatenate(pieces(left), axis=0), right))


def iota(shape, axis):
    return lax.broadcasted_iota(jnp.int32, shape, axis)


def one_hot(test):
    return jnp.where(test, 1.0, 0.0).astype(bf16)


def swap(value):
    return pltpu.roll(value, 64, 1)


def reorder_rows(rows, place):
    number, width = rows.shape
    padding = jnp.zeros((8 - 2 * number, width), jnp.int32)
    split_rows = jnp.concatenate([rows >> 4, rows & 15, padding], axis=0)
    chosen = one_hot(iota((width, width), 0) == place(iota((width, width), 1)))
    moved = jnp.dot(split_rows.astype(f32).astype(bf16), chosen, preferred_element_type=f32)
    return moved[0:number] * 16.0 + moved[number : 2 * number]


def sender_table(rows):
    moved = reorder_rows(rows, lambda n: 8 * (n & 63) + (n >> 6))
    return one_hot(iota((512, 512), 0) == moved.astype(jnp.int32))


def pack_messages(attributes, table):
    placed = dot_exact(attributes, table)
    parts = []
    for pair in range(4):
        both = placed[:, 128 * pair : 128 * pair + 128]
        parts += [both, swap(both)]
    return jnp.transpose(jnp.concatenate(parts, axis=0))[0:64]


def unpack_messages(messages, table):
    turned = jnp.transpose(jnp.concatenate([messages, jnp.zeros_like(messages)], axis=0))
    keep = iota((16, 128), 1) < 64
    parts = []
    for pair in range(4):
        left = turned[32 * pair : 32 * pair + 16]
        right = turned[32 * pair + 16 : 32 * pair + 32]
        parts.append(jnp.where(keep, left, swap(right)))
    return dot_rows_exact(jnp.concatenate(parts, axis=1), table)


def list_tables(lists):
    slot = jnp.concatenate([lists[0:1], lists[1:2]], axis=1).astype(jnp.int32)
    return one_hot(iota((64, 512), 0) == (slot >> 3)), slot & 7


def pick(received, table, group):
    turned = jnp.transpose(jnp.concatenate([received, jnp.zeros_like(received)], axis=0))[:, 0:64]
    found = dot_exact(turned, table)
    found = jnp.where((iota((128, 512), 0) >> 4) == group, found, 0.0)
    total = found[0:16]
    for part in range(1, 8):
        total = total + found[16 * part : 16 * part + 16]
    return total


def unpick(grads, table, group):
    spread = jnp.concatenate([grads] * 8, axis=0)
    spread = jnp.where((iota((128, 512), 0) >> 4) == group, spread, 0.0)
    turned = dot_rows_exact(spread, table)
    return jnp.transpose(jnp.concatenate([turned, jnp.zeros((128, 64), f32)], axis=1))[0:64]


def place_of(position):
    return 32 * (position & 7) + (position >> 3)


def split(rows):
    return [part.astype(f32) for part in pieces(rows)]


def split(rows):
    return [part.astype(f32) for part in pieces(rows)]


def two_pieces(value):
    high = value.astype(bf16)
    return high, (value - high.astype(f32)).astype(bf16)


def padded(rows):
    number = sum(part.shape[0] for part in rows)
    return jnp.concatenate(rows + [jnp.zeros((32 - number, 256), f32)], axis=0).astype(bf16)


def dot_columns(left, right):
    return lax.dot_general(left, right, (((0,), (0,)), ((), ())), preferred_element_type=f32)


def prepare_tile(attributes, across, down, count):
    centre_u = attributes[0:1] - across
    centre_v = attributes[1:2] - down
    alive = place_of(iota((1, 256), 1)).astype(f32) < count
    by_xx = attributes[2:3] * (-0.5 * log2_e)
    by_xy = attributes[3:4] * (-log2_e)
    by_yy = attributes[4:5] * (-0.5 * log2_e)
    by_x = -2.0 * by_xx * centre_u - by_xy * centre_v
    by_y = -2.0 * by_yy * centre_v - by_xy * centre_u
    whole = (by_xx * centre_u + by_xy * centre_v) * centre_u + (by_yy * centre_v) * centre_v
    whole = jnp.where(alive, whole + jnp.log(attributes[5:6]) * log2_e, -1e30)
    power = jnp.concatenate([whole, by_x, by_y, by_xx, by_xy, by_yy], axis=0)
    return power, centre_u, centre_v


def pixels():
    number = iota((1, 256), 1)
    return (number & 15).astype(f32) - 7.5, (number >> 4).astype(f32) - 7.5


def monomials():
    pixel_x, pixel_y = pixels()
    ones = jnp.ones((1, 256), f32)
    return [ones, pixel_x, pixel_y, pixel_x * pixel_x, pixel_x * pixel_y, pixel_y * pixel_y]


def exponents(power):
    return dot_columns(padded(split(power)), padded(monomials() * 3))


def colour_sums(colour, weight):
    chunk = (iota((8, 256), 1) & 7) == iota((8, 256), 0)
    spread = [jnp.where(chunk, colour[c : c + 1], 0.0) for c in range(3)]
    left = jnp.concatenate(split(jnp.concatenate(spread, axis=0)), axis=0).astype(bf16)
    high, middle = two_pieces(weight)
    total = jnp.dot(left, middle, preferred_element_type=f32)
    total = total + jnp.dot(left, high, preferred_element_type=f32)
    total = add_pieces(total)
    return [total[8 * c : 8 * c + 8] for c in range(3)]


def shades(colour, residual):
    high, middle, low = split(colour)
    left = padded([high, high, high, middle, middle, low])
    high, middle, low = split(jnp.concatenate(residual, axis=0))
    return dot_columns(left, padded([high, middle, low, high, middle, high]))


def between(keep, colour, target):
    before = [jnp.ones((1, 256), f32)]
    for chunk in range(7):
        before.append(before[-1] * keep[chunk : chunk + 1])
    before = jnp.concatenate(before, axis=0)
    colour = [part * before for part in colour]
    residual = [jnp.sum(colour[c], axis=0, keepdims=True) - target[c : c + 1] for c in range(3)]
    own = residual[0] * colour[0] + residual[1] * colour[1] + residual[2] * colour[2]
    after = [jnp.zeros((1, 256), f32)]
    for chunk in range(7, 0, -1):
        after.append(after[-1] + own[chunk : chunk + 1])
    after = jnp.concatenate(after[::-1], axis=0)
    squares = residual[0] * residual[0] + residual[1] * residual[1] + residual[2] * residual[2]
    return before, after, residual, 0.5 * jnp.sum(squares, axis=1, keepdims=True)


def back_step(shade, alpha, weight, before, after, later):
    own = weight * shade
    left = 1.0 - alpha
    guess = pl.reciprocal(left, approx=True)
    ratio = alpha * (guess * (2.0 - left * guess))
    slope = before * own - (before * later + after) * ratio
    return slope, before * weight, later + own


def moments(slope, weight, residual):
    shown = split(jnp.concatenate(residual, axis=0))
    factors = jnp.concatenate(monomials() + shown + [jnp.zeros((1, 256), f32)], axis=0).astype(bf16)

    def over_pixels(value):
        high, middle = two_pieces(value)
        return dot_rows(factors, middle) + dot_rows(factors, high)

    by_power = over_pixels(slope)[0:6]
    by_shown = over_pixels(weight)
    by_shown = by_shown[6:9] + (by_shown[9:12] + by_shown[12:15])
    return jnp.concatenate([by_power, by_shown], axis=0)


def finish_tile(sums, attributes, centre_u, centre_v):
    whole, by_x, by_y, by_xx, by_xy, by_yy = [sums[n : n + 1] for n in range(6)]
    sum_x = by_x - centre_u * whole
    sum_y = by_y - centre_v * whole
    sum_xx = by_xx - centre_u * (by_x + sum_x)
    sum_xy = by_xy - centre_u * by_y - centre_v * sum_x
    sum_yy = by_yy - centre_v * (by_y + sum_y)
    conic = [attributes[2 + n : 3 + n] for n in range(3)]
    rows = [
        conic[0] * sum_x + conic[1] * sum_y,
        conic[1] * sum_x + conic[2] * sum_y,
        -0.5 * sum_xx,
        -sum_xy,
        -0.5 * sum_yy,
        whole,
        sums[6:9],
        jnp.zeros((7, 256), f32),
    ]
    return jnp.concatenate(rows, axis=0)


def exchange(
    params_in,
    camera_in,
    rows_in,
    lists_in,
    counts_in,
    tile_ids_in,
    target_in,
    out,
    loss,
    params,
    camera,
    rows,
    lists,
    counts,
    tile_ids,
    target,
    msg,
    land1,
    land2,
    back1,
    land3,
    back2,
    land4,
    facts,
    land_facts,
    own,
    losses,
    away,
    alphas,
    weights,
    shaded,
    table,
    loads,
    send1,
    recv1,
    send2,
    recv2,
    send3,
    recv3,
    send4,
    recv4,
    send5,
    recv5,
    kept5,
    send6,
    recv6,
    send7,
    recv7,
):
    here = lax.axis_index("gauss")
    view = lax.axis_index("view")
    core = lax.rem(here, 2)
    chip = here // 2
    line = chip // SIDE
    side = lax.rem(chip, SIDE)

    other_core = {"gauss": here + 1 - 2 * core, "view": view}

    def over_views(action):
        for step in (2, 1, 3):
            other = lax.rem(view + step, VIEWS)
            action(step, other, {"gauss": here, "view": other})

    barrier = pltpu.get_barrier_semaphore()

    def greet(device):
        pl.semaphore_signal(barrier, inc=1, device_id=device, device_id_type=MESH)

    early = chip < RENDER
    late = jnp.logical_not(early)
    home = {"gauss": lax.rem(chip, RENDER) * 2 + core, "view": view}
    turn = chip // RENDER

    def served(number):
        return {"gauss": lax.rem(chip + number * RENDER, CHIPS) * 2 + core, "view": view}

    def to_renderers(action):
        for step_z in (0, 1, 3, 2):
            for step_x in (2, 1, 3, 0):
                other = lax.rem(line + step_z, 4) * SIDE + lax.rem(side + step_x, SIDE)
                device = {"gauss": other * 2 + core, "view": view}
                pl.when(other != chip)(lambda other=other, device=device: action(other, device))

    def to_all(action):
        def one(number, unused):
            for step_x in (2, 1, 3, 0):
                other = number * SIDE + lax.rem(side + step_x, SIDE)
                device = {"gauss": other * 2 + core, "view": view}
                pl.when(other != chip)(lambda other=other, device=device: action(other, device))
            return unused

        lax.fori_loop(0, LINE, one, 0)

    def greet_late(other, device):
        pl.when(other >= RENDER)(lambda: greet(device))

    @pl.when(early)
    def greet_first():
        to_renderers(lambda other, device: greet(device))
        greet(other_core)

    over_views(lambda step, other, device: greet(device))

    pairs = [
        (rows_in, rows),
        (params_in, params),
        (camera_in, camera),
        (lists_in, lists),
        (counts_in, counts),
        (tile_ids_in, tile_ids),
        (target_in, target),
    ]
    copies = [
        pltpu.make_async_copy(source, place, loads.at[n]) for n, (source, place) in enumerate(pairs)
    ]
    for copy in copies:
        copy.start()

    pl.when(early)(lambda: to_all(greet_late))

    def remote(source, place, sent, arrived, device):
        return pltpu.make_async_remote_copy(
            src_ref=source,
            dst_ref=place,
            send_sem=sent,
            recv_sem=arrived,
            device_id=device,
            device_id_type=MESH,
        )

    def wait_rows(place, count, semaphore):
        whole = place.at[pl.ds(0, count)]
        pltpu.make_async_copy(whole, whole, semaphore).wait()

    low_lanes = iota((64, 128), 1) < 64
    mine = low_lanes == (core == 0)

    def with_other_core(source, place, sent, arrived):
        copy = remote(source, place, sent, arrived, other_core)
        copy.start()
        copy.wait()

    def joined(kept, given):
        return jnp.where(mine, kept, swap(given))

    copies[0].wait()
    table[...] = sender_table(rows[0])
    copies[1].wait()
    copies[2].wait()
    scalars = [camera[0, n] for n in range(12)]
    attributes = project([params[n : n + 1, :] for n in range(59)], scalars)
    messages = pack_messages(
        jnp.concatenate(attributes + [jnp.zeros((7, 512), f32)], axis=0), table[...]
    )
    for number in range(SHARE):
        msg[:, number, :] = messages[RENDER * number : RENDER * number + RENDER]
    for copy in copies[3:]:
        copy.wait()

    facts[0:2, :] = reorder_rows(lists[0], place_of)
    for tile in range(2):
        for channel in range(3):
            row = 2 + 3 * tile + channel
            facts[row : row + 1, :] = target[channel, tile : tile + 1, :]
    spots = iota((1, 256), 1)
    known = jnp.zeros((1, 256), f32)
    for tile in range(2):
        tile_id = tile_ids[0, tile]
        across = (16 * lax.rem(tile_id, 120)).astype(f32) + 7.5
        down = (16 * lax.div(tile_id, 120)).astype(f32) + 7.5
        for n, value in enumerate((across, down, counts[0, tile].astype(f32))):
            known = jnp.where(spots == 3 * tile + n, value, known)
    facts[8:16, :] = jnp.concatenate([known, jnp.zeros((7, 256), f32)], axis=0)

    pl.semaphore_wait(barrier, RENDER + VIEWS - 1)

    def send_attributes(other, device):
        remote(msg.at[other], land1.at[chip], send1, recv1, device).start()

    def send_gradients(other, device):
        remote(back2.at[other], land4.at[chip], send4, recv4, device).start()

    @pl.when(late)
    def send_facts():
        remote(facts, land_facts.at[turn - 1], send6, recv6.at[turn - 1], home).start()

    to_renderers(send_attributes)

    @pl.when(late)
    def late_part():
        remote(facts, land_facts.at[turn - 1], send6, recv6.at[turn - 1], home).wait_send()
        wait_rows(msg, RENDER, send1)
        remote(away.at[0], losses, send7.at[0], recv7, home).wait_recv()
        wait_rows(land4, RENDER, recv4)

    @pl.when(early)
    def render():
        land1[chip] = msg[chip]
        tables = [list_tables(facts[0:2, :])]
        for number in range(1, SHARE):
            place = land_facts.at[number - 1]
            remote(facts, place, send6, recv6.at[number - 1], served(number)).wait_recv()
            tables.append(list_tables(land_facts[number - 1, 0:2, :]))
        wait_rows(land1, CHIPS - 1, recv1)
        with_other_core(land1, land2, send2, recv2)

        tiles = range(2 * SHARE)
        entries, centres, shown = [], [], []
        for number in range(SHARE):
            found = pick(joined(land1[:, number, :], land2[:, number, :]), *tables[number])
            known = facts[...] if number == 0 else land_facts[number - 1]
            for part in range(2):
                chosen = found[:, 256 * part : 256 * part + 256]
                about = [known[8:9, 3 * part + n : 3 * part + n + 1] for n in range(3)]
                power, centre_u, centre_v = prepare_tile(chosen, *about)
                alphas[2 * number + part] = exponents(power)
                entries.append(chosen)
                centres.append((centre_u, centre_v))
                shown.append(known[2 + 3 * part : 5 + 3 * part])

        def forward(step, carry):
            rows_here = pl.ds(pl.multiple_of(step * 8, 8), 8)
            left = []
            for tile, keep in zip(tiles, carry):
                alpha = jnp.exp2(alphas[tile, rows_here, :])
                weight = keep * alpha
                alphas[tile, rows_here, :] = alpha
                weights[tile, rows_here, :] = weight
                left.append(keep - weight)
            return left

        keeps = lax.fori_loop(0, 32, forward, [jnp.ones((8, 256), f32) for tile in tiles], unroll=4)
        around = []
        for tile in tiles:
            colour = colour_sums(entries[tile][6:9], weights[tile])
            around.append(between(keeps[tile], colour, shown[tile]))
            shaded[tile] = shades(entries[tile][6:9], around[tile][2])
        spot = iota((1, 128), 1)
        for number in range(SHARE):
            pair = around[2 * number][3], around[2 * number + 1][3]
            row = jnp.where(spot == 0, pair[0], jnp.where(spot == 1, pair[1], 0.0))
            if number == 0:
                losses[...] = row
            else:
                away[number - 1] = row
                place = away.at[number - 1]
                remote(place, losses, send7.at[number - 1], recv7, served(number)).start()

        for first_tile in range(0, 2 * SHARE, 4):
            some = range(first_tile, first_tile + 4)

            def backward(step, later, some=some):
                rows_here = pl.ds(pl.multiple_of((31 - step) * 8, 8), 8)
                left = []
                for tile, behind in zip(some, later):
                    before, after = around[tile][0:2]
                    slope, weight, rest = back_step(
                        shaded[tile, rows_here, :],
                        alphas[tile, rows_here, :],
                        weights[tile, rows_here, :],
                        before,
                        after,
                        behind,
                    )
                    alphas[tile, rows_here, :] = slope
                    weights[tile, rows_here, :] = weight
                    left.append(rest)
                return left

            lax.fori_loop(0, 32, backward, [jnp.zeros((8, 256), f32)] * 4, unroll=8)
        for number in range(SHARE):
            grads = []
            for tile in (2 * number, 2 * number + 1):
                sums = moments(alphas[tile], weights[tile], around[tile][2])
                grads.append(finish_tile(sums, entries[tile], *centres[tile]))
            back1[number] = unpick(jnp.concatenate(grads, axis=1), *tables[number])

        with_other_core(back1, land3, send3, recv3)
        for number in range(SHARE):
            back2[:, number, :] = joined(back1[number], land3[number])
        to_all(send_gradients)
        land4[chip] = back2[chip]
        for number in range(1, SHARE):
            place = away.at[number - 1]
            remote(place, losses, send7.at[number - 1], recv7, served(number)).wait_send()
        wait_rows(msg, RENDER - 1, send1)
        wait_rows(land4, RENDER - 1, recv4)

    loss_copy = pltpu.make_async_copy(losses, loss, loads.at[7])
    loss_copy.start()
    returned = unpack_messages(
        jnp.concatenate([land4[:, number, :] for number in range(SHARE)], axis=0), table[...]
    )

    lanes = iota((1, 128), 1)
    pose = jnp.zeros((1, 128), f32)
    for n in range(12):
        pose = jnp.where(lanes == n, scalars[n], pose)
    for part in range(4):
        own[10 * part : 10 * part + 9, :] = returned[0:9, 128 * part : 128 * part + 128]
        own[10 * part + 9 : 10 * part + 10, :] = pose

    def share(step, other, device):
        remote(own, out.at[view], send5.at[step], recv5.at[view], device).start()

    def take(step, other, device):
        remote(own, out.at[other], send5.at[step], recv5.at[other], device).wait()

    over_views(share)
    keep = pltpu.make_async_copy(own, out.at[view], kept5)
    keep.start()
    pl.when(early)(lambda: wait_rows(back2, CHIPS - 1, send4))
    loss_copy.wait()
    keep.wait()
    over_views(take)


def update(
    params_in,
    first_in,
    second_in,
    grads_in,
    loss_in,
    new_params,
    new_first,
    new_second,
    tile_loss,
    params,
    first,
    second,
    grads,
    loss,
    spread,
    total,
    loads,
):
    pairs = [
        (params_in, params),
        (grads_in, grads),
        (first_in, first),
        (second_in, second),
        (loss_in, loss),
    ]
    copies = [
        pltpu.make_async_copy(source, place, loads.at[n]) for n, (source, place) in enumerate(pairs)
    ]
    for copy in copies:
        copy.start()
    copies[0].wait()

    for part in range(4):
        block = params[:, 128 * part : 128 * part + 128]
        for view in range(VIEWS):
            start = 64 * (4 * view + part)
            spread[start : start + 59, :] = block
    columns = [spread[pl.ds(n, 16, stride=64), :] for n in range(59)]
    copies[1].wait()
    given = [grads[pl.ds(n, 16, stride=10), :] for n in range(10)]
    camera = [given[9][:, n : n + 1] for n in range(12)]

    def shown(rows):
        attributes = project(rows, camera)
        return attributes[0:5] + attributes[6:9]

    pulled = jax.vjp(shown, columns)[1](given[0:5] + given[6:9])[0]
    pulled[10] = given[5] * (1.0 - 1.0 / (1.0 + jnp.exp(-columns[10])))
    for n in range(59):
        both = pulled[n][0:8] + pulled[n][8:16]
        total[pl.ds(n, 4, stride=64), :] = both[0:4] + both[4:8]
    for copy in copies[2:]:
        copy.wait()
    row = iota((59, 1), 0)
    rate = jnp.where(row < 3, 0.00016, 0.005)
    rate = jnp.where(row < 6, rate, 0.001)
    rate = jnp.where(row < 10, rate, 0.05)
    rate = jnp.where(row < 11, rate, 0.0025)
    rate = jnp.where(row < 14, rate, 0.000125)
    rate = rate / (1.0 - beta_one**adam_step)
    for part in range(4):
        here = slice(128 * part, 128 * part + 128)
        slope = total[64 * part : 64 * part + 59, :]
        moved = beta_one * first[:, here] + (1.0 - beta_one) * slope
        square = beta_two * second[:, here] + (1.0 - beta_two) * slope * slope
        new_first[:, here] = moved
        new_second[:, here] = square
        new_params[:, here] = params[:, here] - rate * moved / (
            jnp.sqrt(square / (1.0 - beta_two**adam_step)) + adam_eps
        )
    tile_loss[...] = loss[:, 0:2]


def body(params, first_moment, second_moment, cameras, send_rows, lists, counts, tile_ids, target):
    vmem = pl.BlockSpec(memory_space=pltpu.VMEM)
    hbm = pl.BlockSpec(memory_space=pltpu.HBM)
    dma = pltpu.SemaphoreType.DMA
    whole = jax.ShapeDtypeStruct((59, 512), f32)
    some = pltpu.CompilerParams(vmem_limit_bytes=VMEM_BYTES)
    grads, loss = pl.pallas_call(
        exchange,
        out_shape=(
            jax.ShapeDtypeStruct((VIEWS, 40, 128), f32),
            jax.ShapeDtypeStruct((1, 128), f32),
        ),
        in_specs=[hbm] * 7,
        out_specs=(hbm,) * 2,
        scratch_shapes=[
            pltpu.VMEM((59, 512), f32),
            pltpu.SMEM((1, 12), f32),
            pltpu.VMEM((1, 1, 512), jnp.int32),
            pltpu.VMEM((1, 2, 256), jnp.int32),
            pltpu.SMEM((1, 2), jnp.int32),
            pltpu.SMEM((1, 2), jnp.int32),
            pltpu.VMEM((3, 2, 256), f32),
            pltpu.VMEM((RENDER, SHARE, 128), f32),
            pltpu.VMEM((CHIPS, SHARE, 128), f32),
            pltpu.VMEM((CHIPS, SHARE, 128), f32),
            pltpu.VMEM((SHARE, CHIPS, 128), f32),
            pltpu.VMEM((SHARE, CHIPS, 128), f32),
            pltpu.VMEM((CHIPS, SHARE, 128), f32),
            pltpu.VMEM((RENDER, SHARE, 128), f32),
            pltpu.VMEM((16, 256), f32),
            pltpu.VMEM((SHARE - 1, 16, 256), f32),
            pltpu.VMEM((40, 128), f32),
            pltpu.VMEM((1, 128), f32),
            pltpu.VMEM((SHARE - 1, 1, 128), f32),
            pltpu.VMEM((2 * SHARE, 256, 256), f32),
            pltpu.VMEM((2 * SHARE, 256, 256), f32),
            pltpu.VMEM((2 * SHARE, 256, 256), f32),
            pltpu.VMEM((512, 512), bf16),
            dma((8,)),
            dma,
            dma,
            dma,
            dma,
            dma,
            dma,
            dma,
            dma,
            dma((VIEWS,)),
            dma((VIEWS,)),
            dma,
            dma,
            dma((SHARE - 1,)),
            dma((SHARE - 1,)),
            dma,
        ],
        compiler_params=pltpu.CompilerParams(
            collective_id=0, has_side_effects=True, vmem_limit_bytes=VMEM_BYTES
        ),
        name="exchange",
    )(
        params,
        cameras,
        send_rows,
        lists,
        counts,
        tile_ids,
        target[0].transpose(1, 0, 2),
    )
    near = pltpu.VMEM((59, 512), f32)
    return pl.pallas_call(
        update,
        out_shape=(whole, whole, whole, jax.ShapeDtypeStruct((1, 2), f32)),
        in_specs=[hbm] * 5,
        out_specs=(vmem,) * 4,
        scratch_shapes=[
            near,
            near,
            near,
            pltpu.VMEM((VIEWS * 40, 128), f32),
            pltpu.VMEM((1, 128), f32),
            pltpu.VMEM((1024, 128), f32),
            pltpu.VMEM((256, 128), f32),
            dma((5,)),
        ],
        compiler_params=some,
        name="update",
    )(params, first_moment, second_moment, grads.reshape(VIEWS * 40, 128), loss)


def solution(mesh):
    in_specs = (
        P(None, "gauss"),
        P(None, "gauss"),
        P(None, "gauss"),
        P("view", None),
        P("view", "gauss", None),
        P("view", "gauss", None),
        P("view", "gauss"),
        P("view", "gauss"),
        P("view", "gauss", None, None),
    )
    out_specs = (P(None, "gauss"), P(None, "gauss"), P(None, "gauss"), P("view", "gauss"))
    return jax.shard_map(body, mesh=mesh, in_specs=in_specs, out_specs=out_specs, check_vma=False)
```

```python
import jax
import jax.numpy as jnp
from jax import lax
from jax.experimental import pallas as pl
from jax.experimental.pallas import tpu as pltpu
from jax.sharding import PartitionSpec as P

focal_length = 1100.0
centre_x = 960.0
centre_y = 540.0
beta_one = 0.9
beta_two = 0.999
adam_eps = 1e-15
adam_step = 100.0
log2_e = 1.4426950408889634
sh_zero = 0.28209479177387814
sh_one = 0.4886025119029199
sh_two = [
    1.0925484305920792,
    -1.0925484305920792,
    0.31539156525252005,
    -1.0925484305920792,
    0.5462742152960396,
]
sh_three = [
    -0.5900435899266435,
    2.890611442640554,
    -0.4570457994644658,
    0.3731763325901154,
    -0.4570457994644658,
    1.445305721320277,
    -0.5900435899266435,
]
LINE = 16
SIDE = 4
CHIPS = LINE * SIDE
SHARE = 4
RENDER = CHIPS // SHARE
VIEWS = 4
VMEM_BYTES = 62 * 1024 * 1024
MESH = pl.DeviceIdType.MESH
f32 = jnp.float32
bf16 = jnp.bfloat16


def harmonics(dir_x, dir_y, dir_z):
    sq_x = dir_x * dir_x
    sq_y = dir_y * dir_y
    sq_z = dir_z * dir_z
    return [
        -sh_one * dir_y,
        sh_one * dir_z,
        -sh_one * dir_x,
        sh_two[0] * dir_x * dir_y,
        sh_two[1] * dir_y * dir_z,
        sh_two[2] * (2.0 * sq_z - sq_x - sq_y),
        sh_two[3] * dir_x * dir_z,
        sh_two[4] * (sq_x - sq_y),
        sh_three[0] * dir_y * (3.0 * sq_x - sq_y),
        sh_three[1] * dir_x * dir_y * dir_z,
        sh_three[2] * dir_y * (4.0 * sq_z - sq_x - sq_y),
        sh_three[3] * dir_z * (2.0 * sq_z - 3.0 * sq_x - 3.0 * sq_y),
        sh_three[4] * dir_x * (4.0 * sq_z - sq_x - sq_y),
        sh_three[5] * dir_z * (sq_x - sq_y),
        sh_three[6] * dir_x * (sq_x - 3.0 * sq_y),
    ]


def project(columns, camera):
    mean_x, mean_y, mean_z = columns[0], columns[1], columns[2]
    scales = [jnp.exp(columns[3 + axis]) for axis in range(3)]
    quat_w, quat_x, quat_y, quat_z = columns[6:10]
    norm = 1.0 / jnp.sqrt(quat_w * quat_w + quat_x * quat_x + quat_y * quat_y + quat_z * quat_z)
    quat_w, quat_x, quat_y, quat_z = quat_w * norm, quat_x * norm, quat_y * norm, quat_z * norm
    turn = [
        [
            1.0 - 2.0 * (quat_y * quat_y + quat_z * quat_z),
            2.0 * (quat_x * quat_y - quat_w * quat_z),
            2.0 * (quat_x * quat_z + quat_w * quat_y),
        ],
        [
            2.0 * (quat_x * quat_y + quat_w * quat_z),
            1.0 - 2.0 * (quat_x * quat_x + quat_z * quat_z),
            2.0 * (quat_y * quat_z - quat_w * quat_x),
        ],
        [
            2.0 * (quat_x * quat_z - quat_w * quat_y),
            2.0 * (quat_y * quat_z + quat_w * quat_x),
            1.0 - 2.0 * (quat_x * quat_x + quat_y * quat_y),
        ],
    ]
    world = [[turn[outer][inner] * scales[inner] for inner in range(3)] for outer in range(3)]
    cam_x, cam_y, depth = [
        camera[3 * outer] * mean_x
        + camera[3 * outer + 1] * mean_y
        + camera[3 * outer + 2] * mean_z
        + camera[9 + outer]
        for outer in range(3)
    ]
    framed = [
        [
            camera[3 * outer] * world[0][inner]
            + camera[3 * outer + 1] * world[1][inner]
            + camera[3 * outer + 2] * world[2][inner]
            for inner in range(3)
        ]
        for outer in range(3)
    ]
    inverse = 1.0 / depth
    near = focal_length * inverse
    slope_x = cam_x * inverse
    slope_y = cam_y * inverse
    row_top = [near * (framed[0][inner] - slope_x * framed[2][inner]) for inner in range(3)]
    row_low = [near * (framed[1][inner] - slope_y * framed[2][inner]) for inner in range(3)]
    cov_a = row_top[0] * row_top[0] + row_top[1] * row_top[1] + row_top[2] * row_top[2] + 0.3
    cov_b = row_top[0] * row_low[0] + row_top[1] * row_low[1] + row_top[2] * row_low[2]
    cov_c = row_low[0] * row_low[0] + row_low[1] * row_low[1] + row_low[2] * row_low[2] + 0.3
    over = 1.0 / (cov_a * cov_c - cov_b * cov_b)
    centre_u = focal_length * slope_x + centre_x
    centre_v = focal_length * slope_y + centre_y
    away = 1.0 / jnp.sqrt(cam_x * cam_x + cam_y * cam_y + depth * depth)
    basis = harmonics(cam_x * away, cam_y * away, depth * away)
    colours = []
    for channel in range(3):
        total = 0.5 + sh_zero * columns[11 + channel]
        for order in range(15):
            total = total + basis[order] * columns[14 + 3 * order + channel]
        colours.append(total)
    opacity = 1.0 / (1.0 + jnp.exp(-columns[10]))
    return [
        centre_u,
        centre_v,
        cov_c * over,
        -cov_b * over,
        cov_a * over,
        opacity,
        colours[0],
        colours[1],
        colours[2],
    ]


def pieces(value):
    high = value.astype(bf16)
    rest = value - high.astype(f32)
    middle = rest.astype(bf16)
    low = (rest - middle.astype(f32)).astype(bf16)
    return high, middle, low


def dot_rows(left, right):
    return lax.dot_general(left, right, (((1,), (1,)), ((), ())), preferred_element_type=f32)


def add_pieces(stacked):
    rows = stacked.shape[0] // 3
    return (stacked[0:rows] + stacked[rows : 2 * rows]) + stacked[2 * rows :]


def dot_exact(left, right):
    stacked = jnp.concatenate(pieces(left), axis=0)
    return add_pieces(jnp.dot(stacked, right, preferred_element_type=f32))


def dot_rows_exact(left, right):
    return add_pieces(dot_rows(jnp.concatenate(pieces(left), axis=0), right))


def iota(shape, axis):
    return lax.broadcasted_iota(jnp.int32, shape, axis)


def one_hot(test):
    return jnp.where(test, 1.0, 0.0).astype(bf16)


def swap(value):
    return pltpu.roll(value, 64, 1)


def reorder_rows(rows, place):
    number, width = rows.shape
    padding = jnp.zeros((8 - 2 * number, width), jnp.int32)
    split_rows = jnp.concatenate([rows >> 4, rows & 15, padding], axis=0)
    chosen = one_hot(iota((width, width), 0) == place(iota((width, width), 1)))
    moved = jnp.dot(split_rows.astype(f32).astype(bf16), chosen, preferred_element_type=f32)
    return moved[0:number] * 16.0 + moved[number : 2 * number]


def sender_table(rows):
    moved = reorder_rows(rows, lambda n: 8 * (n & 63) + (n >> 6))
    return one_hot(iota((512, 512), 0) == moved.astype(jnp.int32))


def pack_messages(attributes, table):
    placed = dot_exact(attributes, table)
    turned = jnp.transpose(jnp.concatenate([placed, jnp.zeros((112, 512), f32)], axis=0))
    lanes = iota((16, 128), 1)
    rows = [jnp.zeros((16, 128), f32)] * 3
    for group in range(8):
        for number in range(SHARE):
            slot = SHARE * group + number
            block = turned[16 * slot : 16 * slot + 16]
            most = jnp.where(lanes < 8, block, 0.0)
            last = jnp.where(lanes == 8, block, 0.0)
            rows[group // 4] = rows[group // 4] + pltpu.roll(most, 8 * (slot % 16), 1)
            rows[2] = rows[2] + pltpu.roll(last, (8 * number + group - 8) % 128, 1)
    return rows


def unpack_messages(messages, table):
    turned = jnp.transpose(jnp.concatenate([messages, jnp.zeros_like(messages)], axis=0))
    keep = iota((16, 128), 1) < 64
    parts = []
    for pair in range(4):
        left = turned[32 * pair : 32 * pair + 16]
        right = turned[32 * pair + 16 : 32 * pair + 32]
        parts.append(jnp.where(keep, left, swap(right)))
    return dot_rows_exact(jnp.concatenate(parts, axis=1), table)


def list_tables(lists):
    slot = jnp.concatenate([lists[0:1], lists[1:2]], axis=1).astype(jnp.int32)
    return one_hot(iota((64, 512), 0) == (slot >> 3)), slot & 7


def turn_received(rows):
    blank = jnp.zeros((64, 128), f32)
    return [jnp.transpose(jnp.concatenate([row, blank], axis=0))[:, 0:64] for row in rows]


def pick(first, second, core, number, table, group):
    most, last = [], []
    for turned in (first, second):
        mine = jnp.where(core == 0, turned[0], turned[1])
        most += [mine[8 * (SHARE * n + number) :][0:8] for n in range(4)]
        ninth = turned[2][8 * number : 8 * number + 8]
        last.append(jnp.where(core == 0, ninth[0:4], ninth[4:8]))
    found = dot_exact(jnp.concatenate(most + last, axis=0), table)
    eight = jnp.where((iota((64, 512), 0) >> 3) == group, found[0:64], 0.0)
    total = eight[0:8]
    for part in range(1, 8):
        total = total + eight[8 * part : 8 * part + 8]
    ninth = jnp.where(iota((8, 512), 0) == group, found[64:72], 0.0)
    return jnp.concatenate([total, jnp.sum(ninth, axis=0, keepdims=True)], axis=0)


def unpick(grads, table, group):
    spread = jnp.concatenate([grads] * 8, axis=0)
    spread = jnp.where((iota((128, 512), 0) >> 4) == group, spread, 0.0)
    turned = dot_rows_exact(spread, table)
    return jnp.transpose(jnp.concatenate([turned, jnp.zeros((128, 64), f32)], axis=1))[0:64]


def place_of(position):
    return 32 * (position & 7) + (position >> 3)


def split(rows):
    return [part.astype(f32) for part in pieces(rows)]


def split(rows):
    return [part.astype(f32) for part in pieces(rows)]


def two_pieces(value):
    high = value.astype(bf16)
    return high, (value - high.astype(f32)).astype(bf16)


def padded(rows):
    number = sum(part.shape[0] for part in rows)
    return jnp.concatenate(rows + [jnp.zeros((32 - number, 256), f32)], axis=0).astype(bf16)


def dot_columns(left, right):
    return lax.dot_general(left, right, (((0,), (0,)), ((), ())), preferred_element_type=f32)


def prepare_tile(attributes, across, down, count):
    centre_u = attributes[0:1] - across
    centre_v = attributes[1:2] - down
    alive = place_of(iota((1, 256), 1)).astype(f32) < count
    by_xx = attributes[2:3] * (-0.5 * log2_e)
    by_xy = attributes[3:4] * (-log2_e)
    by_yy = attributes[4:5] * (-0.5 * log2_e)
    by_x = -2.0 * by_xx * centre_u - by_xy * centre_v
    by_y = -2.0 * by_yy * centre_v - by_xy * centre_u
    whole = (by_xx * centre_u + by_xy * centre_v) * centre_u + (by_yy * centre_v) * centre_v
    whole = jnp.where(alive, whole + jnp.log(attributes[5:6]) * log2_e, -1e30)
    power = jnp.concatenate([whole, by_x, by_y, by_xx, by_xy, by_yy], axis=0)
    return power, centre_u, centre_v


def pixels():
    number = iota((1, 256), 1)
    return (number & 15).astype(f32) - 7.5, (number >> 4).astype(f32) - 7.5


def monomials():
    pixel_x, pixel_y = pixels()
    ones = jnp.ones((1, 256), f32)
    return [ones, pixel_x, pixel_y, pixel_x * pixel_x, pixel_x * pixel_y, pixel_y * pixel_y]


def exponents(power):
    return dot_columns(padded(split(power)), padded(monomials() * 3))


def colour_sums(colour, weight):
    chunk = (iota((8, 256), 1) & 7) == iota((8, 256), 0)
    spread = [jnp.where(chunk, colour[c : c + 1], 0.0) for c in range(3)]
    left = jnp.concatenate(split(jnp.concatenate(spread, axis=0)), axis=0).astype(bf16)
    high, middle = two_pieces(weight)
    total = jnp.dot(left, middle, preferred_element_type=f32)
    total = total + jnp.dot(left, high, preferred_element_type=f32)
    total = add_pieces(total)
    return [total[8 * c : 8 * c + 8] for c in range(3)]


def shades(colour, residual):
    high, middle, low = split(colour)
    left = padded([high, high, high, middle, middle, low])
    high, middle, low = split(jnp.concatenate(residual, axis=0))
    return dot_columns(left, padded([high, middle, low, high, middle, high]))


def between(keep, colour, target):
    before = [jnp.ones((1, 256), f32)]
    for chunk in range(7):
        before.append(before[-1] * keep[chunk : chunk + 1])
    before = jnp.concatenate(before, axis=0)
    colour = [part * before for part in colour]
    residual = [jnp.sum(colour[c], axis=0, keepdims=True) - target[c : c + 1] for c in range(3)]
    own = residual[0] * colour[0] + residual[1] * colour[1] + residual[2] * colour[2]
    after = [jnp.zeros((1, 256), f32)]
    for chunk in range(7, 0, -1):
        after.append(after[-1] + own[chunk : chunk + 1])
    after = jnp.concatenate(after[::-1], axis=0)
    squares = residual[0] * residual[0] + residual[1] * residual[1] + residual[2] * residual[2]
    return before, after, residual, 0.5 * jnp.sum(squares, axis=1, keepdims=True)


def back_step(shade, alpha, weight, before, after, later):
    own = weight * shade
    left = 1.0 - alpha
    guess = pl.reciprocal(left, approx=True)
    ratio = alpha * (guess * (2.0 - left * guess))
    slope = before * own - (before * later + after) * ratio
    return slope, before * weight, later + own


def moments(slope, weight, residual):
    shown = split(jnp.concatenate(residual, axis=0))
    factors = jnp.concatenate(monomials() + shown + [jnp.zeros((1, 256), f32)], axis=0).astype(bf16)

    def over_pixels(value):
        high, middle = two_pieces(value)
        return dot_rows(factors, middle) + dot_rows(factors, high)

    by_power = over_pixels(slope)[0:6]
    by_shown = over_pixels(weight)
    by_shown = by_shown[6:9] + (by_shown[9:12] + by_shown[12:15])
    return jnp.concatenate([by_power, by_shown], axis=0)


def finish_tile(sums, attributes, centre_u, centre_v):
    whole, by_x, by_y, by_xx, by_xy, by_yy = [sums[n : n + 1] for n in range(6)]
    sum_x = by_x - centre_u * whole
    sum_y = by_y - centre_v * whole
    sum_xx = by_xx - centre_u * (by_x + sum_x)
    sum_xy = by_xy - centre_u * by_y - centre_v * sum_x
    sum_yy = by_yy - centre_v * (by_y + sum_y)
    conic = [attributes[2 + n : 3 + n] for n in range(3)]
    rows = [
        conic[0] * sum_x + conic[1] * sum_y,
        conic[1] * sum_x + conic[2] * sum_y,
        -0.5 * sum_xx,
        -sum_xy,
        -0.5 * sum_yy,
        whole,
        sums[6:9],
        jnp.zeros((7, 256), f32),
    ]
    return jnp.concatenate(rows, axis=0)


def exchange(
    params_in,
    camera_in,
    rows_in,
    lists_in,
    counts_in,
    tile_ids_in,
    target_in,
    out,
    loss,
    params,
    camera,
    rows,
    lists,
    counts,
    tile_ids,
    target,
    msg,
    land1,
    land2,
    back1,
    land3,
    back2,
    land4,
    facts,
    land_facts,
    own,
    losses,
    away,
    alphas,
    weights,
    shaded,
    table,
    loads,
    send1,
    recv1,
    send2,
    recv2,
    send3,
    recv3,
    send4,
    recv4,
    send5,
    recv5,
    kept5,
    send6,
    recv6,
    send7,
    recv7,
):
    here = lax.axis_index("gauss")
    view = lax.axis_index("view")
    core = lax.rem(here, 2)
    chip = here // 2
    line = chip // SIDE
    side = lax.rem(chip, SIDE)

    other_core = {"gauss": here + 1 - 2 * core, "view": view}

    def over_views(action):
        for step in (2, 1, 3):
            other = lax.rem(view + step, VIEWS)
            action(step, other, {"gauss": here, "view": other})

    barrier = pltpu.get_barrier_semaphore()

    def greet(device):
        pl.semaphore_signal(barrier, inc=1, device_id=device, device_id_type=MESH)

    early = chip < RENDER
    late = jnp.logical_not(early)
    home = {"gauss": lax.rem(chip, RENDER) * 2 + core, "view": view}
    turn = chip // RENDER

    def served(number):
        return {"gauss": lax.rem(chip + number * RENDER, CHIPS) * 2 + core, "view": view}

    def to_renderers(action):
        for step_z in (0, 1, 3, 2):
            for step_x in (2, 1, 3, 0):
                other = lax.rem(line + step_z, 4) * SIDE + lax.rem(side + step_x, SIDE)
                device = {"gauss": other * 2 + core, "view": view}
                pl.when(other != chip)(lambda other=other, device=device: action(other, device))

    def to_all(action):
        def one(number, unused):
            for step_x in (2, 1, 3, 0):
                other = number * SIDE + lax.rem(side + step_x, SIDE)
                device = {"gauss": other * 2 + core, "view": view}
                pl.when(other != chip)(lambda other=other, device=device: action(other, device))
            return unused

        lax.fori_loop(0, LINE, one, 0)

    def greet_late(other, device):
        pl.when(other >= RENDER)(lambda: greet(device))

    @pl.when(early)
    def greet_first():
        to_renderers(lambda other, device: greet(device))
        greet(other_core)

    over_views(lambda step, other, device: greet(device))

    pairs = [
        (rows_in, rows),
        (params_in, params),
        (camera_in, camera),
        (lists_in, lists),
        (counts_in, counts),
        (tile_ids_in, tile_ids),
        (target_in, target),
    ]
    copies = [
        pltpu.make_async_copy(source, place, loads.at[n]) for n, (source, place) in enumerate(pairs)
    ]
    for copy in copies:
        copy.start()

    pl.when(early)(lambda: to_all(greet_late))

    def remote(source, place, sent, arrived, device):
        return pltpu.make_async_remote_copy(
            src_ref=source,
            dst_ref=place,
            send_sem=sent,
            recv_sem=arrived,
            device_id=device,
            device_id_type=MESH,
        )

    def wait_rows(place, count, semaphore):
        whole = place.at[pl.ds(0, count)]
        pltpu.make_async_copy(whole, whole, semaphore).wait()

    low_lanes = iota((64, 128), 1) < 64
    mine = low_lanes == (core == 0)

    def with_other_core(source, place, sent, arrived):
        copy = remote(source, place, sent, arrived, other_core)
        copy.start()
        copy.wait()

    def joined(kept, given):
        return jnp.where(mine, kept, swap(given))

    copies[0].wait()
    table[...] = sender_table(rows[0])
    copies[1].wait()
    copies[2].wait()
    scalars = [camera[0, n] for n in range(12)]
    attributes = project([params[n : n + 1, :] for n in range(59)], scalars)
    messages = pack_messages(
        jnp.concatenate(attributes + [jnp.zeros((7, 512), f32)], axis=0), table[...]
    )
    for number in range(3):
        msg[:, number, 0, :] = messages[number]
    for copy in copies[3:]:
        copy.wait()

    facts[0:2, :] = reorder_rows(lists[0], place_of)
    for tile in range(2):
        for channel in range(3):
            row = 2 + 3 * tile + channel
            facts[row : row + 1, :] = target[channel, tile : tile + 1, :]
    spots = iota((1, 256), 1)
    known = jnp.zeros((1, 256), f32)
    for tile in range(2):
        tile_id = tile_ids[0, tile]
        across = (16 * lax.rem(tile_id, 120)).astype(f32) + 7.5
        down = (16 * lax.div(tile_id, 120)).astype(f32) + 7.5
        for n, value in enumerate((across, down, counts[0, tile].astype(f32))):
            known = jnp.where(spots == 3 * tile + n, value, known)
    facts[8:16, :] = jnp.concatenate([known, jnp.zeros((7, 256), f32)], axis=0)

    pl.semaphore_wait(barrier, RENDER + VIEWS - 1)

    def send_attributes(other, device):
        remote(msg.at[other], land1.at[chip], send1, recv1, device).start()

    def send_gradients(other, device):
        remote(back2.at[other], land4.at[chip], send4, recv4, device).start()

    @pl.when(late)
    def send_facts():
        remote(facts, land_facts.at[turn - 1], send6, recv6.at[turn - 1], home).start()

    to_renderers(send_attributes)

    @pl.when(late)
    def late_part():
        remote(facts, land_facts.at[turn - 1], send6, recv6.at[turn - 1], home).wait_send()
        wait_rows(msg, RENDER, send1)
        remote(away.at[0], losses, send7.at[0], recv7, home).wait_recv()
        wait_rows(land4, RENDER, recv4)

    @pl.when(early)
    def render():
        land1[chip] = msg[chip]
        tables = [list_tables(facts[0:2, :])]
        for number in range(1, SHARE):
            place = land_facts.at[number - 1]
            remote(facts, place, send6, recv6.at[number - 1], served(number)).wait_recv()
            tables.append(list_tables(land_facts[number - 1, 0:2, :]))
        wait_rows(land1, CHIPS - 1, recv1)
        with_other_core(land1, land2, send2, recv2)

        kept = turn_received([land1[:, n, 0, :] for n in range(3)])
        given = turn_received([land2[:, n, 0, :] for n in range(3)])
        first = [jnp.where(core == 0, a, b) for a, b in zip(kept, given)]
        second = [jnp.where(core == 0, b, a) for a, b in zip(kept, given)]
        tiles = range(2 * SHARE)
        entries, centres, shown = [], [], []
        for number in range(SHARE):
            found = pick(first, second, core, number, *tables[number])
            known = facts[...] if number == 0 else land_facts[number - 1]
            for part in range(2):
                chosen = found[:, 256 * part : 256 * part + 256]
                about = [known[8:9, 3 * part + n : 3 * part + n + 1] for n in range(3)]
                power, centre_u, centre_v = prepare_tile(chosen, *about)
                alphas[2 * number + part] = exponents(power)
                entries.append(chosen)
                centres.append((centre_u, centre_v))
                shown.append(known[2 + 3 * part : 5 + 3 * part])

        def forward(step, carry):
            rows_here = pl.ds(pl.multiple_of(step * 8, 8), 8)
            left = []
            for tile, keep in zip(tiles, carry):
                alpha = jnp.exp2(alphas[tile, rows_here, :])
                weight = keep * alpha
                alphas[tile, rows_here, :] = alpha
                weights[tile, rows_here, :] = weight
                left.append(keep - weight)
            return left

        keeps = lax.fori_loop(0, 32, forward, [jnp.ones((8, 256), f32) for tile in tiles], unroll=4)
        around = []
        for tile in tiles:
            colour = colour_sums(entries[tile][6:9], weights[tile])
            around.append(between(keeps[tile], colour, shown[tile]))
            shaded[tile] = shades(entries[tile][6:9], around[tile][2])
        spot = iota((1, 128), 1)
        for number in range(SHARE):
            pair = around[2 * number][3], around[2 * number + 1][3]
            row = jnp.where(spot == 0, pair[0], jnp.where(spot == 1, pair[1], 0.0))
            if number == 0:
                losses[...] = row
            else:
                away[number - 1] = row
                place = away.at[number - 1]
                remote(place, losses, send7.at[number - 1], recv7, served(number)).start()

        for first_tile in range(0, 2 * SHARE, 4):
            some = range(first_tile, first_tile + 4)

            def backward(step, later, some=some):
                rows_here = pl.ds(pl.multiple_of((31 - step) * 8, 8), 8)
                left = []
                for tile, behind in zip(some, later):
                    before, after = around[tile][0:2]
                    slope, weight, rest = back_step(
                        shaded[tile, rows_here, :],
                        alphas[tile, rows_here, :],
                        weights[tile, rows_here, :],
                        before,
                        after,
                        behind,
                    )
                    alphas[tile, rows_here, :] = slope
                    weights[tile, rows_here, :] = weight
                    left.append(rest)
                return left

            lax.fori_loop(0, 32, backward, [jnp.zeros((8, 256), f32)] * 4, unroll=8)
        for number in range(SHARE):
            grads = []
            for tile in (2 * number, 2 * number + 1):
                sums = moments(alphas[tile], weights[tile], around[tile][2])
                grads.append(finish_tile(sums, entries[tile], *centres[tile]))
            back1[number] = unpick(jnp.concatenate(grads, axis=1), *tables[number])

        with_other_core(back1, land3, send3, recv3)
        for number in range(SHARE):
            back2[:, number, :] = joined(back1[number], land3[number])
        to_all(send_gradients)
        land4[chip] = back2[chip]
        for number in range(1, SHARE):
            place = away.at[number - 1]
            remote(place, losses, send7.at[number - 1], recv7, served(number)).wait_send()
        wait_rows(msg, RENDER - 1, send1)
        wait_rows(land4, RENDER - 1, recv4)

    loss_copy = pltpu.make_async_copy(losses, loss, loads.at[7])
    loss_copy.start()
    returned = unpack_messages(
        jnp.concatenate([land4[:, number, :] for number in range(SHARE)], axis=0), table[...]
    )

    lanes = iota((1, 128), 1)
    pose = jnp.zeros((1, 128), f32)
    for n in range(12):
        pose = jnp.where(lanes == n, scalars[n], pose)
    for part in range(4):
        own[10 * part : 10 * part + 9, :] = returned[0:9, 128 * part : 128 * part + 128]
        own[10 * part + 9 : 10 * part + 10, :] = pose

    def share(step, other, device):
        remote(own, out.at[view], send5.at[step], recv5.at[view], device).start()

    def take(step, other, device):
        remote(own, out.at[other], send5.at[step], recv5.at[other], device).wait()

    over_views(share)
    keep = pltpu.make_async_copy(own, out.at[view], kept5)
    keep.start()
    pl.when(early)(lambda: wait_rows(back2, CHIPS - 1, send4))
    loss_copy.wait()
    keep.wait()
    over_views(take)


def update(
    params_in,
    first_in,
    second_in,
    grads_in,
    loss_in,
    new_params,
    new_first,
    new_second,
    tile_loss,
    params,
    first,
    second,
    grads,
    loss,
    spread,
    total,
    loads,
):
    pairs = [
        (params_in, params),
        (grads_in, grads),
        (first_in, first),
        (second_in, second),
        (loss_in, loss),
    ]
    copies = [
        pltpu.make_async_copy(source, place, loads.at[n]) for n, (source, place) in enumerate(pairs)
    ]
    for copy in copies:
        copy.start()
    copies[0].wait()

    for part in range(4):
        block = params[:, 128 * part : 128 * part + 128]
        for view in range(VIEWS):
            start = 64 * (4 * view + part)
            spread[start : start + 59, :] = block
    columns = [spread[pl.ds(n, 16, stride=64), :] for n in range(59)]
    copies[1].wait()
    given = [grads[pl.ds(n, 16, stride=10), :] for n in range(10)]
    camera = [given[9][:, n : n + 1] for n in range(12)]

    def shown(rows):
        attributes = project(rows, camera)
        return attributes[0:5] + attributes[6:9]

    pulled = jax.vjp(shown, columns)[1](given[0:5] + given[6:9])[0]
    pulled[10] = given[5] * (1.0 - 1.0 / (1.0 + jnp.exp(-columns[10])))
    for n in range(59):
        both = pulled[n][0:8] + pulled[n][8:16]
        total[pl.ds(n, 4, stride=64), :] = both[0:4] + both[4:8]
    for copy in copies[2:]:
        copy.wait()
    row = iota((59, 1), 0)
    rate = jnp.where(row < 3, 0.00016, 0.005)
    rate = jnp.where(row < 6, rate, 0.001)
    rate = jnp.where(row < 10, rate, 0.05)
    rate = jnp.where(row < 11, rate, 0.0025)
    rate = jnp.where(row < 14, rate, 0.000125)
    rate = rate / (1.0 - beta_one**adam_step)
    for part in range(4):
        here = slice(128 * part, 128 * part + 128)
        slope = total[64 * part : 64 * part + 59, :]
        moved = beta_one * first[:, here] + (1.0 - beta_one) * slope
        square = beta_two * second[:, here] + (1.0 - beta_two) * slope * slope
        new_first[:, here] = moved
        new_second[:, here] = square
        new_params[:, here] = params[:, here] - rate * moved / (
            jnp.sqrt(square / (1.0 - beta_two**adam_step)) + adam_eps
        )
    tile_loss[...] = loss[:, 0:2]


def body(params, first_moment, second_moment, cameras, send_rows, lists, counts, tile_ids, target):
    vmem = pl.BlockSpec(memory_space=pltpu.VMEM)
    hbm = pl.BlockSpec(memory_space=pltpu.HBM)
    dma = pltpu.SemaphoreType.DMA
    whole = jax.ShapeDtypeStruct((59, 512), f32)
    some = pltpu.CompilerParams(vmem_limit_bytes=VMEM_BYTES)
    grads, loss = pl.pallas_call(
        exchange,
        out_shape=(
            jax.ShapeDtypeStruct((VIEWS, 40, 128), f32),
            jax.ShapeDtypeStruct((1, 128), f32),
        ),
        in_specs=[hbm] * 7,
        out_specs=(hbm,) * 2,
        scratch_shapes=[
            pltpu.VMEM((59, 512), f32),
            pltpu.SMEM((1, 12), f32),
            pltpu.VMEM((1, 1, 512), jnp.int32),
            pltpu.VMEM((1, 2, 256), jnp.int32),
            pltpu.SMEM((1, 2), jnp.int32),
            pltpu.SMEM((1, 2), jnp.int32),
            pltpu.VMEM((3, 2, 256), f32),
            pltpu.VMEM((RENDER, 3, 1, 128), f32),
            pltpu.VMEM((CHIPS, 3, 1, 128), f32),
            pltpu.VMEM((CHIPS, 3, 1, 128), f32),
            pltpu.VMEM((SHARE, CHIPS, 128), f32),
            pltpu.VMEM((SHARE, CHIPS, 128), f32),
            pltpu.VMEM((CHIPS, SHARE, 128), f32),
            pltpu.VMEM((RENDER, SHARE, 128), f32),
            pltpu.VMEM((16, 256), f32),
            pltpu.VMEM((SHARE - 1, 16, 256), f32),
            pltpu.VMEM((40, 128), f32),
            pltpu.VMEM((1, 128), f32),
            pltpu.VMEM((SHARE - 1, 1, 128), f32),
            pltpu.VMEM((2 * SHARE, 256, 256), f32),
            pltpu.VMEM((2 * SHARE, 256, 256), f32),
            pltpu.VMEM((2 * SHARE, 256, 256), f32),
            pltpu.VMEM((512, 512), bf16),
            dma((8,)),
            dma,
            dma,
            dma,
            dma,
            dma,
            dma,
            dma,
            dma,
            dma((VIEWS,)),
            dma((VIEWS,)),
            dma,
            dma,
            dma((SHARE - 1,)),
            dma((SHARE - 1,)),
            dma,
        ],
        compiler_params=pltpu.CompilerParams(
            collective_id=0, has_side_effects=True, vmem_limit_bytes=VMEM_BYTES
        ),
        name="exchange",
    )(
        params,
        cameras,
        send_rows,
        lists,
        counts,
        tile_ids,
        target[0].transpose(1, 0, 2),
    )
    near = pltpu.VMEM((59, 512), f32)
    return pl.pallas_call(
        update,
        out_shape=(whole, whole, whole, jax.ShapeDtypeStruct((1, 2), f32)),
        in_specs=[hbm] * 5,
        out_specs=(vmem,) * 4,
        scratch_shapes=[
            near,
            near,
            near,
            pltpu.VMEM((VIEWS * 40, 128), f32),
            pltpu.VMEM((1, 128), f32),
            pltpu.VMEM((1024, 128), f32),
            pltpu.VMEM((256, 128), f32),
            dma((5,)),
        ],
        compiler_params=some,
        name="update",
    )(params, first_moment, second_moment, grads.reshape(VIEWS * 40, 128), loss)


def solution(mesh):
    in_specs = (
        P(None, "gauss"),
        P(None, "gauss"),
        P(None, "gauss"),
        P("view", None),
        P("view", "gauss", None),
        P("view", "gauss", None),
        P("view", "gauss"),
        P("view", "gauss"),
        P("view", "gauss", None, None),
    )
    out_specs = (P(None, "gauss"), P(None, "gauss"), P(None, "gauss"), P("view", "gauss"))
    return jax.shard_map(body, mesh=mesh, in_specs=in_specs, out_specs=out_specs, check_vma=False)
```

```python
import jax
import jax.numpy as jnp
from jax import lax
from jax.experimental import pallas as pl
from jax.experimental.pallas import tpu as pltpu
from jax.sharding import PartitionSpec as P

focal_length = 1100.0
centre_x = 960.0
centre_y = 540.0
beta_one = 0.9
beta_two = 0.999
adam_eps = 1e-15
adam_step = 100.0
log2_e = 1.4426950408889634
sh_zero = 0.28209479177387814
sh_one = 0.4886025119029199
sh_two = [
    1.0925484305920792,
    -1.0925484305920792,
    0.31539156525252005,
    -1.0925484305920792,
    0.5462742152960396,
]
sh_three = [
    -0.5900435899266435,
    2.890611442640554,
    -0.4570457994644658,
    0.3731763325901154,
    -0.4570457994644658,
    1.445305721320277,
    -0.5900435899266435,
]
LINE = 16
SIDE = 4
CHIPS = LINE * SIDE
SHARE = 4
RENDER = CHIPS // SHARE
VIEWS = 4
VMEM_BYTES = 62 * 1024 * 1024
MESH = pl.DeviceIdType.MESH
f32 = jnp.float32
bf16 = jnp.bfloat16


def harmonics(dir_x, dir_y, dir_z):
    sq_x = dir_x * dir_x
    sq_y = dir_y * dir_y
    sq_z = dir_z * dir_z
    return [
        -sh_one * dir_y,
        sh_one * dir_z,
        -sh_one * dir_x,
        sh_two[0] * dir_x * dir_y,
        sh_two[1] * dir_y * dir_z,
        sh_two[2] * (2.0 * sq_z - sq_x - sq_y),
        sh_two[3] * dir_x * dir_z,
        sh_two[4] * (sq_x - sq_y),
        sh_three[0] * dir_y * (3.0 * sq_x - sq_y),
        sh_three[1] * dir_x * dir_y * dir_z,
        sh_three[2] * dir_y * (4.0 * sq_z - sq_x - sq_y),
        sh_three[3] * dir_z * (2.0 * sq_z - 3.0 * sq_x - 3.0 * sq_y),
        sh_three[4] * dir_x * (4.0 * sq_z - sq_x - sq_y),
        sh_three[5] * dir_z * (sq_x - sq_y),
        sh_three[6] * dir_x * (sq_x - 3.0 * sq_y),
    ]


def project(columns, camera):
    mean_x, mean_y, mean_z = columns[0], columns[1], columns[2]
    scales = [jnp.exp(columns[3 + axis]) for axis in range(3)]
    quat_w, quat_x, quat_y, quat_z = columns[6:10]
    norm = 1.0 / jnp.sqrt(quat_w * quat_w + quat_x * quat_x + quat_y * quat_y + quat_z * quat_z)
    quat_w, quat_x, quat_y, quat_z = quat_w * norm, quat_x * norm, quat_y * norm, quat_z * norm
    turn = [
        [
            1.0 - 2.0 * (quat_y * quat_y + quat_z * quat_z),
            2.0 * (quat_x * quat_y - quat_w * quat_z),
            2.0 * (quat_x * quat_z + quat_w * quat_y),
        ],
        [
            2.0 * (quat_x * quat_y + quat_w * quat_z),
            1.0 - 2.0 * (quat_x * quat_x + quat_z * quat_z),
            2.0 * (quat_y * quat_z - quat_w * quat_x),
        ],
        [
            2.0 * (quat_x * quat_z - quat_w * quat_y),
            2.0 * (quat_y * quat_z + quat_w * quat_x),
            1.0 - 2.0 * (quat_x * quat_x + quat_y * quat_y),
        ],
    ]
    world = [[turn[outer][inner] * scales[inner] for inner in range(3)] for outer in range(3)]
    cam_x, cam_y, depth = [
        camera[3 * outer] * mean_x
        + camera[3 * outer + 1] * mean_y
        + camera[3 * outer + 2] * mean_z
        + camera[9 + outer]
        for outer in range(3)
    ]
    framed = [
        [
            camera[3 * outer] * world[0][inner]
            + camera[3 * outer + 1] * world[1][inner]
            + camera[3 * outer + 2] * world[2][inner]
            for inner in range(3)
        ]
        for outer in range(3)
    ]
    inverse = 1.0 / depth
    near = focal_length * inverse
    slope_x = cam_x * inverse
    slope_y = cam_y * inverse
    row_top = [near * (framed[0][inner] - slope_x * framed[2][inner]) for inner in range(3)]
    row_low = [near * (framed[1][inner] - slope_y * framed[2][inner]) for inner in range(3)]
    cov_a = row_top[0] * row_top[0] + row_top[1] * row_top[1] + row_top[2] * row_top[2] + 0.3
    cov_b = row_top[0] * row_low[0] + row_top[1] * row_low[1] + row_top[2] * row_low[2]
    cov_c = row_low[0] * row_low[0] + row_low[1] * row_low[1] + row_low[2] * row_low[2] + 0.3
    over = 1.0 / (cov_a * cov_c - cov_b * cov_b)
    centre_u = focal_length * slope_x + centre_x
    centre_v = focal_length * slope_y + centre_y
    away = 1.0 / jnp.sqrt(cam_x * cam_x + cam_y * cam_y + depth * depth)
    basis = harmonics(cam_x * away, cam_y * away, depth * away)
    colours = []
    for channel in range(3):
        total = 0.5 + sh_zero * columns[11 + channel]
        for order in range(15):
            total = total + basis[order] * columns[14 + 3 * order + channel]
        colours.append(total)
    opacity = 1.0 / (1.0 + jnp.exp(-columns[10]))
    return [
        centre_u,
        centre_v,
        cov_c * over,
        -cov_b * over,
        cov_a * over,
        opacity,
        colours[0],
        colours[1],
        colours[2],
    ]


def pieces(value):
    high = value.astype(bf16)
    rest = value - high.astype(f32)
    middle = rest.astype(bf16)
    low = (rest - middle.astype(f32)).astype(bf16)
    return high, middle, low


def dot_rows(left, right):
    return lax.dot_general(left, right, (((1,), (1,)), ((), ())), preferred_element_type=f32)


def add_pieces(stacked):
    rows = stacked.shape[0] // 3
    return (stacked[0:rows] + stacked[rows : 2 * rows]) + stacked[2 * rows :]


def dot_exact(left, right):
    stacked = jnp.concatenate(pieces(left), axis=0)
    return add_pieces(jnp.dot(stacked, right, preferred_element_type=f32))


def dot_rows_exact(left, right):
    return add_pieces(dot_rows(jnp.concatenate(pieces(left), axis=0), right))


def iota(shape, axis):
    return lax.broadcasted_iota(jnp.int32, shape, axis)


def one_hot(test):
    return jnp.where(test, 1.0, 0.0).astype(bf16)


def swap(value):
    return pltpu.roll(value, 64, 1)


def reorder_rows(rows, place):
    number, width = rows.shape
    padding = jnp.zeros((8 - 2 * number, width), jnp.int32)
    split_rows = jnp.concatenate([rows >> 4, rows & 15, padding], axis=0)
    chosen = one_hot(iota((width, width), 0) == place(iota((width, width), 1)))
    moved = jnp.dot(split_rows.astype(f32).astype(bf16), chosen, preferred_element_type=f32)
    return moved[0:number] * 16.0 + moved[number : 2 * number]


def sender_table(rows):
    moved = reorder_rows(rows, lambda n: 8 * (n & 63) + (n >> 6))
    return one_hot(iota((512, 512), 0) == moved.astype(jnp.int32))


def pack_messages(attributes, table):
    placed = dot_exact(attributes, table)
    turned = jnp.transpose(jnp.concatenate([placed, jnp.zeros((112, 512), f32)], axis=0))
    lanes = iota((16, 128), 1)
    rows = [jnp.zeros((16, 128), f32)] * 3
    for group in range(8):
        for number in range(SHARE):
            slot = SHARE * group + number
            block = turned[16 * slot : 16 * slot + 16]
            most = jnp.where(lanes < 8, block, 0.0)
            last = jnp.where(lanes == 8, block, 0.0)
            rows[group // 4] = rows[group // 4] + pltpu.roll(most, 8 * (slot % 16), 1)
            rows[2] = rows[2] + pltpu.roll(last, (8 * number + group - 8) % 128, 1)
    return rows


def unpack_messages(messages, table):
    turned = jnp.transpose(jnp.concatenate([messages, jnp.zeros_like(messages)], axis=0))
    keep = iota((16, 128), 1) < 64
    parts = []
    for pair in range(4):
        left = turned[32 * pair : 32 * pair + 16]
        right = turned[32 * pair + 16 : 32 * pair + 32]
        parts.append(jnp.where(keep, left, swap(right)))
    return dot_rows_exact(jnp.concatenate(parts, axis=1), table)


def list_tables(lists):
    slot = jnp.concatenate([lists[0:1], lists[1:2]], axis=1).astype(jnp.int32)
    return one_hot(iota((64, 512), 0) == (slot >> 3)), slot & 7


def turn_received(rows):
    blank = jnp.zeros((64, 128), f32)
    return [jnp.transpose(jnp.concatenate([row, blank], axis=0))[:, 0:64] for row in rows]


def pick(first, second, core, number, table, group):
    most, last = [], []
    for turned in (first, second):
        mine = jnp.where(core == 0, turned[0], turned[1])
        most += [mine[8 * (SHARE * n + number) :][0:8] for n in range(4)]
        ninth = turned[2][8 * number : 8 * number + 8]
        last.append(jnp.where(core == 0, ninth[0:4], ninth[4:8]))
    found = dot_exact(jnp.concatenate(most + last, axis=0), table)
    eight = jnp.where((iota((64, 512), 0) >> 3) == group, found[0:64], 0.0)
    total = eight[0:8]
    for part in range(1, 8):
        total = total + eight[8 * part : 8 * part + 8]
    ninth = jnp.where(iota((8, 512), 0) == group, found[64:72], 0.0)
    return jnp.concatenate([total, jnp.sum(ninth, axis=0, keepdims=True)], axis=0)


def unpick(grads, table, group):
    spread = jnp.concatenate([grads] * 8, axis=0)
    spread = jnp.where((iota((128, 512), 0) >> 4) == group, spread, 0.0)
    turned = dot_rows_exact(spread, table)
    return jnp.transpose(jnp.concatenate([turned, jnp.zeros((128, 64), f32)], axis=1))[0:64]


def place_of(position):
    return 32 * (position & 7) + (position >> 3)


def split(rows):
    return [part.astype(f32) for part in pieces(rows)]


def split(rows):
    return [part.astype(f32) for part in pieces(rows)]


def two_pieces(value):
    high = value.astype(bf16)
    return high, (value - high.astype(f32)).astype(bf16)


def padded(rows):
    number = sum(part.shape[0] for part in rows)
    return jnp.concatenate(rows + [jnp.zeros((32 - number, 256), f32)], axis=0).astype(bf16)


def dot_columns(left, right):
    return lax.dot_general(left, right, (((0,), (0,)), ((), ())), preferred_element_type=f32)


def prepare_tile(attributes, across, down, count):
    centre_u = attributes[0:1] - across
    centre_v = attributes[1:2] - down
    alive = place_of(iota((1, 256), 1)).astype(f32) < count
    by_xx = attributes[2:3] * (-0.5 * log2_e)
    by_xy = attributes[3:4] * (-log2_e)
    by_yy = attributes[4:5] * (-0.5 * log2_e)
    by_x = -2.0 * by_xx * centre_u - by_xy * centre_v
    by_y = -2.0 * by_yy * centre_v - by_xy * centre_u
    whole = (by_xx * centre_u + by_xy * centre_v) * centre_u + (by_yy * centre_v) * centre_v
    whole = jnp.where(alive, whole + jnp.log(attributes[5:6]) * log2_e, -1e30)
    power = jnp.concatenate([whole, by_x, by_y, by_xx, by_xy, by_yy], axis=0)
    return power, centre_u, centre_v


def pixels():
    number = iota((1, 256), 1)
    return (number & 15).astype(f32) - 7.5, (number >> 4).astype(f32) - 7.5


def monomials():
    pixel_x, pixel_y = pixels()
    ones = jnp.ones((1, 256), f32)
    return [ones, pixel_x, pixel_y, pixel_x * pixel_x, pixel_x * pixel_y, pixel_y * pixel_y]


def exponents(power):
    return dot_columns(padded(split(power)), padded(monomials() * 3))


def colour_sums(colour, weight):
    chunk = (iota((8, 256), 1) & 7) == iota((8, 256), 0)
    spread = [jnp.where(chunk, colour[c : c + 1], 0.0) for c in range(3)]
    left = jnp.concatenate(split(jnp.concatenate(spread, axis=0)), axis=0).astype(bf16)
    high, middle = two_pieces(weight)
    total = jnp.dot(left, middle, preferred_element_type=f32)
    total = total + jnp.dot(left, high, preferred_element_type=f32)
    total = add_pieces(total)
    return [total[8 * c : 8 * c + 8] for c in range(3)]


def shades(colour, residual):
    high, middle, low = split(colour)
    left = padded([high, high, high, middle, middle, low])
    high, middle, low = split(jnp.concatenate(residual, axis=0))
    return dot_columns(left, padded([high, middle, low, high, middle, high]))


def between(keep, colour, target):
    before = [jnp.ones((1, 256), f32)]
    for chunk in range(7):
        before.append(before[-1] * keep[chunk : chunk + 1])
    before = jnp.concatenate(before, axis=0)
    colour = [part * before for part in colour]
    residual = [jnp.sum(colour[c], axis=0, keepdims=True) - target[c : c + 1] for c in range(3)]
    own = residual[0] * colour[0] + residual[1] * colour[1] + residual[2] * colour[2]
    after = [jnp.zeros((1, 256), f32)]
    for chunk in range(7, 0, -1):
        after.append(after[-1] + own[chunk : chunk + 1])
    after = jnp.concatenate(after[::-1], axis=0)
    squares = residual[0] * residual[0] + residual[1] * residual[1] + residual[2] * residual[2]
    return before, after, residual, 0.5 * jnp.sum(squares, axis=1, keepdims=True)


def back_step(shade, alpha, weight, before, after, later):
    own = weight * shade
    left = 1.0 - alpha
    guess = pl.reciprocal(left, approx=True)
    ratio = alpha * (guess * (2.0 - left * guess))
    slope = before * own - (before * later + after) * ratio
    return slope, before * weight, later + own


def moments(slope, weight, residual):
    shown = split(jnp.concatenate(residual, axis=0))
    factors = jnp.concatenate(monomials() + shown + [jnp.zeros((1, 256), f32)], axis=0).astype(bf16)

    def over_pixels(value):
        high, middle = two_pieces(value)
        return dot_rows(factors, middle) + dot_rows(factors, high)

    by_power = over_pixels(slope)[0:6]
    by_shown = over_pixels(weight)
    by_shown = by_shown[6:9] + (by_shown[9:12] + by_shown[12:15])
    return jnp.concatenate([by_power, by_shown], axis=0)


def finish_tile(sums, attributes, centre_u, centre_v):
    whole, by_x, by_y, by_xx, by_xy, by_yy = [sums[n : n + 1] for n in range(6)]
    sum_x = by_x - centre_u * whole
    sum_y = by_y - centre_v * whole
    sum_xx = by_xx - centre_u * (by_x + sum_x)
    sum_xy = by_xy - centre_u * by_y - centre_v * sum_x
    sum_yy = by_yy - centre_v * (by_y + sum_y)
    conic = [attributes[2 + n : 3 + n] for n in range(3)]
    rows = [
        conic[0] * sum_x + conic[1] * sum_y,
        conic[1] * sum_x + conic[2] * sum_y,
        -0.5 * sum_xx,
        -sum_xy,
        -0.5 * sum_yy,
        whole,
        sums[6:9],
        jnp.zeros((7, 256), f32),
    ]
    return jnp.concatenate(rows, axis=0)


def exchange(
    params_in,
    camera_in,
    rows_in,
    lists_in,
    counts_in,
    tile_ids_in,
    target_in,
    out,
    loss,
    params,
    camera,
    rows,
    lists,
    counts,
    tile_ids,
    target,
    msg,
    land1,
    land2,
    back2,
    land4,
    facts,
    land_facts,
    aims,
    land_aims,
    own,
    losses,
    away,
    alphas,
    weights,
    shaded,
    table,
    loads,
    send1,
    recv1,
    send2,
    recv2,
    send4,
    recv4,
    send5,
    recv5,
    kept5,
    send6,
    recv6,
    send7,
    recv7,
    send8,
    recv8,
):
    here = lax.axis_index("gauss")
    view = lax.axis_index("view")
    core = lax.rem(here, 2)
    chip = here // 2
    line = chip // SIDE
    side = lax.rem(chip, SIDE)

    other_core = {"gauss": here + 1 - 2 * core, "view": view}

    def over_views(action):
        for step in (2, 1, 3):
            other = lax.rem(view + step, VIEWS)
            action(step, other, {"gauss": here, "view": other})

    barrier = pltpu.get_barrier_semaphore()

    def greet(device):
        pl.semaphore_signal(barrier, inc=1, device_id=device, device_id_type=MESH)

    early = chip < RENDER
    late = jnp.logical_not(early)
    home = {"gauss": lax.rem(chip, RENDER) * 2 + core, "view": view}
    turn = chip // RENDER

    def served(number):
        return {"gauss": lax.rem(chip + number * RENDER, CHIPS) * 2 + core, "view": view}

    def to_renderers(action):
        for step_z in (0, 1, 3, 2):
            for step_x in (2, 1, 3, 0):
                other = lax.rem(line + step_z, 4) * SIDE + lax.rem(side + step_x, SIDE)
                device = {"gauss": other * 2 + core, "view": view}
                pl.when(other != chip)(lambda other=other, device=device: action(other, device))

    def to_all(action):
        def one(number, unused):
            for step_x in (2, 1, 3, 0):
                other = number * SIDE + lax.rem(side + step_x, SIDE)
                device = {"gauss": other * 2 + core, "view": view}
                pl.when(other != chip)(lambda other=other, device=device: action(other, device))
            return unused

        lax.fori_loop(0, LINE, one, 0)

    def to_all_cores(action):
        def one(number, unused):
            for step_x in (2, 1, 3, 0):
                other = number * SIDE + lax.rem(side + step_x, SIDE)
                for which in range(2):
                    device = {"gauss": other * 2 + which, "view": view}
                    place = which * CHIPS + other
                    pl.when(other * 2 + which != here)(
                        lambda place=place, device=device: action(place, device)
                    )
            return unused

        lax.fori_loop(0, LINE, one, 0)

    def greet_late(other, device):
        pl.when(other >= RENDER)(lambda: greet(device))

    @pl.when(early)
    def greet_first():
        to_renderers(lambda other, device: greet(device))
        greet(other_core)

    over_views(lambda step, other, device: greet(device))

    pairs = [
        (rows_in, rows),
        (params_in, params),
        (camera_in, camera),
        (lists_in, lists),
        (counts_in, counts),
        (tile_ids_in, tile_ids),
        (target_in, target),
    ]
    copies = [
        pltpu.make_async_copy(source, place, loads.at[n]) for n, (source, place) in enumerate(pairs)
    ]
    for copy in copies:
        copy.start()

    pl.when(early)(lambda: to_all(greet_late))

    def remote(source, place, sent, arrived, device):
        return pltpu.make_async_remote_copy(
            src_ref=source,
            dst_ref=place,
            send_sem=sent,
            recv_sem=arrived,
            device_id=device,
            device_id_type=MESH,
        )

    def wait_rows(place, count, semaphore):
        whole = place.at[pl.ds(0, count)]
        pltpu.make_async_copy(whole, whole, semaphore).wait()

    def with_other_core(source, place, sent, arrived):
        copy = remote(source, place, sent, arrived, other_core)
        copy.start()
        copy.wait()

    copies[0].wait()
    table[...] = sender_table(rows[0])
    copies[1].wait()
    copies[2].wait()
    scalars = [camera[0, n] for n in range(12)]
    attributes = project([params[n : n + 1, :] for n in range(59)], scalars)
    messages = pack_messages(
        jnp.concatenate(attributes + [jnp.zeros((7, 512), f32)], axis=0), table[...]
    )
    for number in range(3):
        msg[:, number, 0, :] = messages[number]
    for copy in copies[3:]:
        copy.wait()

    facts[0:2, 0, :] = reorder_rows(lists[0], place_of)
    for tile in range(2):
        for channel in range(3):
            aims[3 * tile + channel, 0:1, :] = target[channel, tile : tile + 1, :]
    spots = iota((1, 256), 1)
    known = jnp.zeros((1, 256), f32)
    for tile in range(2):
        tile_id = tile_ids[0, tile]
        across = (16 * lax.rem(tile_id, 120)).astype(f32) + 7.5
        down = (16 * lax.div(tile_id, 120)).astype(f32) + 7.5
        for n, value in enumerate((across, down, counts[0, tile].astype(f32))):
            known = jnp.where(spots == 3 * tile + n, value, known)
    facts[2, 0:1, :] = known

    pl.semaphore_wait(barrier, RENDER + VIEWS - 1)

    def send_attributes(other, device):
        remote(msg.at[other], land1.at[chip], send1, recv1, device).start()

    def send_gradients(other, device):
        mine = land4.at[core * RENDER + chip]
        remote(back2.at[other], mine, send4, recv4, device).start()

    @pl.when(late)
    def send_facts():
        remote(facts, land_facts.at[turn - 1], send6, recv6.at[turn - 1], home).start()

    to_renderers(send_attributes)

    @pl.when(late)
    def late_part():
        aims_copy = remote(aims, land_aims.at[turn - 1], send8, recv8.at[turn - 1], home)
        aims_copy.start()
        remote(facts, land_facts.at[turn - 1], send6, recv6.at[turn - 1], home).wait_send()
        aims_copy.wait_send()
        wait_rows(msg, RENDER, send1)
        remote(away.at[0], losses, send7.at[0], recv7, home).wait_recv()
        wait_rows(land4, 2 * RENDER, recv4)

    @pl.when(early)
    def render():
        land1[chip] = msg[chip]
        tables = [list_tables(facts[0:2, 0, :])]
        for number in range(1, SHARE):
            place = land_facts.at[number - 1]
            remote(facts, place, send6, recv6.at[number - 1], served(number)).wait_recv()
            tables.append(list_tables(land_facts[number - 1, 0:2, 0, :]))
        wait_rows(land1, CHIPS - 1, recv1)
        with_other_core(land1, land2, send2, recv2)

        kept = turn_received([land1[:, n, 0, :] for n in range(3)])
        given = turn_received([land2[:, n, 0, :] for n in range(3)])
        first = [jnp.where(core == 0, a, b) for a, b in zip(kept, given)]
        second = [jnp.where(core == 0, b, a) for a, b in zip(kept, given)]
        tiles = range(2 * SHARE)
        entries, centres = [], []
        for number in range(SHARE):
            found = pick(first, second, core, number, *tables[number])
            known = facts[2] if number == 0 else land_facts[number - 1, 2]
            for part in range(2):
                chosen = found[:, 256 * part : 256 * part + 256]
                about = [known[:, 3 * part + n : 3 * part + n + 1] for n in range(3)]
                power, centre_u, centre_v = prepare_tile(chosen, *about)
                alphas[2 * number + part] = exponents(power)
                entries.append(chosen)
                centres.append((centre_u, centre_v))

        def forward(step, carry):
            rows_here = pl.ds(pl.multiple_of(step * 8, 8), 8)
            left = []
            for tile, keep in zip(tiles, carry):
                alpha = jnp.exp2(alphas[tile, rows_here, :])
                weight = keep * alpha
                alphas[tile, rows_here, :] = alpha
                weights[tile, rows_here, :] = weight
                left.append(keep - weight)
            return left

        keeps = lax.fori_loop(0, 32, forward, [jnp.ones((8, 256), f32) for tile in tiles], unroll=4)
        shown = [aims[0:3, 0, :], aims[3:6, 0, :]]
        for number in range(SHARE - 1):
            place = land_aims.at[number]
            remote(aims, place, send8, recv8.at[number], served(number + 1)).wait_recv()
            shown += [land_aims[number, 0:3, 0, :], land_aims[number, 3:6, 0, :]]
        around = []
        for tile in tiles:
            colour = colour_sums(entries[tile][6:9], weights[tile])
            around.append(between(keeps[tile], colour, shown[tile]))
            shaded[tile] = shades(entries[tile][6:9], around[tile][2])
        spot = iota((1, 128), 1)
        for number in range(SHARE):
            pair = around[2 * number][3], around[2 * number + 1][3]
            row = jnp.where(spot == 0, pair[0], jnp.where(spot == 1, pair[1], 0.0))
            if number == 0:
                losses[...] = row
            else:
                away[number - 1] = row
                place = away.at[number - 1]
                remote(place, losses, send7.at[number - 1], recv7, served(number)).start()

        for first_tile in range(0, 2 * SHARE, 4):
            some = range(first_tile, first_tile + 4)

            def backward(step, later, some=some):
                rows_here = pl.ds(pl.multiple_of((31 - step) * 8, 8), 8)
                left = []
                for tile, behind in zip(some, later):
                    before, after = around[tile][0:2]
                    slope, weight, rest = back_step(
                        shaded[tile, rows_here, :],
                        alphas[tile, rows_here, :],
                        weights[tile, rows_here, :],
                        before,
                        after,
                        behind,
                    )
                    alphas[tile, rows_here, :] = slope
                    weights[tile, rows_here, :] = weight
                    left.append(rest)
                return left

            lax.fori_loop(0, 32, backward, [jnp.zeros((8, 256), f32)] * 4, unroll=8)
        back = []
        for number in range(SHARE):
            grads = []
            for tile in (2 * number, 2 * number + 1):
                sums = moments(alphas[tile], weights[tile], around[tile][2])
                grads.append(finish_tile(sums, entries[tile], *centres[tile]))
            back.append(unpick(jnp.concatenate(grads, axis=1), *tables[number]))

        low_lanes = iota((CHIPS, 128), 1) < 64
        for pair in range(2):
            one, two = back[2 * pair], back[2 * pair + 1]
            back2[0:CHIPS, pair, :] = jnp.where(low_lanes, one, swap(two))
            back2[CHIPS:, pair, :] = jnp.where(low_lanes, swap(one), two)
        to_all_cores(send_gradients)
        land4[core * RENDER + chip] = back2[core * CHIPS + chip]
        for number in range(1, SHARE):
            place = away.at[number - 1]
            remote(place, losses, send7.at[number - 1], recv7, served(number)).wait_send()
        wait_rows(msg, RENDER - 1, send1)
        wait_rows(land4, 2 * RENDER - 1, recv4)

    loss_copy = pltpu.make_async_copy(losses, loss, loads.at[7])
    loss_copy.start()
    low_rows = iota((RENDER, 128), 1) < 64
    messages = []
    for pair in range(2):
        zero, one = land4[0:RENDER, pair, :], land4[RENDER:, pair, :]
        messages.append(jnp.where(low_rows, zero, swap(one)))
        messages.append(jnp.where(low_rows, swap(zero), one))
    returned = unpack_messages(jnp.concatenate(messages, axis=0), table[...])

    lanes = iota((1, 128), 1)
    pose = jnp.zeros((1, 128), f32)
    for n in range(12):
        pose = jnp.where(lanes == n, scalars[n], pose)
    for part in range(4):
        own[10 * part : 10 * part + 9, :] = returned[0:9, 128 * part : 128 * part + 128]
        own[10 * part + 9 : 10 * part + 10, :] = pose

    def share(step, other, device):
        remote(own, out.at[view], send5.at[step], recv5.at[view], device).start()

    def take(step, other, device):
        remote(own, out.at[other], send5.at[step], recv5.at[other], device).wait()

    over_views(share)
    keep = pltpu.make_async_copy(own, out.at[view], kept5)
    keep.start()
    pl.when(early)(lambda: wait_rows(back2, 2 * CHIPS - 1, send4))
    loss_copy.wait()
    keep.wait()
    over_views(take)


def update(
    params_in,
    first_in,
    second_in,
    grads_in,
    loss_in,
    new_params,
    new_first,
    new_second,
    tile_loss,
    params,
    first,
    second,
    grads,
    loss,
    spread,
    total,
    loads,
):
    pairs = [
        (params_in, params),
        (grads_in, grads),
        (first_in, first),
        (second_in, second),
        (loss_in, loss),
    ]
    copies = [
        pltpu.make_async_copy(source, place, loads.at[n]) for n, (source, place) in enumerate(pairs)
    ]
    for copy in copies:
        copy.start()
    copies[0].wait()

    for part in range(4):
        block = params[:, 128 * part : 128 * part + 128]
        for view in range(VIEWS):
            start = 64 * (4 * view + part)
            spread[start : start + 59, :] = block
    columns = [spread[pl.ds(n, 16, stride=64), :] for n in range(59)]
    copies[1].wait()
    given = [grads[pl.ds(n, 16, stride=10), :] for n in range(10)]
    camera = [given[9][:, n : n + 1] for n in range(12)]

    def shown(rows):
        attributes = project(rows, camera)
        return attributes[0:5] + attributes[6:9]

    pulled = jax.vjp(shown, columns)[1](given[0:5] + given[6:9])[0]
    pulled[10] = given[5] * (1.0 - 1.0 / (1.0 + jnp.exp(-columns[10])))
    for n in range(59):
        both = pulled[n][0:8] + pulled[n][8:16]
        total[pl.ds(n, 4, stride=64), :] = both[0:4] + both[4:8]
    for copy in copies[2:]:
        copy.wait()
    row = iota((59, 1), 0)
    rate = jnp.where(row < 3, 0.00016, 0.005)
    rate = jnp.where(row < 6, rate, 0.001)
    rate = jnp.where(row < 10, rate, 0.05)
    rate = jnp.where(row < 11, rate, 0.0025)
    rate = jnp.where(row < 14, rate, 0.000125)
    rate = rate / (1.0 - beta_one**adam_step)
    for part in range(4):
        here = slice(128 * part, 128 * part + 128)
        slope = total[64 * part : 64 * part + 59, :]
        moved = beta_one * first[:, here] + (1.0 - beta_one) * slope
        square = beta_two * second[:, here] + (1.0 - beta_two) * slope * slope
        new_first[:, here] = moved
        new_second[:, here] = square
        new_params[:, here] = params[:, here] - rate * moved / (
            jnp.sqrt(square / (1.0 - beta_two**adam_step)) + adam_eps
        )
    tile_loss[...] = loss[:, 0:2]


def body(params, first_moment, second_moment, cameras, send_rows, lists, counts, tile_ids, target):
    vmem = pl.BlockSpec(memory_space=pltpu.VMEM)
    hbm = pl.BlockSpec(memory_space=pltpu.HBM)
    dma = pltpu.SemaphoreType.DMA
    whole = jax.ShapeDtypeStruct((59, 512), f32)
    some = pltpu.CompilerParams(vmem_limit_bytes=VMEM_BYTES)
    grads, loss = pl.pallas_call(
        exchange,
        out_shape=(
            jax.ShapeDtypeStruct((VIEWS, 40, 128), f32),
            jax.ShapeDtypeStruct((1, 128), f32),
        ),
        in_specs=[hbm] * 7,
        out_specs=(hbm,) * 2,
        scratch_shapes=[
            pltpu.VMEM((59, 512), f32),
            pltpu.SMEM((1, 12), f32),
            pltpu.VMEM((1, 1, 512), jnp.int32),
            pltpu.VMEM((1, 2, 256), jnp.int32),
            pltpu.SMEM((1, 2), jnp.int32),
            pltpu.SMEM((1, 2), jnp.int32),
            pltpu.VMEM((3, 2, 256), f32),
            pltpu.VMEM((RENDER, 3, 1, 128), f32),
            pltpu.VMEM((CHIPS, 3, 1, 128), f32),
            pltpu.VMEM((CHIPS, 3, 1, 128), f32),
            pltpu.VMEM((2 * CHIPS, 2, 128), f32),
            pltpu.VMEM((2 * RENDER, 2, 128), f32),
            pltpu.VMEM((3, 1, 256), f32),
            pltpu.VMEM((SHARE - 1, 3, 1, 256), f32),
            pltpu.VMEM((6, 1, 256), f32),
            pltpu.VMEM((SHARE - 1, 6, 1, 256), f32),
            pltpu.VMEM((40, 128), f32),
            pltpu.VMEM((1, 128), f32),
            pltpu.VMEM((SHARE - 1, 1, 128), f32),
            pltpu.VMEM((2 * SHARE, 256, 256), f32),
            pltpu.VMEM((2 * SHARE, 256, 256), f32),
            pltpu.VMEM((2 * SHARE, 256, 256), f32),
            pltpu.VMEM((512, 512), bf16),
            dma((8,)),
            dma,
            dma,
            dma,
            dma,
            dma,
            dma,
            dma((VIEWS,)),
            dma((VIEWS,)),
            dma,
            dma,
            dma((SHARE - 1,)),
            dma((SHARE - 1,)),
            dma,
            dma,
            dma((SHARE - 1,)),
        ],
        compiler_params=pltpu.CompilerParams(
            collective_id=0, has_side_effects=True, vmem_limit_bytes=VMEM_BYTES
        ),
        name="exchange",
    )(
        params,
        cameras,
        send_rows,
        lists,
        counts,
        tile_ids,
        target[0].transpose(1, 0, 2),
    )
    near = pltpu.VMEM((59, 512), f32)
    return pl.pallas_call(
        update,
        out_shape=(whole, whole, whole, jax.ShapeDtypeStruct((1, 2), f32)),
        in_specs=[hbm] * 5,
        out_specs=(vmem,) * 4,
        scratch_shapes=[
            near,
            near,
            near,
            pltpu.VMEM((VIEWS * 40, 128), f32),
            pltpu.VMEM((1, 128), f32),
            pltpu.VMEM((1024, 128), f32),
            pltpu.VMEM((256, 128), f32),
            dma((5,)),
        ],
        compiler_params=some,
        name="update",
    )(params, first_moment, second_moment, grads.reshape(VIEWS * 40, 128), loss)


def solution(mesh):
    in_specs = (
        P(None, "gauss"),
        P(None, "gauss"),
        P(None, "gauss"),
        P("view", None),
        P("view", "gauss", None),
        P("view", "gauss", None),
        P("view", "gauss"),
        P("view", "gauss"),
        P("view", "gauss", None, None),
    )
    out_specs = (P(None, "gauss"), P(None, "gauss"), P(None, "gauss"), P("view", "gauss"))
    return jax.shard_map(body, mesh=mesh, in_specs=in_specs, out_specs=out_specs, check_vma=False)
```

```python
import jax
import jax.numpy as jnp
from jax import lax
from jax.experimental import pallas as pl
from jax.experimental.pallas import tpu as pltpu
from jax.sharding import PartitionSpec as P

focal_length = 1100.0
centre_x = 960.0
centre_y = 540.0
beta_one = 0.9
beta_two = 0.999
adam_eps = 1e-15
adam_step = 100.0
log2_e = 1.4426950408889634
sh_zero = 0.28209479177387814
sh_one = 0.4886025119029199
sh_two = [
    1.0925484305920792,
    -1.0925484305920792,
    0.31539156525252005,
    -1.0925484305920792,
    0.5462742152960396,
]
sh_three = [
    -0.5900435899266435,
    2.890611442640554,
    -0.4570457994644658,
    0.3731763325901154,
    -0.4570457994644658,
    1.445305721320277,
    -0.5900435899266435,
]
LINE = 16
SIDE = 4
CHIPS = LINE * SIDE
SHARE = 4
RENDER = CHIPS // SHARE
VIEWS = 4
VMEM_BYTES = 62 * 1024 * 1024
MESH = pl.DeviceIdType.MESH
f32 = jnp.float32
bf16 = jnp.bfloat16


def harmonics(dir_x, dir_y, dir_z):
    sq_x = dir_x * dir_x
    sq_y = dir_y * dir_y
    sq_z = dir_z * dir_z
    return [
        -sh_one * dir_y,
        sh_one * dir_z,
        -sh_one * dir_x,
        sh_two[0] * dir_x * dir_y,
        sh_two[1] * dir_y * dir_z,
        sh_two[2] * (2.0 * sq_z - sq_x - sq_y),
        sh_two[3] * dir_x * dir_z,
        sh_two[4] * (sq_x - sq_y),
        sh_three[0] * dir_y * (3.0 * sq_x - sq_y),
        sh_three[1] * dir_x * dir_y * dir_z,
        sh_three[2] * dir_y * (4.0 * sq_z - sq_x - sq_y),
        sh_three[3] * dir_z * (2.0 * sq_z - 3.0 * sq_x - 3.0 * sq_y),
        sh_three[4] * dir_x * (4.0 * sq_z - sq_x - sq_y),
        sh_three[5] * dir_z * (sq_x - sq_y),
        sh_three[6] * dir_x * (sq_x - 3.0 * sq_y),
    ]


def project(columns, camera):
    mean_x, mean_y, mean_z = columns[0], columns[1], columns[2]
    scales = [jnp.exp(columns[3 + axis]) for axis in range(3)]
    quat_w, quat_x, quat_y, quat_z = columns[6:10]
    norm = 1.0 / jnp.sqrt(quat_w * quat_w + quat_x * quat_x + quat_y * quat_y + quat_z * quat_z)
    quat_w, quat_x, quat_y, quat_z = quat_w * norm, quat_x * norm, quat_y * norm, quat_z * norm
    turn = [
        [
            1.0 - 2.0 * (quat_y * quat_y + quat_z * quat_z),
            2.0 * (quat_x * quat_y - quat_w * quat_z),
            2.0 * (quat_x * quat_z + quat_w * quat_y),
        ],
        [
            2.0 * (quat_x * quat_y + quat_w * quat_z),
            1.0 - 2.0 * (quat_x * quat_x + quat_z * quat_z),
            2.0 * (quat_y * quat_z - quat_w * quat_x),
        ],
        [
            2.0 * (quat_x * quat_z - quat_w * quat_y),
            2.0 * (quat_y * quat_z + quat_w * quat_x),
            1.0 - 2.0 * (quat_x * quat_x + quat_y * quat_y),
        ],
    ]
    world = [[turn[outer][inner] * scales[inner] for inner in range(3)] for outer in range(3)]
    cam_x, cam_y, depth = [
        camera[3 * outer] * mean_x
        + camera[3 * outer + 1] * mean_y
        + camera[3 * outer + 2] * mean_z
        + camera[9 + outer]
        for outer in range(3)
    ]
    framed = [
        [
            camera[3 * outer] * world[0][inner]
            + camera[3 * outer + 1] * world[1][inner]
            + camera[3 * outer + 2] * world[2][inner]
            for inner in range(3)
        ]
        for outer in range(3)
    ]
    inverse = 1.0 / depth
    near = focal_length * inverse
    slope_x = cam_x * inverse
    slope_y = cam_y * inverse
    row_top = [near * (framed[0][inner] - slope_x * framed[2][inner]) for inner in range(3)]
    row_low = [near * (framed[1][inner] - slope_y * framed[2][inner]) for inner in range(3)]
    cov_a = row_top[0] * row_top[0] + row_top[1] * row_top[1] + row_top[2] * row_top[2] + 0.3
    cov_b = row_top[0] * row_low[0] + row_top[1] * row_low[1] + row_top[2] * row_low[2]
    cov_c = row_low[0] * row_low[0] + row_low[1] * row_low[1] + row_low[2] * row_low[2] + 0.3
    over = 1.0 / (cov_a * cov_c - cov_b * cov_b)
    centre_u = focal_length * slope_x + centre_x
    centre_v = focal_length * slope_y + centre_y
    away = 1.0 / jnp.sqrt(cam_x * cam_x + cam_y * cam_y + depth * depth)
    basis = harmonics(cam_x * away, cam_y * away, depth * away)
    colours = []
    for channel in range(3):
        total = 0.5 + sh_zero * columns[11 + channel]
        for order in range(15):
            total = total + basis[order] * columns[14 + 3 * order + channel]
        colours.append(total)
    opacity = 1.0 / (1.0 + jnp.exp(-columns[10]))
    return [
        centre_u,
        centre_v,
        cov_c * over,
        -cov_b * over,
        cov_a * over,
        opacity,
        colours[0],
        colours[1],
        colours[2],
    ]


def pieces(value):
    high = value.astype(bf16)
    rest = value - high.astype(f32)
    middle = rest.astype(bf16)
    low = (rest - middle.astype(f32)).astype(bf16)
    return high, middle, low


def dot_rows(left, right):
    return lax.dot_general(left, right, (((1,), (1,)), ((), ())), preferred_element_type=f32)


def add_pieces(stacked):
    rows = stacked.shape[0] // 3
    return (stacked[0:rows] + stacked[rows : 2 * rows]) + stacked[2 * rows :]


def dot_exact(left, right):
    stacked = jnp.concatenate(pieces(left), axis=0)
    return add_pieces(jnp.dot(stacked, right, preferred_element_type=f32))


def dot_rows_exact(left, right):
    return add_pieces(dot_rows(jnp.concatenate(pieces(left), axis=0), right))


def iota(shape, axis):
    return lax.broadcasted_iota(jnp.int32, shape, axis)


def one_hot(test):
    return jnp.where(test, 1.0, 0.0).astype(bf16)


def swap(value):
    return pltpu.roll(value, 64, 1)


def reorder_rows(rows, place):
    number, width = rows.shape
    padding = jnp.zeros((8 - 2 * number, width), jnp.int32)
    split_rows = jnp.concatenate([rows >> 4, rows & 15, padding], axis=0)
    chosen = one_hot(iota((width, width), 0) == place(iota((width, width), 1)))
    moved = jnp.dot(split_rows.astype(f32).astype(bf16), chosen, preferred_element_type=f32)
    return moved[0:number] * 16.0 + moved[number : 2 * number]


def sender_table(rows):
    moved = reorder_rows(rows, lambda n: 8 * (n & 63) + (n >> 6))
    return one_hot(iota((512, 512), 0) == moved.astype(jnp.int32))


def pack_messages(attributes, table):
    placed = dot_exact(attributes, table)
    turned = jnp.transpose(jnp.concatenate([placed, jnp.zeros((112, 512), f32)], axis=0))
    lanes = iota((16, 128), 1)
    rows = [jnp.zeros((16, 128), f32)] * 3
    for group in range(8):
        for number in range(SHARE):
            slot = SHARE * group + number
            block = turned[16 * slot : 16 * slot + 16]
            most = jnp.where(lanes < 8, block, 0.0)
            last = jnp.where(lanes == 8, block, 0.0)
            rows[group // 4] = rows[group // 4] + pltpu.roll(most, 8 * (slot % 16), 1)
            rows[2] = rows[2] + pltpu.roll(last, (8 * number + group - 8) % 128, 1)
    return rows


def unpack_messages(messages, table):
    turned = jnp.transpose(jnp.concatenate([messages, jnp.zeros_like(messages)], axis=0))
    keep = iota((16, 128), 1) < 64
    parts = []
    for pair in range(4):
        left = turned[32 * pair : 32 * pair + 16]
        right = turned[32 * pair + 16 : 32 * pair + 32]
        parts.append(jnp.where(keep, left, swap(right)))
    return dot_rows_exact(jnp.concatenate(parts, axis=1), table)


def list_tables(lists):
    slot = jnp.concatenate([lists[0:1], lists[1:2]], axis=1).astype(jnp.int32)
    return one_hot(iota((64, 512), 0) == (slot >> 3)), slot & 7


def turn_received(rows):
    blank = jnp.zeros((64, 128), f32)
    return [jnp.transpose(jnp.concatenate([row, blank], axis=0))[:, 0:64] for row in rows]


def pick(turned, sender, core, number, table, group):
    mine = jnp.where(core == 0, turned[0], turned[1])
    rows = [mine[8 * (SHARE * n + number) :][0:8] for n in range(4)]
    ninth = turned[2][8 * number : 8 * number + 8]
    rows.append(jnp.where(core == 0, ninth, pltpu.roll(ninth, 4, 0)))
    found = dot_exact(jnp.concatenate(rows, axis=0), table)
    place = group - 4 * sender
    total = jnp.where(place == 0, found[0:8], 0.0)
    for part in range(1, 4):
        total = total + jnp.where(place == part, found[8 * part : 8 * part + 8], 0.0)
    last = jnp.where(iota((4, 512), 0) == place, found[32:36], 0.0)
    return jnp.concatenate([total, jnp.sum(last, axis=0, keepdims=True)], axis=0)


def unpick(grads, table, group):
    spread = jnp.concatenate([grads] * 8, axis=0)
    spread = jnp.where((iota((128, 512), 0) >> 4) == group, spread, 0.0)
    turned = dot_rows_exact(spread, table)
    return jnp.transpose(jnp.concatenate([turned, jnp.zeros((128, 64), f32)], axis=1))[0:64]


def place_of(position):
    return 32 * (position & 7) + (position >> 3)


def split(rows):
    return [part.astype(f32) for part in pieces(rows)]


def split(rows):
    return [part.astype(f32) for part in pieces(rows)]


def two_pieces(value):
    high = value.astype(bf16)
    return high, (value - high.astype(f32)).astype(bf16)


def padded(rows):
    number = sum(part.shape[0] for part in rows)
    return jnp.concatenate(rows + [jnp.zeros((32 - number, 256), f32)], axis=0).astype(bf16)


def dot_columns(left, right):
    return lax.dot_general(left, right, (((0,), (0,)), ((), ())), preferred_element_type=f32)


def prepare_tile(attributes, across, down, count):
    centre_u = attributes[0:1] - across
    centre_v = attributes[1:2] - down
    alive = place_of(iota((1, 256), 1)).astype(f32) < count
    by_xx = attributes[2:3] * (-0.5 * log2_e)
    by_xy = attributes[3:4] * (-log2_e)
    by_yy = attributes[4:5] * (-0.5 * log2_e)
    by_x = -2.0 * by_xx * centre_u - by_xy * centre_v
    by_y = -2.0 * by_yy * centre_v - by_xy * centre_u
    whole = (by_xx * centre_u + by_xy * centre_v) * centre_u + (by_yy * centre_v) * centre_v
    whole = jnp.where(alive, whole + jnp.log(attributes[5:6]) * log2_e, -1e30)
    power = jnp.concatenate([whole, by_x, by_y, by_xx, by_xy, by_yy], axis=0)
    return power, centre_u, centre_v


def pixels():
    number = iota((1, 256), 1)
    return (number & 15).astype(f32) - 7.5, (number >> 4).astype(f32) - 7.5


def monomials():
    pixel_x, pixel_y = pixels()
    ones = jnp.ones((1, 256), f32)
    return [ones, pixel_x, pixel_y, pixel_x * pixel_x, pixel_x * pixel_y, pixel_y * pixel_y]


def exponents(power):
    return dot_columns(padded(split(power)), padded(monomials() * 3))


def colour_sums(colour, weight):
    chunk = (iota((8, 256), 1) & 7) == iota((8, 256), 0)
    spread = [jnp.where(chunk, colour[c : c + 1], 0.0) for c in range(3)]
    left = jnp.concatenate(split(jnp.concatenate(spread, axis=0)), axis=0).astype(bf16)
    high, middle = two_pieces(weight)
    total = jnp.dot(left, middle, preferred_element_type=f32)
    total = total + jnp.dot(left, high, preferred_element_type=f32)
    total = add_pieces(total)
    return [total[8 * c : 8 * c + 8] for c in range(3)]


def shades(colour, residual):
    high, middle, low = split(colour)
    left = padded([high, high, high, middle, middle, low])
    high, middle, low = split(jnp.concatenate(residual, axis=0))
    return dot_columns(left, padded([high, middle, low, high, middle, high]))


def between(keep, colour, target):
    before = [jnp.ones((1, 256), f32)]
    for chunk in range(7):
        before.append(before[-1] * keep[chunk : chunk + 1])
    before = jnp.concatenate(before, axis=0)
    colour = [part * before for part in colour]
    residual = [jnp.sum(colour[c], axis=0, keepdims=True) - target[c : c + 1] for c in range(3)]
    own = residual[0] * colour[0] + residual[1] * colour[1] + residual[2] * colour[2]
    after = [jnp.zeros((1, 256), f32)]
    for chunk in range(7, 0, -1):
        after.append(after[-1] + own[chunk : chunk + 1])
    after = jnp.concatenate(after[::-1], axis=0)
    squares = residual[0] * residual[0] + residual[1] * residual[1] + residual[2] * residual[2]
    return before, after, residual, 0.5 * jnp.sum(squares, axis=1, keepdims=True)


def back_step(shade, alpha, weight, before, after, later):
    own = weight * shade
    left = 1.0 - alpha
    guess = pl.reciprocal(left, approx=True)
    ratio = alpha * (guess * (2.0 - left * guess))
    slope = before * own - (before * later + after) * ratio
    return slope, before * weight, later + own


def moments(slope, weight, residual):
    shown = split(jnp.concatenate(residual, axis=0))
    factors = jnp.concatenate(monomials() + shown + [jnp.zeros((1, 256), f32)], axis=0).astype(bf16)

    def over_pixels(value):
        high, middle = two_pieces(value)
        return dot_rows(factors, middle) + dot_rows(factors, high)

    by_power = over_pixels(slope)[0:6]
    by_shown = over_pixels(weight)
    by_shown = by_shown[6:9] + (by_shown[9:12] + by_shown[12:15])
    return jnp.concatenate([by_power, by_shown], axis=0)


def finish_tile(sums, attributes, centre_u, centre_v):
    whole, by_x, by_y, by_xx, by_xy, by_yy = [sums[n : n + 1] for n in range(6)]
    sum_x = by_x - centre_u * whole
    sum_y = by_y - centre_v * whole
    sum_xx = by_xx - centre_u * (by_x + sum_x)
    sum_xy = by_xy - centre_u * by_y - centre_v * sum_x
    sum_yy = by_yy - centre_v * (by_y + sum_y)
    conic = [attributes[2 + n : 3 + n] for n in range(3)]
    rows = [
        conic[0] * sum_x + conic[1] * sum_y,
        conic[1] * sum_x + conic[2] * sum_y,
        -0.5 * sum_xx,
        -sum_xy,
        -0.5 * sum_yy,
        whole,
        sums[6:9],
        jnp.zeros((7, 256), f32),
    ]
    return jnp.concatenate(rows, axis=0)


def exchange(
    params_in,
    camera_in,
    rows_in,
    lists_in,
    counts_in,
    tile_ids_in,
    target_in,
    out,
    loss,
    params,
    camera,
    rows,
    lists,
    counts,
    tile_ids,
    target,
    msg,
    land1,
    land2,
    halves,
    back2,
    land4,
    facts,
    land_facts,
    aims,
    land_aims,
    own,
    losses,
    away,
    alphas,
    weights,
    shaded,
    table,
    loads,
    send1,
    recv1,
    send2,
    recv2,
    send4,
    recv4,
    send5,
    recv5,
    kept5,
    send6,
    recv6,
    send7,
    recv7,
    send8,
    recv8,
):
    here = lax.axis_index("gauss")
    view = lax.axis_index("view")
    core = lax.rem(here, 2)
    chip = here // 2
    line = chip // SIDE
    side = lax.rem(chip, SIDE)

    other_core = {"gauss": here + 1 - 2 * core, "view": view}

    def over_views(action):
        for step in (2, 1, 3):
            other = lax.rem(view + step, VIEWS)
            action(step, other, {"gauss": here, "view": other})

    barrier = pltpu.get_barrier_semaphore()

    def greet(device):
        pl.semaphore_signal(barrier, inc=1, device_id=device, device_id_type=MESH)

    early = chip < RENDER
    late = jnp.logical_not(early)
    home = {"gauss": lax.rem(chip, RENDER) * 2 + core, "view": view}
    turn = chip // RENDER

    def served(number):
        return {"gauss": lax.rem(chip + number * RENDER, CHIPS) * 2 + core, "view": view}

    def to_renderers(action):
        for step_z in (0, 1, 3, 2):
            for step_x in (2, 1, 3, 0):
                other = lax.rem(line + step_z, 4) * SIDE + lax.rem(side + step_x, SIDE)
                device = {"gauss": other * 2 + core, "view": view}
                pl.when(other != chip)(lambda other=other, device=device: action(other, device))

    def to_all(action):
        def one(number, unused):
            for step_x in (2, 1, 3, 0):
                other = number * SIDE + lax.rem(side + step_x, SIDE)
                device = {"gauss": other * 2 + core, "view": view}
                pl.when(other != chip)(lambda other=other, device=device: action(other, device))
            return unused

        lax.fori_loop(0, LINE, one, 0)

    def to_all_cores(action):
        def one(number, unused):
            for step_x in (2, 1, 3, 0):
                other = number * SIDE + lax.rem(side + step_x, SIDE)
                for which in range(2):
                    device = {"gauss": other * 2 + which, "view": view}
                    place = which * CHIPS + other
                    pl.when(other * 2 + which != here)(
                        lambda place=place, device=device: action(place, device)
                    )
            return unused

        lax.fori_loop(0, LINE, one, 0)

    def greet_late(other, device):
        pl.when(other >= RENDER)(lambda: greet(device))

    @pl.when(early)
    def greet_first():
        to_renderers(lambda other, device: greet(device))
        greet(other_core)

    over_views(lambda step, other, device: greet(device))

    pairs = [
        (rows_in, rows),
        (params_in, params),
        (camera_in, camera),
        (lists_in, lists),
        (counts_in, counts),
        (tile_ids_in, tile_ids),
        (target_in, target),
    ]
    copies = [
        pltpu.make_async_copy(source, place, loads.at[n]) for n, (source, place) in enumerate(pairs)
    ]
    for copy in copies:
        copy.start()

    pl.when(early)(lambda: to_all(greet_late))

    def remote(source, place, sent, arrived, device):
        return pltpu.make_async_remote_copy(
            src_ref=source,
            dst_ref=place,
            send_sem=sent,
            recv_sem=arrived,
            device_id=device,
            device_id_type=MESH,
        )

    def wait_rows(place, count, semaphore):
        whole = place.at[pl.ds(0, count)]
        pltpu.make_async_copy(whole, whole, semaphore).wait()

    copies[0].wait()
    table[...] = sender_table(rows[0])
    copies[1].wait()
    copies[2].wait()
    scalars = [camera[0, n] for n in range(12)]
    attributes = project([params[n : n + 1, :] for n in range(59)], scalars)
    messages = pack_messages(
        jnp.concatenate(attributes + [jnp.zeros((7, 512), f32)], axis=0), table[...]
    )
    for number in range(3):
        msg[:, number, 0, :] = messages[number]
    pl.semaphore_wait(barrier, RENDER + VIEWS - 1)

    def send_attributes(other, device):
        remote(msg.at[other], land1.at[chip], send1, recv1, device).start()

    def send_gradients(other, device):
        mine = land4.at[core * RENDER + chip]
        remote(back2.at[other], mine, send4, recv4, device).start()

    to_renderers(send_attributes)

    for copy in copies[3:]:
        copy.wait()

    facts[0:2, 0, :] = reorder_rows(lists[0], place_of)
    for tile in range(2):
        for channel in range(3):
            aims[3 * tile + channel, 0:1, :] = target[channel, tile : tile + 1, :]
    spots = iota((1, 256), 1)
    known = jnp.zeros((1, 256), f32)
    for tile in range(2):
        tile_id = tile_ids[0, tile]
        across = (16 * lax.rem(tile_id, 120)).astype(f32) + 7.5
        down = (16 * lax.div(tile_id, 120)).astype(f32) + 7.5
        for n, value in enumerate((across, down, counts[0, tile].astype(f32))):
            known = jnp.where(spots == 3 * tile + n, value, known)
    facts[2, 0:1, :] = known

    @pl.when(late)
    def send_facts():
        remote(facts, land_facts.at[turn - 1], send6, recv6.at[turn - 1], home).start()

    @pl.when(late)
    def late_part():
        aims_copy = remote(aims, land_aims.at[turn - 1], send8, recv8.at[turn - 1], home)
        aims_copy.start()
        remote(facts, land_facts.at[turn - 1], send6, recv6.at[turn - 1], home).wait_send()
        aims_copy.wait_send()
        wait_rows(msg, RENDER, send1)
        remote(away.at[0], losses, send7.at[0], recv7, home).wait_recv()
        wait_rows(land4, 2 * RENDER, recv4)

    @pl.when(early)
    def render():
        land1[chip] = msg[chip]
        tables = [list_tables(facts[0:2, 0, :])]
        for number in range(1, SHARE):
            place = land_facts.at[number - 1]
            remote(facts, place, send6, recv6.at[number - 1], served(number)).wait_recv()
            tables.append(list_tables(land_facts[number - 1, 0:2, 0, :]))
        wait_rows(land1, CHIPS - 1, recv1)
        core_copy = remote(land1, land2, send2, recv2, other_core)
        core_copy.start()
        kept = turn_received([land1[:, n, 0, :] for n in range(3)])
        for number in range(SHARE):
            halves[number] = pick(kept, core, core, number, *tables[number])
        core_copy.wait()

        given = turn_received([land2[:, n, 0, :] for n in range(3)])
        tiles = range(2 * SHARE)
        entries, centres = [], []
        for number in range(SHARE):
            found = halves[number] + pick(given, 1 - core, core, number, *tables[number])
            known = facts[2] if number == 0 else land_facts[number - 1, 2]
            for part in range(2):
                chosen = found[:, 256 * part : 256 * part + 256]
                about = [known[:, 3 * part + n : 3 * part + n + 1] for n in range(3)]
                power, centre_u, centre_v = prepare_tile(chosen, *about)
                alphas[2 * number + part] = exponents(power)
                entries.append(chosen)
                centres.append((centre_u, centre_v))

        def forward(step, carry):
            rows_here = pl.ds(pl.multiple_of(step * 8, 8), 8)
            left = []
            for tile, keep in zip(tiles, carry):
                alpha = jnp.exp2(alphas[tile, rows_here, :])
                weight = keep * alpha
                alphas[tile, rows_here, :] = alpha
                weights[tile, rows_here, :] = weight
                left.append(keep - weight)
            return left

        keeps = lax.fori_loop(0, 32, forward, [jnp.ones((8, 256), f32) for tile in tiles], unroll=4)
        shown = [aims[0:3, 0, :], aims[3:6, 0, :]]
        for number in range(SHARE - 1):
            place = land_aims.at[number]
            remote(aims, place, send8, recv8.at[number], served(number + 1)).wait_recv()
            shown += [land_aims[number, 0:3, 0, :], land_aims[number, 3:6, 0, :]]
        around = []
        for tile in tiles:
            colour = colour_sums(entries[tile][6:9], weights[tile])
            around.append(between(keeps[tile], colour, shown[tile]))
            shaded[tile] = shades(entries[tile][6:9], around[tile][2])
        spot = iota((1, 128), 1)
        for number in range(SHARE):
            pair = around[2 * number][3], around[2 * number + 1][3]
            row = jnp.where(spot == 0, pair[0], jnp.where(spot == 1, pair[1], 0.0))
            if number == 0:
                losses[...] = row
            else:
                away[number - 1] = row
                place = away.at[number - 1]
                remote(place, losses, send7.at[number - 1], recv7, served(number)).start()

        for first_tile in range(0, 2 * SHARE, 4):
            some = range(first_tile, first_tile + 4)

            def backward(step, later, some=some):
                rows_here = pl.ds(pl.multiple_of((31 - step) * 8, 8), 8)
                left = []
                for tile, behind in zip(some, later):
                    before, after = around[tile][0:2]
                    slope, weight, rest = back_step(
                        shaded[tile, rows_here, :],
                        alphas[tile, rows_here, :],
                        weights[tile, rows_here, :],
                        before,
                        after,
                        behind,
                    )
                    alphas[tile, rows_here, :] = slope
                    weights[tile, rows_here, :] = weight
                    left.append(rest)
                return left

            lax.fori_loop(0, 32, backward, [jnp.zeros((8, 256), f32)] * 4, unroll=8)
        back = []
        for number in range(SHARE):
            grads = []
            for tile in (2 * number, 2 * number + 1):
                sums = moments(alphas[tile], weights[tile], around[tile][2])
                grads.append(finish_tile(sums, entries[tile], *centres[tile]))
            back.append(unpick(jnp.concatenate(grads, axis=1), *tables[number]))

        low_lanes = iota((CHIPS, 128), 1) < 64
        for pair in range(2):
            one, two = back[2 * pair], back[2 * pair + 1]
            back2[0:CHIPS, pair, :] = jnp.where(low_lanes, one, swap(two))
            back2[CHIPS:, pair, :] = jnp.where(low_lanes, swap(one), two)
        to_all_cores(send_gradients)
        land4[core * RENDER + chip] = back2[core * CHIPS + chip]
        for number in range(1, SHARE):
            place = away.at[number - 1]
            remote(place, losses, send7.at[number - 1], recv7, served(number)).wait_send()
        wait_rows(msg, RENDER - 1, send1)
        wait_rows(land4, 2 * RENDER - 1, recv4)

    loss_copy = pltpu.make_async_copy(losses, loss, loads.at[7])
    loss_copy.start()
    low_rows = iota((RENDER, 128), 1) < 64
    messages = []
    for pair in range(2):
        zero, one = land4[0:RENDER, pair, :], land4[RENDER:, pair, :]
        messages.append(jnp.where(low_rows, zero, swap(one)))
        messages.append(jnp.where(low_rows, swap(zero), one))
    returned = unpack_messages(jnp.concatenate(messages, axis=0), table[...])

    lanes = iota((1, 128), 1)
    pose = jnp.zeros((1, 128), f32)
    for n in range(12):
        pose = jnp.where(lanes == n, scalars[n], pose)
    for part in range(4):
        own[10 * part : 10 * part + 9, :] = returned[0:9, 128 * part : 128 * part + 128]
        own[10 * part + 9 : 10 * part + 10, :] = pose

    def share(step, other, device):
        remote(own, out.at[view], send5.at[step], recv5.at[view], device).start()

    def take(step, other, device):
        remote(own, out.at[other], send5.at[step], recv5.at[other], device).wait()

    over_views(share)
    keep = pltpu.make_async_copy(own, out.at[view], kept5)
    keep.start()
    pl.when(early)(lambda: wait_rows(back2, 2 * CHIPS - 1, send4))
    loss_copy.wait()
    keep.wait()
    over_views(take)


def update(
    params_in,
    first_in,
    second_in,
    grads_in,
    loss_in,
    new_params,
    new_first,
    new_second,
    tile_loss,
    params,
    first,
    second,
    grads,
    loss,
    spread,
    total,
    loads,
):
    pairs = [
        (params_in, params),
        (grads_in, grads),
        (first_in, first),
        (second_in, second),
        (loss_in, loss),
    ]
    copies = [
        pltpu.make_async_copy(source, place, loads.at[n]) for n, (source, place) in enumerate(pairs)
    ]
    for copy in copies:
        copy.start()
    copies[0].wait()

    for part in range(4):
        block = params[:, 128 * part : 128 * part + 128]
        for view in range(VIEWS):
            start = 64 * (4 * view + part)
            spread[start : start + 59, :] = block
    columns = [spread[pl.ds(n, 16, stride=64), :] for n in range(59)]
    copies[1].wait()
    given = [grads[pl.ds(n, 16, stride=10), :] for n in range(10)]
    camera = [given[9][:, n : n + 1] for n in range(12)]

    def shown(rows):
        attributes = project(rows, camera)
        return attributes[0:5] + attributes[6:9]

    pulled = jax.vjp(shown, columns)[1](given[0:5] + given[6:9])[0]
    pulled[10] = given[5] * (1.0 - 1.0 / (1.0 + jnp.exp(-columns[10])))
    for n in range(59):
        both = pulled[n][0:8] + pulled[n][8:16]
        total[pl.ds(n, 4, stride=64), :] = both[0:4] + both[4:8]
    for copy in copies[2:]:
        copy.wait()
    row = iota((59, 1), 0)
    rate = jnp.where(row < 3, 0.00016, 0.005)
    rate = jnp.where(row < 6, rate, 0.001)
    rate = jnp.where(row < 10, rate, 0.05)
    rate = jnp.where(row < 11, rate, 0.0025)
    rate = jnp.where(row < 14, rate, 0.000125)
    rate = rate / (1.0 - beta_one**adam_step)
    for part in range(4):
        here = slice(128 * part, 128 * part + 128)
        slope = total[64 * part : 64 * part + 59, :]
        moved = beta_one * first[:, here] + (1.0 - beta_one) * slope
        square = beta_two * second[:, here] + (1.0 - beta_two) * slope * slope
        new_first[:, here] = moved
        new_second[:, here] = square
        new_params[:, here] = params[:, here] - rate * moved / (
            jnp.sqrt(square / (1.0 - beta_two**adam_step)) + adam_eps
        )
    tile_loss[...] = loss[:, 0:2]


def body(params, first_moment, second_moment, cameras, send_rows, lists, counts, tile_ids, target):
    vmem = pl.BlockSpec(memory_space=pltpu.VMEM)
    hbm = pl.BlockSpec(memory_space=pltpu.HBM)
    dma = pltpu.SemaphoreType.DMA
    whole = jax.ShapeDtypeStruct((59, 512), f32)
    some = pltpu.CompilerParams(vmem_limit_bytes=VMEM_BYTES)
    grads, loss = pl.pallas_call(
        exchange,
        out_shape=(
            jax.ShapeDtypeStruct((VIEWS, 40, 128), f32),
            jax.ShapeDtypeStruct((1, 128), f32),
        ),
        in_specs=[hbm] * 7,
        out_specs=(hbm,) * 2,
        scratch_shapes=[
            pltpu.VMEM((59, 512), f32),
            pltpu.SMEM((1, 12), f32),
            pltpu.VMEM((1, 1, 512), jnp.int32),
            pltpu.VMEM((1, 2, 256), jnp.int32),
            pltpu.SMEM((1, 2), jnp.int32),
            pltpu.SMEM((1, 2), jnp.int32),
            pltpu.VMEM((3, 2, 256), f32),
            pltpu.VMEM((RENDER, 3, 1, 128), f32),
            pltpu.VMEM((CHIPS, 3, 1, 128), f32),
            pltpu.VMEM((CHIPS, 3, 1, 128), f32),
            pltpu.VMEM((SHARE, 9, 512), f32),
            pltpu.VMEM((2 * CHIPS, 2, 128), f32),
            pltpu.VMEM((2 * RENDER, 2, 128), f32),
            pltpu.VMEM((3, 1, 256), f32),
            pltpu.VMEM((SHARE - 1, 3, 1, 256), f32),
            pltpu.VMEM((6, 1, 256), f32),
            pltpu.VMEM((SHARE - 1, 6, 1, 256), f32),
            pltpu.VMEM((40, 128), f32),
            pltpu.VMEM((1, 128), f32),
            pltpu.VMEM((SHARE - 1, 1, 128), f32),
            pltpu.VMEM((2 * SHARE, 256, 256), f32),
            pltpu.VMEM((2 * SHARE, 256, 256), f32),
            pltpu.VMEM((2 * SHARE, 256, 256), f32),
            pltpu.VMEM((512, 512), bf16),
            dma((8,)),
            dma,
            dma,
            dma,
            dma,
            dma,
            dma,
            dma((VIEWS,)),
            dma((VIEWS,)),
            dma,
            dma,
            dma((SHARE - 1,)),
            dma((SHARE - 1,)),
            dma,
            dma,
            dma((SHARE - 1,)),
        ],
        compiler_params=pltpu.CompilerParams(
            collective_id=0, has_side_effects=True, vmem_limit_bytes=VMEM_BYTES
        ),
        name="exchange",
    )(
        params,
        cameras,
        send_rows,
        lists,
        counts,
        tile_ids,
        target[0].transpose(1, 0, 2),
    )
    near = pltpu.VMEM((59, 512), f32)
    return pl.pallas_call(
        update,
        out_shape=(whole, whole, whole, jax.ShapeDtypeStruct((1, 2), f32)),
        in_specs=[hbm] * 5,
        out_specs=(vmem,) * 4,
        scratch_shapes=[
            near,
            near,
            near,
            pltpu.VMEM((VIEWS * 40, 128), f32),
            pltpu.VMEM((1, 128), f32),
            pltpu.VMEM((1024, 128), f32),
            pltpu.VMEM((256, 128), f32),
            dma((5,)),
        ],
        compiler_params=some,
        name="update",
    )(params, first_moment, second_moment, grads.reshape(VIEWS * 40, 128), loss)


def solution(mesh):
    in_specs = (
        P(None, "gauss"),
        P(None, "gauss"),
        P(None, "gauss"),
        P("view", None),
        P("view", "gauss", None),
        P("view", "gauss", None),
        P("view", "gauss"),
        P("view", "gauss"),
        P("view", "gauss", None, None),
    )
    out_specs = (P(None, "gauss"), P(None, "gauss"), P(None, "gauss"), P("view", "gauss"))
    return jax.shard_map(body, mesh=mesh, in_specs=in_specs, out_specs=out_specs, check_vma=False)
```

```python
import jax
import jax.numpy as jnp
from jax import lax
from jax.experimental import pallas as pl
from jax.experimental.pallas import tpu as pltpu
from jax.sharding import PartitionSpec as P

focal_length = 1100.0
centre_x = 960.0
centre_y = 540.0
beta_one = 0.9
beta_two = 0.999
adam_eps = 1e-15
adam_step = 100.0
log2_e = 1.4426950408889634
sh_zero = 0.28209479177387814
sh_one = 0.4886025119029199
sh_two = [
    1.0925484305920792,
    -1.0925484305920792,
    0.31539156525252005,
    -1.0925484305920792,
    0.5462742152960396,
]
sh_three = [
    -0.5900435899266435,
    2.890611442640554,
    -0.4570457994644658,
    0.3731763325901154,
    -0.4570457994644658,
    1.445305721320277,
    -0.5900435899266435,
]
LINE = 16
SIDE = 4
CHIPS = LINE * SIDE
SHARE = 4
RENDER = CHIPS // SHARE
VIEWS = 4
VMEM_BYTES = 62 * 1024 * 1024
MESH = pl.DeviceIdType.MESH
f32 = jnp.float32
bf16 = jnp.bfloat16


def harmonics(dir_x, dir_y, dir_z):
    sq_x = dir_x * dir_x
    sq_y = dir_y * dir_y
    sq_z = dir_z * dir_z
    return [
        -sh_one * dir_y,
        sh_one * dir_z,
        -sh_one * dir_x,
        sh_two[0] * dir_x * dir_y,
        sh_two[1] * dir_y * dir_z,
        sh_two[2] * (2.0 * sq_z - sq_x - sq_y),
        sh_two[3] * dir_x * dir_z,
        sh_two[4] * (sq_x - sq_y),
        sh_three[0] * dir_y * (3.0 * sq_x - sq_y),
        sh_three[1] * dir_x * dir_y * dir_z,
        sh_three[2] * dir_y * (4.0 * sq_z - sq_x - sq_y),
        sh_three[3] * dir_z * (2.0 * sq_z - 3.0 * sq_x - 3.0 * sq_y),
        sh_three[4] * dir_x * (4.0 * sq_z - sq_x - sq_y),
        sh_three[5] * dir_z * (sq_x - sq_y),
        sh_three[6] * dir_x * (sq_x - 3.0 * sq_y),
    ]


def project(columns, camera):
    mean_x, mean_y, mean_z = columns[0], columns[1], columns[2]
    scales = [jnp.exp(columns[3 + axis]) for axis in range(3)]
    quat_w, quat_x, quat_y, quat_z = columns[6:10]
    norm = 1.0 / jnp.sqrt(quat_w * quat_w + quat_x * quat_x + quat_y * quat_y + quat_z * quat_z)
    quat_w, quat_x, quat_y, quat_z = quat_w * norm, quat_x * norm, quat_y * norm, quat_z * norm
    turn = [
        [
            1.0 - 2.0 * (quat_y * quat_y + quat_z * quat_z),
            2.0 * (quat_x * quat_y - quat_w * quat_z),
            2.0 * (quat_x * quat_z + quat_w * quat_y),
        ],
        [
            2.0 * (quat_x * quat_y + quat_w * quat_z),
            1.0 - 2.0 * (quat_x * quat_x + quat_z * quat_z),
            2.0 * (quat_y * quat_z - quat_w * quat_x),
        ],
        [
            2.0 * (quat_x * quat_z - quat_w * quat_y),
            2.0 * (quat_y * quat_z + quat_w * quat_x),
            1.0 - 2.0 * (quat_x * quat_x + quat_y * quat_y),
        ],
    ]
    world = [[turn[outer][inner] * scales[inner] for inner in range(3)] for outer in range(3)]
    cam_x, cam_y, depth = [
        camera[3 * outer] * mean_x
        + camera[3 * outer + 1] * mean_y
        + camera[3 * outer + 2] * mean_z
        + camera[9 + outer]
        for outer in range(3)
    ]
    framed = [
        [
            camera[3 * outer] * world[0][inner]
            + camera[3 * outer + 1] * world[1][inner]
            + camera[3 * outer + 2] * world[2][inner]
            for inner in range(3)
        ]
        for outer in range(3)
    ]
    inverse = 1.0 / depth
    near = focal_length * inverse
    slope_x = cam_x * inverse
    slope_y = cam_y * inverse
    row_top = [near * (framed[0][inner] - slope_x * framed[2][inner]) for inner in range(3)]
    row_low = [near * (framed[1][inner] - slope_y * framed[2][inner]) for inner in range(3)]
    cov_a = row_top[0] * row_top[0] + row_top[1] * row_top[1] + row_top[2] * row_top[2] + 0.3
    cov_b = row_top[0] * row_low[0] + row_top[1] * row_low[1] + row_top[2] * row_low[2]
    cov_c = row_low[0] * row_low[0] + row_low[1] * row_low[1] + row_low[2] * row_low[2] + 0.3
    over = 1.0 / (cov_a * cov_c - cov_b * cov_b)
    centre_u = focal_length * slope_x + centre_x
    centre_v = focal_length * slope_y + centre_y
    away = 1.0 / jnp.sqrt(cam_x * cam_x + cam_y * cam_y + depth * depth)
    basis = harmonics(cam_x * away, cam_y * away, depth * away)
    colours = []
    for channel in range(3):
        total = 0.5 + sh_zero * columns[11 + channel]
        for order in range(15):
            total = total + basis[order] * columns[14 + 3 * order + channel]
        colours.append(total)
    opacity = 1.0 / (1.0 + jnp.exp(-columns[10]))
    return [
        centre_u,
        centre_v,
        cov_c * over,
        -cov_b * over,
        cov_a * over,
        opacity,
        colours[0],
        colours[1],
        colours[2],
    ]


def pieces(value):
    high = value.astype(bf16)
    rest = value - high.astype(f32)
    middle = rest.astype(bf16)
    low = (rest - middle.astype(f32)).astype(bf16)
    return high, middle, low


def dot_rows(left, right):
    return lax.dot_general(left, right, (((1,), (1,)), ((), ())), preferred_element_type=f32)


def add_pieces(stacked):
    rows = stacked.shape[0] // 3
    return (stacked[0:rows] + stacked[rows : 2 * rows]) + stacked[2 * rows :]


def dot_exact(left, right):
    stacked = jnp.concatenate(pieces(left), axis=0)
    return add_pieces(jnp.dot(stacked, right, preferred_element_type=f32))


def dot_rows_exact(left, right):
    return add_pieces(dot_rows(jnp.concatenate(pieces(left), axis=0), right))


def iota(shape, axis):
    return lax.broadcasted_iota(jnp.int32, shape, axis)


def one_hot(test):
    return jnp.where(test, 1.0, 0.0).astype(bf16)


def swap(value):
    return pltpu.roll(value, 64, 1)


def reorder_rows(rows, place):
    number, width = rows.shape
    padding = jnp.zeros((8 - 2 * number, width), jnp.int32)
    split_rows = jnp.concatenate([rows >> 4, rows & 15, padding], axis=0)
    chosen = one_hot(iota((width, width), 0) == place(iota((width, width), 1)))
    moved = jnp.dot(split_rows.astype(f32).astype(bf16), chosen, preferred_element_type=f32)
    return moved[0:number] * 16.0 + moved[number : 2 * number]


def sender_table(rows):
    moved = reorder_rows(rows, lambda n: 8 * (n & 63) + (n >> 6))
    return one_hot(iota((512, 512), 0) == moved.astype(jnp.int32))


def pack_messages(attributes, table):
    placed = dot_exact(attributes, table)
    turned = jnp.transpose(jnp.concatenate([placed, jnp.zeros((112, 512), f32)], axis=0))
    lanes = iota((16, 128), 1)
    rows = [jnp.zeros((16, 128), f32)] * 3
    for group in range(8):
        for number in range(SHARE):
            slot = SHARE * group + number
            block = turned[16 * slot : 16 * slot + 16]
            most = jnp.where(lanes < 8, block, 0.0)
            last = jnp.where(lanes == 8, block, 0.0)
            rows[group // 4] = rows[group // 4] + pltpu.roll(most, 8 * (slot % 16), 1)
            rows[2] = rows[2] + pltpu.roll(last, (8 * number + group - 8) % 128, 1)
    return rows


def unpack_messages(messages):
    turned = jnp.transpose(jnp.concatenate([messages, jnp.zeros_like(messages)], axis=0))
    keep = iota((16, 128), 1) < 64
    parts = []
    for pair in range(4):
        left = turned[32 * pair : 32 * pair + 16]
        right = turned[32 * pair + 16 : 32 * pair + 32]
        parts.append(jnp.where(keep, left, swap(right)))
    return jnp.concatenate(parts, axis=1)


def list_tables(lists):
    slot = jnp.concatenate([lists[0:1], lists[1:2]], axis=1).astype(jnp.int32)
    return one_hot(iota((64, 512), 0) == (slot >> 3)), slot & 7


def turn_received(rows):
    blank = jnp.zeros((64, 128), f32)
    return [jnp.transpose(jnp.concatenate([row, blank], axis=0))[:, 0:64] for row in rows]


def pick(turned, sender, core, number, table, group):
    mine = jnp.where(core == 0, turned[0], turned[1])
    rows = [mine[8 * (SHARE * n + number) :][0:8] for n in range(4)]
    ninth = turned[2][8 * number : 8 * number + 8]
    rows.append(jnp.where(core == 0, ninth, pltpu.roll(ninth, 4, 0)))
    found = dot_exact(jnp.concatenate(rows, axis=0), table)
    place = group - 4 * sender
    total = jnp.where(place == 0, found[0:8], 0.0)
    for part in range(1, 4):
        total = total + jnp.where(place == part, found[8 * part : 8 * part + 8], 0.0)
    last = jnp.where(iota((4, 512), 0) == place, found[32:36], 0.0)
    return jnp.concatenate([total, jnp.sum(last, axis=0, keepdims=True)], axis=0)


def unpick(grads, table, group):
    spread = jnp.concatenate([grads] * 8, axis=0)
    spread = jnp.where((iota((128, 512), 0) >> 4) == group, spread, 0.0)
    turned = dot_rows_exact(spread, table)
    return jnp.transpose(jnp.concatenate([turned, jnp.zeros((128, 64), f32)], axis=1))[0:64]


def place_of(position):
    return 32 * (position & 7) + (position >> 3)


def split(rows):
    return [part.astype(f32) for part in pieces(rows)]


def split(rows):
    return [part.astype(f32) for part in pieces(rows)]


def two_pieces(value):
    high = value.astype(bf16)
    return high, (value - high.astype(f32)).astype(bf16)


def padded(rows):
    number = sum(part.shape[0] for part in rows)
    return jnp.concatenate(rows + [jnp.zeros((32 - number, 256), f32)], axis=0).astype(bf16)


def dot_columns(left, right):
    return lax.dot_general(left, right, (((0,), (0,)), ((), ())), preferred_element_type=f32)


def prepare_tile(attributes, across, down, count):
    centre_u = attributes[0:1] - across
    centre_v = attributes[1:2] - down
    alive = place_of(iota((1, 256), 1)).astype(f32) < count
    by_xx = attributes[2:3] * (-0.5 * log2_e)
    by_xy = attributes[3:4] * (-log2_e)
    by_yy = attributes[4:5] * (-0.5 * log2_e)
    by_x = -2.0 * by_xx * centre_u - by_xy * centre_v
    by_y = -2.0 * by_yy * centre_v - by_xy * centre_u
    whole = (by_xx * centre_u + by_xy * centre_v) * centre_u + (by_yy * centre_v) * centre_v
    whole = jnp.where(alive, whole + jnp.log(attributes[5:6]) * log2_e, -1e30)
    power = jnp.concatenate([whole, by_x, by_y, by_xx, by_xy, by_yy], axis=0)
    return power, centre_u, centre_v


def pixels():
    number = iota((1, 256), 1)
    return (number & 15).astype(f32) - 7.5, (number >> 4).astype(f32) - 7.5


def monomials():
    pixel_x, pixel_y = pixels()
    ones = jnp.ones((1, 256), f32)
    return [ones, pixel_x, pixel_y, pixel_x * pixel_x, pixel_x * pixel_y, pixel_y * pixel_y]


def exponents(power):
    return dot_columns(padded(split(power)), padded(monomials() * 3))


def colour_sums(colour, weight):
    chunk = (iota((8, 256), 1) & 7) == iota((8, 256), 0)
    spread = [jnp.where(chunk, colour[c : c + 1], 0.0) for c in range(3)]
    left = jnp.concatenate(split(jnp.concatenate(spread, axis=0)), axis=0).astype(bf16)
    high, middle = two_pieces(weight)
    total = jnp.dot(left, middle, preferred_element_type=f32)
    total = total + jnp.dot(left, high, preferred_element_type=f32)
    total = add_pieces(total)
    return [total[8 * c : 8 * c + 8] for c in range(3)]


def shades(colour, residual):
    high, middle, low = split(colour)
    left = padded([high, high, high, middle, middle, low])
    high, middle, low = split(jnp.concatenate(residual, axis=0))
    return dot_columns(left, padded([high, middle, low, high, middle, high]))


def between(keep, colour, target):
    before = [jnp.ones((1, 256), f32)]
    for chunk in range(7):
        before.append(before[-1] * keep[chunk : chunk + 1])
    before = jnp.concatenate(before, axis=0)
    colour = [part * before for part in colour]
    residual = [jnp.sum(colour[c], axis=0, keepdims=True) - target[c : c + 1] for c in range(3)]
    own = residual[0] * colour[0] + residual[1] * colour[1] + residual[2] * colour[2]
    after = [jnp.zeros((1, 256), f32)]
    for chunk in range(7, 0, -1):
        after.append(after[-1] + own[chunk : chunk + 1])
    after = jnp.concatenate(after[::-1], axis=0)
    squares = residual[0] * residual[0] + residual[1] * residual[1] + residual[2] * residual[2]
    return before, after, residual, 0.5 * jnp.sum(squares, axis=1, keepdims=True)


def back_step(shade, alpha, weight, before, after, later):
    own = weight * shade
    left = 1.0 - alpha
    guess = pl.reciprocal(left, approx=True)
    ratio = alpha * (guess * (2.0 - left * guess))
    slope = before * own - (before * later + after) * ratio
    return slope, before * weight, later + own


def moments(slope, weight, residual):
    shown = split(jnp.concatenate(residual, axis=0))
    factors = jnp.concatenate(monomials() + shown + [jnp.zeros((1, 256), f32)], axis=0).astype(bf16)

    def over_pixels(value):
        high, middle = two_pieces(value)
        return dot_rows(factors, middle) + dot_rows(factors, high)

    by_power = over_pixels(slope)[0:6]
    by_shown = over_pixels(weight)
    by_shown = by_shown[6:9] + (by_shown[9:12] + by_shown[12:15])
    return jnp.concatenate([by_power, by_shown], axis=0)


def finish_tile(sums, attributes, centre_u, centre_v):
    whole, by_x, by_y, by_xx, by_xy, by_yy = [sums[n : n + 1] for n in range(6)]
    sum_x = by_x - centre_u * whole
    sum_y = by_y - centre_v * whole
    sum_xx = by_xx - centre_u * (by_x + sum_x)
    sum_xy = by_xy - centre_u * by_y - centre_v * sum_x
    sum_yy = by_yy - centre_v * (by_y + sum_y)
    conic = [attributes[2 + n : 3 + n] for n in range(3)]
    rows = [
        conic[0] * sum_x + conic[1] * sum_y,
        conic[1] * sum_x + conic[2] * sum_y,
        -0.5 * sum_xx,
        -sum_xy,
        -0.5 * sum_yy,
        whole,
        sums[6:9],
        jnp.zeros((7, 256), f32),
    ]
    return jnp.concatenate(rows, axis=0)


def exchange(
    params_in,
    camera_in,
    rows_in,
    lists_in,
    counts_in,
    tile_ids_in,
    target_in,
    out,
    loss,
    params,
    camera,
    rows,
    lists,
    counts,
    tile_ids,
    target,
    msg,
    land1,
    land2,
    halves,
    back2,
    land4,
    facts,
    land_facts,
    aims,
    land_aims,
    own,
    losses,
    away,
    alphas,
    weights,
    shaded,
    table,
    loads,
    send1,
    recv1,
    send2,
    recv2,
    send4,
    recv4,
    send5,
    recv5,
    kept5,
    send6,
    recv6,
    send7,
    recv7,
    send8,
    recv8,
):
    here = lax.axis_index("gauss")
    view = lax.axis_index("view")
    core = lax.rem(here, 2)
    chip = here // 2
    line = chip // SIDE
    side = lax.rem(chip, SIDE)

    other_core = {"gauss": here + 1 - 2 * core, "view": view}

    def over_views(action):
        for step in (2, 1, 3):
            other = lax.rem(view + step, VIEWS)
            action(step, other, {"gauss": here, "view": other})

    barrier = pltpu.get_barrier_semaphore()

    def greet(device):
        pl.semaphore_signal(barrier, inc=1, device_id=device, device_id_type=MESH)

    early = chip < RENDER
    late = jnp.logical_not(early)
    home = {"gauss": lax.rem(chip, RENDER) * 2 + core, "view": view}
    turn = chip // RENDER

    def served(number):
        return {"gauss": lax.rem(chip + number * RENDER, CHIPS) * 2 + core, "view": view}

    def to_renderers(action):
        for step_z in (0, 1, 3, 2):
            for step_x in (2, 1, 3, 0):
                other = lax.rem(line + step_z, 4) * SIDE + lax.rem(side + step_x, SIDE)
                device = {"gauss": other * 2 + core, "view": view}
                pl.when(other != chip)(lambda other=other, device=device: action(other, device))

    def to_all(action):
        def one(number, unused):
            for step_x in (2, 1, 3, 0):
                other = number * SIDE + lax.rem(side + step_x, SIDE)
                device = {"gauss": other * 2 + core, "view": view}
                pl.when(other != chip)(lambda other=other, device=device: action(other, device))
            return unused

        lax.fori_loop(0, LINE, one, 0)

    def to_all_cores(action):
        def one(number, unused):
            for step_x in (2, 1, 3, 0):
                other = number * SIDE + lax.rem(side + step_x, SIDE)
                for which in range(2):
                    device = {"gauss": other * 2 + which, "view": view}
                    place = which * CHIPS + other
                    pl.when(other * 2 + which != here)(
                        lambda place=place, device=device: action(place, device)
                    )
            return unused

        lax.fori_loop(0, LINE, one, 0)

    def greet_late(other, device):
        pl.when(other >= RENDER)(lambda: greet(device))

    @pl.when(early)
    def greet_first():
        to_renderers(lambda other, device: greet(device))
        greet(other_core)

    over_views(lambda step, other, device: greet(device))

    pairs = [
        (rows_in, rows),
        (params_in, params),
        (camera_in, camera),
        (lists_in, lists),
        (counts_in, counts),
        (tile_ids_in, tile_ids),
        (target_in, target),
    ]
    copies = [
        pltpu.make_async_copy(source, place, loads.at[n]) for n, (source, place) in enumerate(pairs)
    ]
    for copy in copies:
        copy.start()

    pl.when(early)(lambda: to_all(greet_late))

    def remote(source, place, sent, arrived, device):
        return pltpu.make_async_remote_copy(
            src_ref=source,
            dst_ref=place,
            send_sem=sent,
            recv_sem=arrived,
            device_id=device,
            device_id_type=MESH,
        )

    def wait_rows(place, count, semaphore):
        whole = place.at[pl.ds(0, count)]
        pltpu.make_async_copy(whole, whole, semaphore).wait()

    copies[0].wait()
    table[...] = sender_table(rows[0])
    copies[1].wait()
    copies[2].wait()
    scalars = [camera[0, n] for n in range(12)]
    attributes = project([params[n : n + 1, :] for n in range(59)], scalars)
    messages = pack_messages(
        jnp.concatenate(attributes + [jnp.zeros((7, 512), f32)], axis=0), table[...]
    )
    for number in range(3):
        msg[:, number, 0, :] = messages[number]
    pl.semaphore_wait(barrier, RENDER + VIEWS - 1)

    def send_attributes(other, device):
        remote(msg.at[other], land1.at[chip], send1, recv1, device).start()

    def send_gradients(other, device):
        mine = land4.at[core * RENDER + chip]
        remote(back2.at[other], mine, send4, recv4, device).start()

    to_renderers(send_attributes)

    for copy in copies[3:]:
        copy.wait()

    facts[0:2, 0, :] = reorder_rows(lists[0], place_of)
    for tile in range(2):
        for channel in range(3):
            aims[3 * tile + channel, 0:1, :] = target[channel, tile : tile + 1, :]
    spots = iota((1, 256), 1)
    known = jnp.zeros((1, 256), f32)
    for tile in range(2):
        tile_id = tile_ids[0, tile]
        across = (16 * lax.rem(tile_id, 120)).astype(f32) + 7.5
        down = (16 * lax.div(tile_id, 120)).astype(f32) + 7.5
        for n, value in enumerate((across, down, counts[0, tile].astype(f32))):
            known = jnp.where(spots == 3 * tile + n, value, known)
    facts[2, 0:1, :] = known

    @pl.when(late)
    def send_facts():
        remote(facts, land_facts.at[turn - 1], send6, recv6.at[turn - 1], home).start()

    @pl.when(late)
    def late_part():
        aims_copy = remote(aims, land_aims.at[turn - 1], send8, recv8.at[turn - 1], home)
        aims_copy.start()
        remote(facts, land_facts.at[turn - 1], send6, recv6.at[turn - 1], home).wait_send()
        aims_copy.wait_send()
        wait_rows(msg, RENDER, send1)
        remote(away.at[0], losses, send7.at[0], recv7, home).wait_recv()
        wait_rows(land4, 2 * RENDER, recv4)

    @pl.when(early)
    def render():
        land1[chip] = msg[chip]
        tables = [list_tables(facts[0:2, 0, :])]
        for number in range(1, SHARE):
            place = land_facts.at[number - 1]
            remote(facts, place, send6, recv6.at[number - 1], served(number)).wait_recv()
            tables.append(list_tables(land_facts[number - 1, 0:2, 0, :]))
        wait_rows(land1, CHIPS - 1, recv1)
        core_copy = remote(land1, land2, send2, recv2, other_core)
        core_copy.start()
        kept = turn_received([land1[:, n, 0, :] for n in range(3)])
        for number in range(SHARE):
            halves[number] = pick(kept, core, core, number, *tables[number])
        core_copy.wait()

        given = turn_received([land2[:, n, 0, :] for n in range(3)])
        tiles = range(2 * SHARE)
        entries, centres = [], []
        for number in range(SHARE):
            found = halves[number] + pick(given, 1 - core, core, number, *tables[number])
            known = facts[2] if number == 0 else land_facts[number - 1, 2]
            for part in range(2):
                chosen = found[:, 256 * part : 256 * part + 256]
                about = [known[:, 3 * part + n : 3 * part + n + 1] for n in range(3)]
                power, centre_u, centre_v = prepare_tile(chosen, *about)
                alphas[2 * number + part] = exponents(power)
                entries.append(chosen)
                centres.append((centre_u, centre_v))

        def forward(step, carry):
            rows_here = pl.ds(pl.multiple_of(step * 8, 8), 8)
            left = []
            for tile, keep in zip(tiles, carry):
                alpha = jnp.exp2(alphas[tile, rows_here, :])
                weight = keep * alpha
                alphas[tile, rows_here, :] = alpha
                weights[tile, rows_here, :] = weight
                left.append(keep - weight)
            return left

        keeps = lax.fori_loop(0, 32, forward, [jnp.ones((8, 256), f32) for tile in tiles], unroll=4)
        shown = [aims[0:3, 0, :], aims[3:6, 0, :]]
        for number in range(SHARE - 1):
            place = land_aims.at[number]
            remote(aims, place, send8, recv8.at[number], served(number + 1)).wait_recv()
            shown += [land_aims[number, 0:3, 0, :], land_aims[number, 3:6, 0, :]]
        around = []
        for tile in tiles:
            colour = colour_sums(entries[tile][6:9], weights[tile])
            around.append(between(keeps[tile], colour, shown[tile]))
            shaded[tile] = shades(entries[tile][6:9], around[tile][2])
        spot = iota((1, 128), 1)
        for number in range(SHARE):
            pair = around[2 * number][3], around[2 * number + 1][3]
            row = jnp.where(spot == 0, pair[0], jnp.where(spot == 1, pair[1], 0.0))
            if number == 0:
                losses[...] = row
            else:
                away[number - 1] = row
                place = away.at[number - 1]
                remote(place, losses, send7.at[number - 1], recv7, served(number)).start()

        for first_tile in range(0, 2 * SHARE, 4):
            some = range(first_tile, first_tile + 4)

            def backward(step, later, some=some):
                rows_here = pl.ds(pl.multiple_of((31 - step) * 8, 8), 8)
                left = []
                for tile, behind in zip(some, later):
                    before, after = around[tile][0:2]
                    slope, weight, rest = back_step(
                        shaded[tile, rows_here, :],
                        alphas[tile, rows_here, :],
                        weights[tile, rows_here, :],
                        before,
                        after,
                        behind,
                    )
                    alphas[tile, rows_here, :] = slope
                    weights[tile, rows_here, :] = weight
                    left.append(rest)
                return left

            lax.fori_loop(0, 32, backward, [jnp.zeros((8, 256), f32)] * 4, unroll=8)
        back = []
        for number in range(SHARE):
            grads = []
            for tile in (2 * number, 2 * number + 1):
                sums = moments(alphas[tile], weights[tile], around[tile][2])
                grads.append(finish_tile(sums, entries[tile], *centres[tile]))
            back.append(unpick(jnp.concatenate(grads, axis=1), *tables[number]))

        low_lanes = iota((CHIPS, 128), 1) < 64
        for pair in range(2):
            one, two = back[2 * pair], back[2 * pair + 1]
            back2[0:CHIPS, pair, :] = jnp.where(low_lanes, one, swap(two))
            back2[CHIPS:, pair, :] = jnp.where(low_lanes, swap(one), two)
        to_all_cores(send_gradients)
        land4[core * RENDER + chip] = back2[core * CHIPS + chip]
        for number in range(1, SHARE):
            place = away.at[number - 1]
            remote(place, losses, send7.at[number - 1], recv7, served(number)).wait_send()
        wait_rows(msg, RENDER - 1, send1)
        wait_rows(land4, 2 * RENDER - 1, recv4)

    loss_copy = pltpu.make_async_copy(losses, loss, loads.at[7])
    loss_copy.start()
    low_rows = iota((RENDER, 128), 1) < 64
    messages = []
    for pair in range(2):
        zero, one = land4[0:RENDER, pair, :], land4[RENDER:, pair, :]
        messages.append(jnp.where(low_rows, zero, swap(one)))
        messages.append(jnp.where(low_rows, swap(zero), one))
    returned = unpack_messages(jnp.concatenate(messages, axis=0))

    lanes = iota((1, 128), 1)
    pose = jnp.zeros((1, 128), f32)
    for n in range(12):
        pose = jnp.where(lanes == n, scalars[n], pose)
    def share(half, step, other, device):
        rows_here = pl.ds(24 * half, 24)
        place = out.at[view, rows_here]
        sent, arrived = send5.at[half, step], recv5.at[half, view]
        remote(own.at[rows_here], place, sent, arrived, device).start()

    def take(half, step, other, device):
        rows_here = pl.ds(24 * half, 24)
        place = out.at[other, rows_here]
        remote(own.at[rows_here], place, send5.at[half, step], recv5.at[half, other], device).wait()

    for half in range(2):
        ordered = dot_rows_exact(returned, table[256 * half : 256 * half + 256, :])
        for part in range(2):
            block = [ordered[0:9, 128 * part : 128 * part + 128], pose, jnp.zeros((2, 128), f32)]
            start = 24 * half + 12 * part
            own[start : start + 12, :] = jnp.concatenate(block, axis=0)
        over_views(lambda *peer, half=half: share(half, *peer))
    keep = pltpu.make_async_copy(own, out.at[view], kept5)
    keep.start()
    pl.when(early)(lambda: wait_rows(back2, 2 * CHIPS - 1, send4))
    loss_copy.wait()
    keep.wait()
    for half in range(2):
        over_views(lambda *peer, half=half: take(half, *peer))


def update(
    params_in,
    first_in,
    second_in,
    grads_in,
    loss_in,
    new_params,
    new_first,
    new_second,
    tile_loss,
    params,
    first,
    second,
    grads,
    loss,
    spread,
    total,
    loads,
):
    pairs = [
        (params_in, params),
        (grads_in, grads),
        (first_in, first),
        (second_in, second),
        (loss_in, loss),
    ]
    copies = [
        pltpu.make_async_copy(source, place, loads.at[n]) for n, (source, place) in enumerate(pairs)
    ]
    for copy in copies:
        copy.start()
    copies[0].wait()

    for part in range(4):
        block = params[:, 128 * part : 128 * part + 128]
        for view in range(VIEWS):
            start = 64 * (4 * view + part)
            spread[start : start + 59, :] = block
    columns = [spread[pl.ds(n, 16, stride=64), :] for n in range(59)]
    copies[1].wait()
    given = [grads[pl.ds(n, 16, stride=12), :] for n in range(10)]
    camera = [given[9][:, n : n + 1] for n in range(12)]

    def shown(rows):
        attributes = project(rows, camera)
        return attributes[0:5] + attributes[6:9]

    pulled = jax.vjp(shown, columns)[1](given[0:5] + given[6:9])[0]
    pulled[10] = given[5] * (1.0 - 1.0 / (1.0 + jnp.exp(-columns[10])))
    for n in range(59):
        both = pulled[n][0:8] + pulled[n][8:16]
        total[pl.ds(n, 4, stride=64), :] = both[0:4] + both[4:8]
    for copy in copies[2:]:
        copy.wait()
    row = iota((59, 1), 0)
    rate = jnp.where(row < 3, 0.00016, 0.005)
    rate = jnp.where(row < 6, rate, 0.001)
    rate = jnp.where(row < 10, rate, 0.05)
    rate = jnp.where(row < 11, rate, 0.0025)
    rate = jnp.where(row < 14, rate, 0.000125)
    rate = rate / (1.0 - beta_one**adam_step)
    for part in range(4):
        here = slice(128 * part, 128 * part + 128)
        slope = total[64 * part : 64 * part + 59, :]
        moved = beta_one * first[:, here] + (1.0 - beta_one) * slope
        square = beta_two * second[:, here] + (1.0 - beta_two) * slope * slope
        new_first[:, here] = moved
        new_second[:, here] = square
        new_params[:, here] = params[:, here] - rate * moved / (
            jnp.sqrt(square / (1.0 - beta_two**adam_step)) + adam_eps
        )
    tile_loss[...] = loss[:, 0:2]


def body(params, first_moment, second_moment, cameras, send_rows, lists, counts, tile_ids, target):
    vmem = pl.BlockSpec(memory_space=pltpu.VMEM)
    hbm = pl.BlockSpec(memory_space=pltpu.HBM)
    dma = pltpu.SemaphoreType.DMA
    whole = jax.ShapeDtypeStruct((59, 512), f32)
    some = pltpu.CompilerParams(vmem_limit_bytes=VMEM_BYTES)
    grads, loss = pl.pallas_call(
        exchange,
        out_shape=(
            jax.ShapeDtypeStruct((VIEWS, 48, 128), f32),
            jax.ShapeDtypeStruct((1, 128), f32),
        ),
        in_specs=[hbm] * 7,
        out_specs=(hbm,) * 2,
        scratch_shapes=[
            pltpu.VMEM((59, 512), f32),
            pltpu.SMEM((1, 12), f32),
            pltpu.VMEM((1, 1, 512), jnp.int32),
            pltpu.VMEM((1, 2, 256), jnp.int32),
            pltpu.SMEM((1, 2), jnp.int32),
            pltpu.SMEM((1, 2), jnp.int32),
            pltpu.VMEM((3, 2, 256), f32),
            pltpu.VMEM((RENDER, 3, 1, 128), f32),
            pltpu.VMEM((CHIPS, 3, 1, 128), f32),
            pltpu.VMEM((CHIPS, 3, 1, 128), f32),
            pltpu.VMEM((SHARE, 9, 512), f32),
            pltpu.VMEM((2 * CHIPS, 2, 128), f32),
            pltpu.VMEM((2 * RENDER, 2, 128), f32),
            pltpu.VMEM((3, 1, 256), f32),
            pltpu.VMEM((SHARE - 1, 3, 1, 256), f32),
            pltpu.VMEM((6, 1, 256), f32),
            pltpu.VMEM((SHARE - 1, 6, 1, 256), f32),
            pltpu.VMEM((48, 128), f32),
            pltpu.VMEM((1, 128), f32),
            pltpu.VMEM((SHARE - 1, 1, 128), f32),
            pltpu.VMEM((2 * SHARE, 256, 256), f32),
            pltpu.VMEM((2 * SHARE, 256, 256), f32),
            pltpu.VMEM((2 * SHARE, 256, 256), f32),
            pltpu.VMEM((512, 512), bf16),
            dma((8,)),
            dma,
            dma,
            dma,
            dma,
            dma,
            dma,
            dma((2, VIEWS)),
            dma((2, VIEWS)),
            dma,
            dma,
            dma((SHARE - 1,)),
            dma((SHARE - 1,)),
            dma,
            dma,
            dma((SHARE - 1,)),
        ],
        compiler_params=pltpu.CompilerParams(
            collective_id=0, has_side_effects=True, vmem_limit_bytes=VMEM_BYTES
        ),
        name="exchange",
    )(
        params,
        cameras,
        send_rows,
        lists,
        counts,
        tile_ids,
        target[0].transpose(1, 0, 2),
    )
    near = pltpu.VMEM((59, 512), f32)
    return pl.pallas_call(
        update,
        out_shape=(whole, whole, whole, jax.ShapeDtypeStruct((1, 2), f32)),
        in_specs=[hbm] * 5,
        out_specs=(vmem,) * 4,
        scratch_shapes=[
            near,
            near,
            near,
            pltpu.VMEM((VIEWS * 48, 128), f32),
            pltpu.VMEM((1, 128), f32),
            pltpu.VMEM((1024, 128), f32),
            pltpu.VMEM((256, 128), f32),
            dma((5,)),
        ],
        compiler_params=some,
        name="update",
    )(params, first_moment, second_moment, grads.reshape(VIEWS * 48, 128), loss)


def solution(mesh):
    in_specs = (
        P(None, "gauss"),
        P(None, "gauss"),
        P(None, "gauss"),
        P("view", None),
        P("view", "gauss", None),
        P("view", "gauss", None),
        P("view", "gauss"),
        P("view", "gauss"),
        P("view", "gauss", None, None),
    )
    out_specs = (P(None, "gauss"), P(None, "gauss"), P(None, "gauss"), P("view", "gauss"))
    return jax.shard_map(body, mesh=mesh, in_specs=in_specs, out_specs=out_specs, check_vma=False)
```
